32 devices in a mesh: session: 2 (over y), seq: 4 (over z), tensor: 4 (over x, core).
Axes of the slice: x: 2, y: 2, z: 4, core: 2. Of those that a mesh axis runs over, the one named last changes fastest.
Arguments:
- queries: bfloat16 [1536, 3072], P(('session', 'seq'), 'tensor'), parts along dimension 0, may hold values from -210 to 210
- new_keys: bfloat16 [1536, 3072], P(('session', 'seq'), 'tensor'), parts along dimension 0, may hold values from -5 to 5
- new_values: bfloat16 [1536, 3072], P(('session', 'seq'), 'tensor'), parts along dimension 0, may hold values from -6 to 6
- context_queries: bfloat16 [1024, 3072], P(('session', 'seq'), 'tensor'), parts along dimension 0, may hold values from -6 to 6
- context_keys: bfloat16 [1024, 3072], P(('session', 'seq'), 'tensor'), parts along dimension 0, may hold values from -6 to 6
- context_values: bfloat16 [1024, 3072], P(('session', 'seq'), 'tensor'), parts along dimension 0, may hold values from -6 to 6
- levels: int32 [16], P('session'), parts along dimension 0, may hold values from 0 to 1
- frame_mask: int32 [4, 8], P('session'), parts along dimension 0, may hold values 0 or 1
- owners: int32 [256], P('session'), parts along dimension 0, may hold values from 0 to 3, as said below
- out_weight: bfloat16 [3072, 3072], P('tensor'), may hold values from -0.15625 to 0.15625
Outputs:
- block_out: bfloat16 [1536, 3072], P(('session', 'seq'), 'tensor'), parts along dimension 0
- context_out: bfloat16 [1024, 3072], P(('session', 'seq'), 'tensor'), parts along dimension 0
- cache_keys: bfloat16 [1024, 3072], P(('session', 'seq'), 'tensor'), parts along dimension 0
- cache_values: bfloat16 [1024, 3072], P(('session', 'seq'), 'tensor'), parts along dimension 0
The draws below stay inside these ranges and needn't reach their ends.
There are 2 independent parts, one for each index of `session`. The reference program is written for one: setup_inputs(seed, part) draws one part's arguments, and reference() takes and returns one part's arrays. A program takes and returns all parts, laid end to end along the dimension named above; an argument that names none is the same for every part. Nothing has to cross between parts.
Inputs may be any that keep to these rules, and one draw needn't show every extreme that they name: `owners`: every seq index owns exactly 32 blocks; a seq index gives either none or exactly 16 of its own blocks to each owner, and the owner minus the giver, modulo the number of seq indices, takes the same 32 // 16 values for every giver.
All inputs are finite; a program needn't handle non-finite values.
Results may differ from the reference program's by a relative error of at most 0.014.
Values may be sent and summed in bfloat16 or wider, within the bound.
No kernel may reach another device: no remote copies, remote signals or barrier semaphores. Data moves between devices by JAX's collectives and lax.ppermute only.
A program may use at most 64 MiB of HBM per device.

```python
import math
import jax
import jax.numpy as jnp
from jax import lax

HEADS = 24
HEAD_DIM = 128
D = 3072
NEW_FRAMES = 2
CF = 8
BLK_DEV = 32
PAIR = 16
NEW = 768
CTX_BLOCKS = 128
N_SEQ = 4


def shared_keys(key):
    return jnp.clip(jax.random.normal(key, (NEW, D), jnp.float32), -4.0, 4.0)


def draw_queries(key, part):
    key = jax.random.fold_in(key, 11)
    fresh = jnp.clip(jax.random.normal(key, (NEW, D), jnp.float32), -4.0, 4.0)
    return fresh.astype(jnp.bfloat16)


def draw_new_keys(key, part):
    base = shared_keys(key)
    return base.astype(jnp.bfloat16)


def draw_owners(key, part):
    key = jax.random.fold_in(key, 21)
    first_key, second_key = jax.random.split(key)
    groups = BLK_DEV // PAIR
    offsets = jax.random.permutation(first_key, N_SEQ)[:groups]
    table = jnp.repeat(offsets, PAIR, total_repeat_length=BLK_DEV)
    orders = jax.vmap(lambda item: jax.random.permutation(item, BLK_DEV))(jax.random.split(second_key, N_SEQ))
    senders = jnp.arange(N_SEQ)[:, None]
    return ((senders + table[orders]) % N_SEQ).reshape(-1).astype(jnp.int32)


def touch_ends(entries, stream_key, low, largest):
    longest = entries.shape.index(max(entries.shape))
    spots = []
    for shift in (0, 1):
        where = [jax.random.randint(jax.random.fold_in(stream_key, axis), (), 0, length) for axis, length in enumerate(entries.shape)]
        where[longest] = (where[longest] + shift) % entries.shape[longest]
        spots.append(tuple(where))
    return entries.at[spots[0]].set(low).at[spots[1]].set(largest)


def spiked(entries, own_key, source, target, parts, factor):
    def block_of(axis_at):
        return (jnp.arange(entries.shape[axis_at]) // (entries.shape[axis_at] // parts)).reshape((-1,) + (1,) * (entries.ndim - 1 - axis_at))

    first = jax.random.permutation(own_key, parts)[block_of(target)]
    other_side = (block_of(target) + parts // 2) % parts
    return jnp.where((block_of(source) == first) | (block_of(source) == other_side), factor * entries, entries)


def shard_levels(rng, shape, cuts, low, largest):
    def one(position, parts):
        draws = jax.random.uniform(jax.random.fold_in(jax.random.fold_in(rng, 6), position), (parts,), jnp.float32, low / len(cuts), largest / len(cuts))
        return jnp.repeat(jnp.exp(draws), shape[position] // parts).reshape((-1,) + (1,) * (len(shape) - position - 1))

    loudness = one(*cuts[0])
    for cut in cuts[1:]:
        loudness = loudness * one(*cut)
    return loudness


def centred(rng, dims, width, bound, cuts=(), kind=jnp.bfloat16):
    drawn = jax.random.normal(rng, dims, jnp.float32) * width
    if len(cuts) > 0:
        drawn = shard_levels(rng, dims, cuts, -0.22, 0.18) * drawn
    return jnp.clip(drawn, min=-bound, max=bound).astype(kind)


def bell_draw_with(rng, shape, deviation, reach, pieces, heavy, held_as=jnp.bfloat16):
    result = deviation * jax.random.normal(rng, shape, jnp.float32)
    if pieces:
        result = result * shard_levels(rng, shape, pieces, -0.22, 0.18)
    return jnp.clip(spiked(result, jax.random.fold_in(rng, 3), *heavy), -reach, reach).astype(held_as)


def setup_inputs(seed: int = 0, part: int = 0) -> dict:
    keys = jax.random.split(jax.random.key(seed), 11)
    own_keys = jax.random.split(jax.random.fold_in(keys[10], part), 11)
    queries = draw_queries(jax.random.fold_in(jax.random.fold_in(keys[10], part), 71), part)
    new_keys = draw_new_keys(jax.random.fold_in(jax.random.fold_in(keys[10], part), 71), part)
    new_values = centred(own_keys[2], (NEW, D), 1.0, 6.0, ((0, 4), (1, 4)))
    context_queries = centred(own_keys[3], (4 * CTX_BLOCKS, D), 1.0, 6.0, ((0, 4), (1, 4)))
    context_keys = centred(own_keys[4], (4 * CTX_BLOCKS, D), 1.0, 6.0, ((0, 4), (1, 4)))
    context_values = centred(own_keys[5], (4 * CTX_BLOCKS, D), 1.0, 6.0, ((0, 4), (1, 4)))
    levels = touch_ends(jax.random.randint(own_keys[6], (CF,), 0, 2), jax.random.fold_in(own_keys[6], 1), 0, 1).astype(jnp.int32)
    frame_mask = touch_ends((jax.random.randint(own_keys[7], (NEW_FRAMES, CF), 0, 4) < 3).astype(jnp.int32), jax.random.fold_in(own_keys[7], 1), 0, 1)
    owners = draw_owners(jax.random.fold_in(jax.random.fold_in(keys[10], part), 71), part)
    out_weight = bell_draw_with(keys[9], (D, D), D ** -0.5, 0.15625, ((0, 4),), (0, 1, 4, 2.0))
    return {"queries": queries, "new_keys": new_keys, "new_values": new_values, "context_queries": context_queries, "context_keys": context_keys, "context_values": context_values, "levels": levels, "frame_mask": frame_mask, "owners": owners, "out_weight": out_weight}


def pool(rows, coarse):
    blocks = rows.reshape(CTX_BLOCKS, 4, D)
    mean = lax.optimization_barrier(jnp.mean(blocks.astype(jnp.float32), axis=1)).astype(jnp.bfloat16)
    first = (jnp.arange(4) == 0)[None, :, None]
    pooled = jnp.where(first, mean[:, None, :], jnp.zeros_like(blocks))
    return jnp.where(coarse[:, None, None], pooled, blocks)

def reference(queries, new_keys, new_values, context_queries, context_keys, context_values, levels, frame_mask, owners, out_weight):
    block_ids = jnp.arange(CTX_BLOCKS, dtype=jnp.int32)
    block_frame = block_ids * CF // CTX_BLOCKS
    coarse = levels[block_frame] == 1
    pooled_q = pool(context_queries, coarse)
    pooled_k = pool(context_keys, coarse)
    pooled_v = pool(context_values, coarse)
    live = jnp.logical_or(jnp.logical_not(coarse)[:, None], (jnp.arange(4) == 0)[None, :])
    order = jnp.argsort(owners, stable=True).astype(jnp.int32)
    held_q = pooled_q[order].reshape(-1, D)
    cache_keys = pooled_k[order].reshape(-1, D)
    cache_values = pooled_v[order].reshape(-1, D)
    held_live = live[order].reshape(-1)
    all_q = jnp.concatenate([queries, held_q], axis=0)
    all_k = jnp.concatenate([new_keys, pooled_k.reshape(-1, D)], axis=0)
    all_v = jnp.concatenate([new_values, pooled_v.reshape(-1, D)], axis=0)
    q_frame = jnp.arange(NEW, dtype=jnp.int32) * NEW_FRAMES // NEW
    key_frame = jnp.repeat(block_frame, 4)
    key_live = live.reshape(-1)
    new_part = jnp.logical_and(frame_mask[q_frame][:, key_frame] == 1, key_live[None, :])
    ctx_part = jnp.broadcast_to(key_live[None, :], (4 * CTX_BLOCKS, 4 * CTX_BLOCKS))
    ctx_allowed = jnp.concatenate([new_part, ctx_part], axis=0)
    rows_q = NEW + 4 * CTX_BLOCKS
    allowed = jnp.concatenate([jnp.ones((rows_q, NEW), dtype=bool), ctx_allowed], axis=1)
    scale = 1.0 / math.sqrt(HEAD_DIM)

    def one_head(head):
        offset = (head * HEAD_DIM).astype(jnp.int32)
        q_head = lax.dynamic_slice_in_dim(all_q, offset, HEAD_DIM, 1)
        k_head = lax.dynamic_slice_in_dim(all_k, offset, HEAD_DIM, 1)
        v_head = lax.dynamic_slice_in_dim(all_v, offset, HEAD_DIM, 1)
        scores = jnp.dot(q_head, k_head.T, preferred_element_type=jnp.float32) * scale
        top = lax.optimization_barrier(jnp.max(jnp.where(allowed, scores, -jnp.inf), axis=1, keepdims=True))
        weights = jnp.where(allowed, jnp.exp(scores - top), 0.0)
        total = lax.optimization_barrier(jnp.sum(weights, axis=1, keepdims=True))
        return jnp.dot(weights.astype(jnp.bfloat16), v_head, preferred_element_type=jnp.float32) / total
    heads_out = lax.map(one_head, jnp.arange(HEADS, dtype=jnp.int32))
    mixed = heads_out.transpose(1, 0, 2).reshape(rows_q, D)
    live_rows = jnp.concatenate([jnp.ones((NEW,), dtype=bool), held_live], axis=0)
    mixed = jnp.where(live_rows[:, None], mixed, 0.0).astype(jnp.bfloat16)
    projected = jnp.dot(mixed, out_weight, preferred_element_type=jnp.float32).astype(jnp.bfloat16)
    return (projected[:NEW], projected[NEW:], cache_keys, cache_values)
```

```python
import functools
import math

import jax
import jax.numpy as jnp
from jax import lax
from jax.experimental import pallas as pl
from jax.experimental.pallas import tpu as pltpu
from jax.sharding import PartitionSpec as P

HEAD_DIM = 128


NEGATIVE = -1e30


def lookup(table, index):
    hits = index[..., None] == jnp.arange(table.shape[0], dtype=jnp.int32)
    return jnp.sum(jnp.where(hits, table, 0), axis=-1)


def pool_blocks(rows, coarse):
    blocks = rows.reshape(-1, 4, rows.shape[-1])
    mean = jnp.mean(blocks.astype(jnp.float32), axis=1).astype(jnp.bfloat16)
    first = (jnp.arange(4) == 0)[None, :, None]
    pooled = jnp.where(first, mean[:, None, :], jnp.zeros_like(blocks))
    return jnp.where(coarse[:, None, None], pooled, blocks)


def group_plan(total_rows, shard_rows):
    shards = total_rows // shard_rows
    group = math.gcd(shards, max(1, 1024 // shard_rows))
    return (shards // group, group)


def attend(state, heads_q, keys, values, allowed, scale):
    best, total, accum = state
    count = keys.shape[0]
    heads = heads_q.shape[0]
    hdim = heads_q.shape[2]
    keys_h = keys.reshape(count, heads, hdim)
    values_h = values.reshape(count, heads, hdim)
    scores = jnp.einsum("hqd,khd->hqk", heads_q, keys_h, preferred_element_type=jnp.float32) * scale
    if allowed is not None:
        scores = jnp.where(allowed[None], scores, NEGATIVE)
    fresh = jnp.maximum(best, jnp.max(scores, axis=2))
    weights = jnp.exp(scores - fresh[..., None])
    if allowed is not None:
        weights = jnp.where(allowed[None], weights, 0.0)
    decay = jnp.exp(best - fresh)
    total = total * decay + jnp.sum(weights, axis=2)
    accum = accum * decay[..., None] + jnp.einsum(
        "hqk,khd->hqd", weights.astype(jnp.bfloat16), values_h, preferred_element_type=jnp.float32
    )
    return (fresh, total, accum)


def per_device(
    queries,
    new_keys,
    new_values,
    context_queries,
    context_keys,
    context_values,
    levels,
    frame_mask,
    owners,
    out_weight,
):
    width = queries.shape[1]
    new_rows = queries.shape[0]
    ctx_rows = context_keys.shape[0]
    blocks_dev = ctx_rows // 4
    devices = lax.axis_size("seq")
    place = lax.axis_index("seq")
    blocks_all = blocks_dev * devices
    frames_ctx = levels.shape[0]
    frames_new = frame_mask.shape[0]
    new_all = new_rows * devices
    hdim = HEAD_DIM
    heads = width // hdim
    scale = 1.0 / math.sqrt(hdim)
    pair = max(2, 2 * blocks_dev // devices)
    block_ids = jnp.arange(blocks_all, dtype=jnp.int32)
    block_frame = block_ids * frames_ctx // blocks_all
    coarse_all = lookup(levels, block_frame) == 1
    mine = owners == place
    rank = jnp.cumsum(mine.astype(jnp.int32)) - 1
    own_coarse = lax.dynamic_slice_in_dim(coarse_all, place * blocks_dev, blocks_dev)
    pooled_q = pool_blocks(context_queries, own_coarse)
    pooled_k = pool_blocks(context_keys, own_coarse)
    pooled_v = pool_blocks(context_values, own_coarse)
    slots = jnp.arange(blocks_dev, dtype=jnp.int32)[:, None] == rank[None, :]
    held_coarse = jnp.any(slots & mine[None, :] & coarse_all[None, :], axis=1)
    held_live = jnp.logical_or(
        jnp.logical_not(held_coarse)[:, None], (jnp.arange(4) == 0)[None, :]
    ).reshape(ctx_rows)
    my_owners = lax.dynamic_slice_in_dim(owners, place * blocks_dev, blocks_dev)
    hits = my_owners[:, None] == jnp.arange(devices, dtype=jnp.int32)[None, :]
    within = jnp.sum(jnp.where(hits, jnp.cumsum(hits.astype(jnp.int32), axis=0) - 1, 0), axis=1)
    send_slot = my_owners * pair + within

    def pack(blocks):
        buffer = jnp.zeros((devices * pair, 4, width), blocks.dtype).at[send_slot].set(blocks)
        return buffer.reshape(devices, pair * 4, width)

    counts = jnp.sum((owners.reshape(devices, blocks_dev) == place).astype(jnp.int32), axis=1)
    before = jnp.cumsum(counts) - counts
    order_in = jnp.arange(pair, dtype=jnp.int32)[None, :]
    target = jnp.where(order_in < counts[:, None], before[:, None] + order_in, blocks_dev).reshape(
        -1
    )

    def unpack(arrived):
        blocks = arrived.reshape(devices * pair, 4, width)
        return jnp.zeros((blocks_dev, 4, width), arrived.dtype).at[target].set(blocks, mode="drop")

    arrived = (
        lax.all_to_all(pack(pooled_q), "seq", split_axis=0, concat_axis=0, tiled=True),
        lax.all_to_all(pack(pooled_k), "seq", split_axis=0, concat_axis=0, tiled=True),
        lax.all_to_all(pack(pooled_v), "seq", split_axis=0, concat_axis=0, tiled=True),
    )
    held_q = unpack(arrived[0])
    held_k = unpack(arrived[1])
    held_v = unpack(arrived[2])
    all_q = jnp.concatenate([queries, held_q.reshape(ctx_rows, width)], axis=0)
    rows_q = all_q.shape[0]
    heads_q = all_q.reshape(rows_q, heads, hdim).transpose(1, 0, 2)
    q_global = place * new_rows + jnp.arange(new_rows, dtype=jnp.int32)
    q_frame = q_global * frames_new // new_all
    frame_hits = (q_frame[:, None] == jnp.arange(frames_new, dtype=jnp.int32)[None, :])[:, :, None]
    new_mask = jnp.sum(jnp.where(frame_hits, frame_mask[None], 0), axis=1)
    query_mask = jnp.concatenate(
        [new_mask, jnp.ones((ctx_rows, frames_ctx), jnp.int32)], axis=0
    ).astype(jnp.float32)

    def context_allowed(first_shard, count_rows):
        index = first_shard * ctx_rows + jnp.arange(count_rows, dtype=jnp.int32)
        frame = index // 4 * frames_ctx // blocks_all
        coarse = lookup(levels, frame) == 1
        live = jnp.logical_or(jnp.logical_not(coarse), index % 4 == 0)
        onehot = (frame[:, None] == jnp.arange(frames_ctx, dtype=jnp.int32)[None, :]).astype(
            jnp.float32
        )
        reach = jnp.dot(query_mask, onehot.T) > 0.5
        return jnp.logical_and(reach, live[None, :])

    def take_new(state, keys, values):
        return attend(state, heads_q, keys, values, None, scale)

    def take_context(state, keys, values, first_shard):
        allowed = context_allowed(first_shard, keys.shape[0])
        return attend(state, heads_q, keys, values, allowed, scale)

    start_state = (
        jnp.full((heads, rows_q), NEGATIVE, jnp.float32),
        jnp.zeros((heads, rows_q), jnp.float32),
        jnp.zeros((heads, rows_q, hdim), jnp.float32),
    )
    empty_cache = (
        jnp.zeros((blocks_dev, 4, width), jnp.bfloat16),
        jnp.zeros((blocks_dev, 4, width), jnp.bfloat16),
    )
    flat_k = pooled_k.reshape(ctx_rows, width)
    flat_v = pooled_v.reshape(ctx_rows, width)
    piece = (
        lax.all_gather(new_keys, "seq", axis=0, tiled=True),
        lax.all_gather(new_values, "seq", axis=0, tiled=True),
    )
    steps, group = group_plan(piece[0].shape[0], new_rows)
    size = group * new_rows
    stacked = (piece[0].reshape(steps, size, width), piece[1].reshape(steps, size, width))

    def one(carry, item):
        return (take_new(carry, item[0], item[1]), None)

    state = lax.scan(one, start_state, stacked)[0]
    piece = (
        lax.all_gather(flat_k, "seq", axis=0, tiled=True),
        lax.all_gather(flat_v, "seq", axis=0, tiled=True),
    )
    steps, group = group_plan(piece[0].shape[0], ctx_rows)
    size = group * ctx_rows
    firsts = jnp.arange(steps, dtype=jnp.int32) * group
    stacked = (piece[0].reshape(steps, size, width), piece[1].reshape(steps, size, width), firsts)

    def one(inner, item):
        keys, values, first = item
        attended = take_context(inner[0], keys, values, first)
        cache = inner[1]
        return ((attended, cache), None)

    state, cache = lax.scan(one, (state, empty_cache), stacked)[0]
    best, total, accum = state
    mixed = (accum / total[..., None]).transpose(1, 0, 2).reshape(rows_q, width)
    live_rows = jnp.concatenate([jnp.ones((new_rows,), dtype=bool), held_live], axis=0)
    mixed = jnp.where(live_rows[:, None], mixed, 0.0).astype(jnp.bfloat16)
    summed = lax.psum_scatter(
        lax.dot_general(
            out_weight, mixed, (((0,), (1,)), ((), ())), preferred_element_type=jnp.float32
        ).astype(jnp.bfloat16),
        "tensor",
        scatter_dimension=0,
        tiled=True,
    ).astype(jnp.float32)
    result = summed.T.astype(jnp.bfloat16)
    return (
        result[:new_rows],
        result[new_rows:],
        held_k.reshape(ctx_rows, width),
        held_v.reshape(ctx_rows, width),
    )


def place_index(shape, dim):
    return lax.broadcasted_iota(jnp.int32, shape, dim)


def coarse_of(frame, levels_ref, frames_ctx):
    coarse = frame < 0
    for f in range(frames_ctx):
        coarse = jnp.logical_or(coarse, jnp.logical_and(frame == f, levels_ref[f] == 1))
    return coarse


def pack_kernel(levels, q, k, v, cq, ck, cv, near, far):
    z = lax.axis_index("seq")
    devices = lax.axis_size("seq")
    new_rows = q.shape[0]
    ctx_rows = cq.shape[0]
    width = q.shape[1]
    half = width // 2
    rows = new_rows + ctx_rows
    frames_ctx = levels.shape[0]
    index = place_index((ctx_rows, 1), 0)
    frame = (z * ctx_rows + index) * frames_ctx // (devices * ctx_rows)
    coarse = coarse_of(frame, levels, frames_ctx)
    first = index % 4 == 0

    def pooled(ref, lanes):
        x = ref[:, lanes]
        wide = x.astype(jnp.float32)
        pairs = wide + pltpu.roll(wide, ctx_rows - 1, 0)
        quads = pairs + pltpu.roll(pairs, ctx_rows - 2, 0)
        mean = jnp.where(first, quads * 0.25, 0.0)
        return jnp.where(coarse, mean, wide).astype(jnp.bfloat16)

    def put(a, b):
        for part, (fresh, ctx) in enumerate(((k, ck), (v, cv), (q, cq))):
            base = part * rows
            for out, lo in ((a, 0), (b, half)):
                lanes = slice(lo, lo + half)
                out[base : base + new_rows] = fresh[:, lanes]
                out[base + new_rows : base + rows] = pooled(ctx, lanes)

    @pl.when(z < devices // 2)
    def _():
        put(near, far)

    @pl.when(z >= devices // 2)
    def _():
        put(far, near)


def plan_kernel(owners, levels, order, alive):
    blocks = owners.shape[1]
    size = order.shape[0]
    per = size // blocks
    devices = lax.axis_size("seq")
    frames_ctx = levels.shape[0]
    row = owners[...].astype(jnp.float32)
    r = place_index((blocks, blocks), 0)
    c = place_index((blocks, blocks), 1)
    col = jnp.sum(jnp.where(r == c, row, 0.0), axis=1, keepdims=True)
    ahead = jnp.logical_and(col == row, r < c)
    rank = jnp.sum(ahead.astype(jnp.float32), axis=0, keepdims=True)
    spot = row * float(blocks // devices) + rank
    spread = (
        place_index((blocks, size), 1) // per == place_index((blocks, size), 0)
    ).astype(jnp.bfloat16)
    wide = jnp.dot(
        jnp.broadcast_to(spot, (16, blocks)).astype(jnp.bfloat16),
        spread,
        preferred_element_type=jnp.float32,
    )[0:1]
    lane = place_index((1, size), 1)
    target = wide.astype(jnp.int32) * per + lane % per
    move = (place_index((size, size), 0) == target).astype(jnp.bfloat16)
    order[...] = move
    index = place_index((size, alive.shape[1]), 0)
    coarse = coarse_of(index * frames_ctx // size, levels, frames_ctx)
    live = jnp.logical_or(jnp.logical_not(coarse), index % per == 0)
    alive[...] = jnp.dot(
        move, live.astype(jnp.bfloat16), preferred_element_type=jnp.float32
    )


def far_places(z):
    across = 3 - z
    beside = jnp.where(z == 1, 0, 3)
    return (z, beside, across, 3 - beside)


def attend_kernel(scale, new_rows, levels, masks, s0, s1, s2, s3, order, alive, o0, o1, o2, o3, kc, va, qc):
    z = lax.axis_index("seq")
    ctx_rows = s0.shape[0] // 3 - new_rows
    rows = new_rows + ctx_rows
    sources = (s0, s1, s2, s3)
    outs = (o0, o1, o2, o3)
    count = len(sources)
    fresh = count * new_rows
    ctx = count * ctx_rows
    hdim = s0.shape[1]
    frames_ctx = levels.shape[0]
    frames_new = masks.shape[0]
    factor = scale * math.log2(math.e)

    @pl.when(jnp.logical_or(z == 1, z == 2))
    def _():
        places = far_places(z)
        va[:, hdim:] = jnp.ones((fresh + ctx, hdim), jnp.bfloat16)
        for i, src in enumerate(sources):
            at = slice(i * new_rows, (i + 1) * new_rows)
            to = pl.ds(pl.multiple_of(fresh + places[i] * ctx_rows, ctx_rows), ctx_rows)
            kc[at] = src[0:new_rows]
            kc[to] = src[new_rows:rows]
            va[at, :hdim] = src[rows : rows + new_rows]
            va[to, :hdim] = src[rows + new_rows : 2 * rows]
            qc[pl.ds(pl.multiple_of(places[i] * ctx_rows, ctx_rows), ctx_rows)] = src[
                2 * rows + new_rows : 3 * rows
            ]
        index = place_index((1, ctx), 1)
        frame = index * frames_ctx // ctx
        live = jnp.logical_or(
            jnp.logical_not(coarse_of(frame, levels, frames_ctx)), index % 4 == 0
        )

        def weigh(q, allowed):
            scores = lax.dot_general(
                q, kc[...], (((1,), (1,)), ((), ())), preferred_element_type=jnp.float32
            )
            bias = jnp.where(allowed, 0.0, NEGATIVE)
            ahead = scores[:, :fresh]
            behind = scores[:, fresh:] + bias
            top = jnp.maximum(
                jnp.max(ahead, axis=1, keepdims=True), jnp.max(behind, axis=1, keepdims=True)
            )
            w_ahead = jnp.exp2((ahead - top) * factor).astype(jnp.bfloat16)
            w_behind = jnp.exp2((behind - top) * factor).astype(jnp.bfloat16)
            both = jnp.dot(
                w_ahead, va[:fresh], preferred_element_type=jnp.float32
            ) + jnp.dot(w_behind, va[fresh:], preferred_element_type=jnp.float32)
            return both[:, :hdim] / both[:, hdim:]

        for i, (src, out) in enumerate(zip(sources, outs)):
            row_frame = places[i] * frames_new // count
            seen = frame < 0
            for f in range(frames_ctx):
                seen = jnp.logical_or(
                    seen, jnp.logical_and(frame == f, masks[row_frame, f] == 1)
                )
            q = src[2 * rows : 2 * rows + new_rows]
            out[0:new_rows] = weigh(q, jnp.logical_and(live, seen)).astype(jnp.bfloat16)
        for i, out in enumerate(outs):
            part = pl.ds(pl.multiple_of(places[i] * ctx_rows, ctx_rows), ctx_rows)
            q = jnp.dot(order[part], qc[...], preferred_element_type=jnp.float32)
            mixed = weigh(q.astype(jnp.bfloat16), live) * alive[part]
            out[new_rows:rows] = mixed.astype(jnp.bfloat16)


def cache_kernel(new_rows, s0, s1, s2, s3, order, c0, c1, c2, c3, kk):
    z = lax.axis_index("seq")
    ctx_rows = s0.shape[0] // 3 - new_rows
    rows = new_rows + ctx_rows
    sources = (s0, s1, s2, s3)
    width = s0.shape[1]

    @pl.when(jnp.logical_or(z == 1, z == 2))
    def _():
        places = far_places(z)
        for i, src in enumerate(sources):
            to = pl.ds(pl.multiple_of(places[i] * ctx_rows, ctx_rows), ctx_rows)
            kk[to, :width] = src[new_rows:rows]
            kk[to, width:] = src[rows + new_rows : 2 * rows]
        for i, out in enumerate((c0, c1, c2, c3)):
            part = pl.ds(pl.multiple_of(places[i] * ctx_rows, ctx_rows), ctx_rows)
            moved = jnp.dot(order[part], kk[...], preferred_element_type=jnp.float32)
            out[:ctx_rows] = moved[:, :width].astype(jnp.bfloat16)
            out[ctx_rows:] = moved[:, width:].astype(jnp.bfloat16)


def halves(z, own, beside, across, beyond):
    own, beside, across, beyond = own[...], beside[...], across[...], beyond[...]
    inner = jnp.logical_or(z == 1, z == 2)
    low = z < 2
    near = jnp.where(inner, own, beside)
    far = jnp.where(inner, across, beyond)
    return (jnp.where(low, near, far), jnp.where(low, far, near))


def project_kernel(cols, o0, o1, o2, o3, weight, out):
    z = lax.axis_index("seq")
    a, b = halves(z, o0, o1, o2, o3)
    half = a.shape[1]
    total = jnp.dot(a, weight[:half], preferred_element_type=jnp.float32)
    total += jnp.dot(b, weight[half:], preferred_element_type=jnp.float32)
    out[...] = total.astype(out.dtype)


def add_kernel(keep, came, out):
    chip = lax.axis_index("tensor") // 2
    rows = out.shape[0]
    at = pl.ds(pl.multiple_of((1 - chip) * rows, rows), rows)
    out[...] = (keep[at] + came[at].astype(jnp.float32)).astype(jnp.bfloat16)


def finish_kernel(keep, came, last, out, out_ctx):
    chip = lax.axis_index("tensor") // 2
    rows = last.shape[0]
    at = pl.ds(pl.multiple_of(chip * rows, rows), rows)
    total = keep[at] + came[at].astype(jnp.float32) + last[...].astype(jnp.float32)
    total = total.astype(jnp.bfloat16)
    out[...] = total[: out.shape[0]]
    out_ctx[...] = total[out.shape[0] :]


def store_kernel(c0, c1, c2, c3, keys, values):
    z = lax.axis_index("seq")
    a, b = halves(z, c0, c1, c2, c3)
    half = a.shape[1]
    ctx_rows = keys.shape[0]
    keys[:, :half] = a[:ctx_rows]
    keys[:, half:] = b[:ctx_rows]
    values[:, :half] = a[ctx_rows:]
    values[:, half:] = b[ctx_rows:]


SMALL = pl.BlockSpec(memory_space=pltpu.SMEM)
LIMIT = pltpu.CompilerParams(vmem_limit_bytes=48 * 1024 * 1024)


def shape16(*dims):
    return jax.ShapeDtypeStruct(dims, jnp.bfloat16)


def permute(x, pairs):
    return lax.ppermute(x, "seq", pairs)


BESIDE = ((0, 1), (3, 2))
ACROSS = ((1, 2), (2, 1))
BEYOND = ((0, 2), (3, 1))


def back(pairs):
    return tuple((b, a) for a, b in pairs)


def fast_device(
    queries,
    new_keys,
    new_values,
    context_queries,
    context_keys,
    context_values,
    levels,
    frame_mask,
    owners,
    out_weight,
):
    new_rows, width = queries.shape
    ctx_rows = context_keys.shape[0]
    rows = new_rows + ctx_rows
    half = width // 2
    devices = lax.axis_size("seq")
    ctx_all = ctx_rows * devices
    hdim = HEAD_DIM
    scale = 1.0 / math.sqrt(hdim)
    whole = pl.BlockSpec()
    near, far = pl.pallas_call(
        pack_kernel,
        out_shape=(shape16(3 * rows, half), shape16(3 * rows, half)),
        in_specs=[SMALL] + [whole] * 6,
        compiler_params=LIMIT,
    )(levels, queries, new_keys, new_values, context_queries, context_keys, context_values)
    beside = permute(near, BESIDE)
    across = permute(far, ACROSS)
    beyond = permute(far, BEYOND)
    order, alive = pl.pallas_call(
        plan_kernel,
        out_shape=(shape16(ctx_all, ctx_all), jax.ShapeDtypeStruct((ctx_all, hdim), jnp.float32)),
        in_specs=[whole, SMALL],
        compiler_params=LIMIT,
    )(owners.reshape(1, -1), levels)
    per_head = lambda length: pl.BlockSpec((length, hdim), lambda h: (0, h))
    mixed = pl.pallas_call(
        functools.partial(attend_kernel, scale, new_rows),
        grid=(half // hdim,),
        out_shape=[shape16(rows, half)] * 4,
        in_specs=[SMALL, SMALL]
        + [per_head(3 * rows)] * 4
        + [
            pl.BlockSpec((ctx_all, ctx_all), lambda h: (0, 0)),
            pl.BlockSpec((ctx_all, hdim), lambda h: (0, 0)),
        ],
        out_specs=[per_head(rows)] * 4,
        scratch_shapes=[
            pltpu.VMEM((rows * devices, hdim), jnp.bfloat16),
            pltpu.VMEM((rows * devices, 2 * hdim), jnp.bfloat16),
            pltpu.VMEM((ctx_all, hdim), jnp.bfloat16),
        ],
        compiler_params=LIMIT,
    )(levels, frame_mask, near, beside, across, beyond, order, alive)
    got = (
        mixed[0],
        permute(mixed[1], back(BESIDE)),
        permute(mixed[2], ACROSS),
        permute(mixed[3], back(BEYOND)),
    )
    caches = pl.pallas_call(
        functools.partial(cache_kernel, new_rows),
        out_shape=[shape16(2 * ctx_rows, half)] * 4,
        scratch_shapes=[pltpu.VMEM((ctx_all, width), jnp.bfloat16)],
        compiler_params=LIMIT,
    )(near, beside, across, beyond, order)

    def project(which, dtype):
        def column(p, me):
            core = me[0] % 2
            return (0, 2 * p + (core if which else 1 - core))

        full = pl.BlockSpec((rows, half), lambda p, me: (0, 0))
        return pl.pallas_call(
            lambda me, *refs: project_kernel(width, *refs),
            grid_spec=pltpu.PrefetchScalarGridSpec(
                num_scalar_prefetch=1,
                grid=(2,),
                in_specs=[full] * 4 + [pl.BlockSpec((width, width), column)],
                out_specs=pl.BlockSpec((rows, width), lambda p, me: (p, 0)),
            ),
            out_shape=jax.ShapeDtypeStruct((2 * rows, width), dtype),
            compiler_params=LIMIT,
        )(me, *got, out_weight)

    me = lax.axis_index("tensor").reshape(1).astype(jnp.int32)
    give = project(False, jnp.bfloat16)
    came = lax.ppermute(give, "tensor", ((0, 1), (1, 0), (2, 3), (3, 2)))
    keep = project(True, jnp.float32)
    other = pl.pallas_call(add_kernel, out_shape=shape16(rows, width), compiler_params=LIMIT)(
        keep, came
    )
    last = lax.ppermute(other, "tensor", ((0, 2), (2, 0), (1, 3), (3, 1)))
    stored = (
        caches[0],
        permute(caches[1], back(BESIDE)),
        permute(caches[2], ACROSS),
        permute(caches[3], back(BEYOND)),
    )
    cache_keys, cache_values = pl.pallas_call(
        store_kernel,
        out_shape=(shape16(ctx_rows, width), shape16(ctx_rows, width)),
        compiler_params=LIMIT,
    )(*stored)
    block_out, context_out = pl.pallas_call(
        finish_kernel,
        out_shape=(shape16(new_rows, width), shape16(ctx_rows, width)),
        compiler_params=LIMIT,
    )(keep, came, last)
    return (block_out, context_out, cache_keys, cache_values)


def fits_fast(mesh):
    sizes = mesh.shape
    return sizes["seq"] == 4 and sizes["tensor"] == 4


def solution(mesh):
    in_specs = (
        P(("session", "seq"), "tensor"),
        P(("session", "seq"), "tensor"),
        P(("session", "seq"), "tensor"),
        P(("session", "seq"), "tensor"),
        P(("session", "seq"), "tensor"),
        P(("session", "seq"), "tensor"),
        P("session"),
        P("session", None),
        P("session"),
        P("tensor", None),
    )
    out_specs = (
        P(("session", "seq"), "tensor"),
        P(("session", "seq"), "tensor"),
        P(("session", "seq"), "tensor"),
        P(("session", "seq"), "tensor"),
    )
    step = fast_device if fits_fast(mesh) else per_device
    return jax.shard_map(step, mesh=mesh, in_specs=in_specs, out_specs=out_specs, check_vma=False)
```

```python
import functools
import math

import jax
import jax.numpy as jnp
from jax import lax
from jax.experimental import pallas as pl
from jax.experimental.pallas import tpu as pltpu
from jax.sharding import PartitionSpec as P

HEAD_DIM = 128


NEGATIVE = -1e30


def lookup(table, index):
    hits = index[..., None] == jnp.arange(table.shape[0], dtype=jnp.int32)
    return jnp.sum(jnp.where(hits, table, 0), axis=-1)


def pool_blocks(rows, coarse):
    blocks = rows.reshape(-1, 4, rows.shape[-1])
    mean = jnp.mean(blocks.astype(jnp.float32), axis=1).astype(jnp.bfloat16)
    first = (jnp.arange(4) == 0)[None, :, None]
    pooled = jnp.where(first, mean[:, None, :], jnp.zeros_like(blocks))
    return jnp.where(coarse[:, None, None], pooled, blocks)


def group_plan(total_rows, shard_rows):
    shards = total_rows // shard_rows
    group = math.gcd(shards, max(1, 1024 // shard_rows))
    return (shards // group, group)


def attend(state, heads_q, keys, values, allowed, scale):
    best, total, accum = state
    count = keys.shape[0]
    heads = heads_q.shape[0]
    hdim = heads_q.shape[2]
    keys_h = keys.reshape(count, heads, hdim)
    values_h = values.reshape(count, heads, hdim)
    scores = jnp.einsum("hqd,khd->hqk", heads_q, keys_h, preferred_element_type=jnp.float32) * scale
    if allowed is not None:
        scores = jnp.where(allowed[None], scores, NEGATIVE)
    fresh = jnp.maximum(best, jnp.max(scores, axis=2))
    weights = jnp.exp(scores - fresh[..., None])
    if allowed is not None:
        weights = jnp.where(allowed[None], weights, 0.0)
    decay = jnp.exp(best - fresh)
    total = total * decay + jnp.sum(weights, axis=2)
    accum = accum * decay[..., None] + jnp.einsum(
        "hqk,khd->hqd", weights.astype(jnp.bfloat16), values_h, preferred_element_type=jnp.float32
    )
    return (fresh, total, accum)


def per_device(
    queries,
    new_keys,
    new_values,
    context_queries,
    context_keys,
    context_values,
    levels,
    frame_mask,
    owners,
    out_weight,
):
    width = queries.shape[1]
    new_rows = queries.shape[0]
    ctx_rows = context_keys.shape[0]
    blocks_dev = ctx_rows // 4
    devices = lax.axis_size("seq")
    place = lax.axis_index("seq")
    blocks_all = blocks_dev * devices
    frames_ctx = levels.shape[0]
    frames_new = frame_mask.shape[0]
    new_all = new_rows * devices
    hdim = HEAD_DIM
    heads = width // hdim
    scale = 1.0 / math.sqrt(hdim)
    pair = max(2, 2 * blocks_dev // devices)
    block_ids = jnp.arange(blocks_all, dtype=jnp.int32)
    block_frame = block_ids * frames_ctx // blocks_all
    coarse_all = lookup(levels, block_frame) == 1
    mine = owners == place
    rank = jnp.cumsum(mine.astype(jnp.int32)) - 1
    own_coarse = lax.dynamic_slice_in_dim(coarse_all, place * blocks_dev, blocks_dev)
    pooled_q = pool_blocks(context_queries, own_coarse)
    pooled_k = pool_blocks(context_keys, own_coarse)
    pooled_v = pool_blocks(context_values, own_coarse)
    slots = jnp.arange(blocks_dev, dtype=jnp.int32)[:, None] == rank[None, :]
    held_coarse = jnp.any(slots & mine[None, :] & coarse_all[None, :], axis=1)
    held_live = jnp.logical_or(
        jnp.logical_not(held_coarse)[:, None], (jnp.arange(4) == 0)[None, :]
    ).reshape(ctx_rows)
    my_owners = lax.dynamic_slice_in_dim(owners, place * blocks_dev, blocks_dev)
    hits = my_owners[:, None] == jnp.arange(devices, dtype=jnp.int32)[None, :]
    within = jnp.sum(jnp.where(hits, jnp.cumsum(hits.astype(jnp.int32), axis=0) - 1, 0), axis=1)
    send_slot = my_owners * pair + within

    def pack(blocks):
        buffer = jnp.zeros((devices * pair, 4, width), blocks.dtype).at[send_slot].set(blocks)
        return buffer.reshape(devices, pair * 4, width)

    counts = jnp.sum((owners.reshape(devices, blocks_dev) == place).astype(jnp.int32), axis=1)
    before = jnp.cumsum(counts) - counts
    order_in = jnp.arange(pair, dtype=jnp.int32)[None, :]
    target = jnp.where(order_in < counts[:, None], before[:, None] + order_in, blocks_dev).reshape(
        -1
    )

    def unpack(arrived):
        blocks = arrived.reshape(devices * pair, 4, width)
        return jnp.zeros((blocks_dev, 4, width), arrived.dtype).at[target].set(blocks, mode="drop")

    arrived = (
        lax.all_to_all(pack(pooled_q), "seq", split_axis=0, concat_axis=0, tiled=True),
        lax.all_to_all(pack(pooled_k), "seq", split_axis=0, concat_axis=0, tiled=True),
        lax.all_to_all(pack(pooled_v), "seq", split_axis=0, concat_axis=0, tiled=True),
    )
    held_q = unpack(arrived[0])
    held_k = unpack(arrived[1])
    held_v = unpack(arrived[2])
    all_q = jnp.concatenate([queries, held_q.reshape(ctx_rows, width)], axis=0)
    rows_q = all_q.shape[0]
    heads_q = all_q.reshape(rows_q, heads, hdim).transpose(1, 0, 2)
    q_global = place * new_rows + jnp.arange(new_rows, dtype=jnp.int32)
    q_frame = q_global * frames_new // new_all
    frame_hits = (q_frame[:, None] == jnp.arange(frames_new, dtype=jnp.int32)[None, :])[:, :, None]
    new_mask = jnp.sum(jnp.where(frame_hits, frame_mask[None], 0), axis=1)
    query_mask = jnp.concatenate(
        [new_mask, jnp.ones((ctx_rows, frames_ctx), jnp.int32)], axis=0
    ).astype(jnp.float32)

    def context_allowed(first_shard, count_rows):
        index = first_shard * ctx_rows + jnp.arange(count_rows, dtype=jnp.int32)
        frame = index // 4 * frames_ctx // blocks_all
        coarse = lookup(levels, frame) == 1
        live = jnp.logical_or(jnp.logical_not(coarse), index % 4 == 0)
        onehot = (frame[:, None] == jnp.arange(frames_ctx, dtype=jnp.int32)[None, :]).astype(
            jnp.float32
        )
        reach = jnp.dot(query_mask, onehot.T) > 0.5
        return jnp.logical_and(reach, live[None, :])

    def take_new(state, keys, values):
        return attend(state, heads_q, keys, values, None, scale)

    def take_context(state, keys, values, first_shard):
        allowed = context_allowed(first_shard, keys.shape[0])
        return attend(state, heads_q, keys, values, allowed, scale)

    start_state = (
        jnp.full((heads, rows_q), NEGATIVE, jnp.float32),
        jnp.zeros((heads, rows_q), jnp.float32),
        jnp.zeros((heads, rows_q, hdim), jnp.float32),
    )
    empty_cache = (
        jnp.zeros((blocks_dev, 4, width), jnp.bfloat16),
        jnp.zeros((blocks_dev, 4, width), jnp.bfloat16),
    )
    flat_k = pooled_k.reshape(ctx_rows, width)
    flat_v = pooled_v.reshape(ctx_rows, width)
    piece = (
        lax.all_gather(new_keys, "seq", axis=0, tiled=True),
        lax.all_gather(new_values, "seq", axis=0, tiled=True),
    )
    steps, group = group_plan(piece[0].shape[0], new_rows)
    size = group * new_rows
    stacked = (piece[0].reshape(steps, size, width), piece[1].reshape(steps, size, width))

    def one(carry, item):
        return (take_new(carry, item[0], item[1]), None)

    state = lax.scan(one, start_state, stacked)[0]
    piece = (
        lax.all_gather(flat_k, "seq", axis=0, tiled=True),
        lax.all_gather(flat_v, "seq", axis=0, tiled=True),
    )
    steps, group = group_plan(piece[0].shape[0], ctx_rows)
    size = group * ctx_rows
    firsts = jnp.arange(steps, dtype=jnp.int32) * group
    stacked = (piece[0].reshape(steps, size, width), piece[1].reshape(steps, size, width), firsts)

    def one(inner, item):
        keys, values, first = item
        attended = take_context(inner[0], keys, values, first)
        cache = inner[1]
        return ((attended, cache), None)

    state, cache = lax.scan(one, (state, empty_cache), stacked)[0]
    best, total, accum = state
    mixed = (accum / total[..., None]).transpose(1, 0, 2).reshape(rows_q, width)
    live_rows = jnp.concatenate([jnp.ones((new_rows,), dtype=bool), held_live], axis=0)
    mixed = jnp.where(live_rows[:, None], mixed, 0.0).astype(jnp.bfloat16)
    summed = lax.psum_scatter(
        lax.dot_general(
            out_weight, mixed, (((0,), (1,)), ((), ())), preferred_element_type=jnp.float32
        ).astype(jnp.bfloat16),
        "tensor",
        scatter_dimension=0,
        tiled=True,
    ).astype(jnp.float32)
    result = summed.T.astype(jnp.bfloat16)
    return (
        result[:new_rows],
        result[new_rows:],
        held_k.reshape(ctx_rows, width),
        held_v.reshape(ctx_rows, width),
    )


def place_index(shape, dim):
    return lax.broadcasted_iota(jnp.int32, shape, dim)


def coarse_of(frame, levels_ref, frames_ctx):
    coarse = frame < 0
    for f in range(frames_ctx):
        coarse = jnp.logical_or(coarse, jnp.logical_and(frame == f, levels_ref[f] == 1))
    return coarse


def pack_kernel(levels, q, k, v, cq, ck, cv, near_a, near_b, far_a, far_b, lv, sq, sk, sv, sems):
    z = lax.axis_index("seq")
    devices = lax.axis_size("seq")
    new_rows, width = q.shape
    ctx_rows = cq.shape[0]
    half = width // 2
    rows = new_rows + ctx_rows
    frames_ctx = levels.shape[0]
    low = jnp.where(z < devices // 2, 0, half)
    near_lanes = pl.ds(pl.multiple_of(low, 128), half)
    far_lanes = pl.ds(pl.multiple_of(half - low, 128), half)
    pairs = [(levels, lv), (ck, sk), (cv, sv), (cq, sq)]
    for out_a, out_b, lanes in ((far_a, far_b, far_lanes), (near_a, near_b, near_lanes)):
        pairs.append((k.at[:, lanes], out_a.at[0:new_rows]))
        pairs.append((v.at[:, lanes], out_a.at[rows : rows + new_rows]))
        pairs.append((q.at[:, lanes], out_b))
    copies = [pltpu.make_async_copy(src, dst, sems.at[i]) for i, (src, dst) in enumerate(pairs)]
    for copy in copies:
        copy.start()
    index = place_index((ctx_rows, 1), 0)
    first = index % 4 == 0
    copies[0].wait()
    frame = (z * ctx_rows + index) * frames_ctx // (devices * ctx_rows)
    coarse = coarse_of(frame, lv, frames_ctx)
    for part, (ref, copy) in enumerate(((sk, copies[1]), (sv, copies[2]), (sq, copies[3]))):
        copy.wait()
        at = slice(part * rows + new_rows, (part + 1) * rows)
        if part == 2:
            at = slice(2 * rows, 2 * rows + ctx_rows)
        for out, lanes in ((far_a, far_lanes), (near_a, near_lanes)):
            wide = ref[:, lanes].astype(jnp.float32)
            pair = wide + pltpu.roll(wide, ctx_rows - 1, 0)
            quad = pair + pltpu.roll(pair, ctx_rows - 2, 0)
            mean = jnp.where(first, quad * 0.25, 0.0)
            out[at] = jnp.where(coarse, mean, wide).astype(jnp.bfloat16)
    for copy in copies[4:]:
        copy.wait()


def plan_kernel(owners, levels, masks, order, alive, biases):
    blocks = owners.shape[1]
    size = order.shape[0]
    per = size // blocks
    devices = lax.axis_size("seq")
    frames_ctx = levels.shape[0]
    row = owners[...].astype(jnp.float32)
    r = place_index((blocks, blocks), 0)
    c = place_index((blocks, blocks), 1)
    col = jnp.sum(jnp.where(r == c, row, 0.0), axis=1, keepdims=True)
    ahead = jnp.logical_and(col == row, r < c)
    rank = jnp.sum(ahead.astype(jnp.float32), axis=0, keepdims=True)
    spot = row * float(blocks // devices) + rank
    spread = (
        place_index((blocks, size), 1) // per == place_index((blocks, size), 0)
    ).astype(jnp.bfloat16)
    wide = jnp.dot(
        jnp.broadcast_to(spot, (16, blocks)).astype(jnp.bfloat16),
        spread,
        preferred_element_type=jnp.float32,
    )[0:1]
    lane = place_index((1, size), 1)
    target = wide.astype(jnp.int32) * per + lane % per
    move = (place_index((size, size), 0) == target).astype(jnp.bfloat16)
    order[...] = move
    index = place_index((size, alive.shape[1]), 0)
    coarse = coarse_of(index * frames_ctx // size, levels, frames_ctx)
    live = jnp.logical_or(jnp.logical_not(coarse), index % per == 0)
    alive[...] = jnp.dot(
        move, live.astype(jnp.bfloat16), preferred_element_type=jnp.float32
    )
    frame = lane * frames_ctx // size
    live = jnp.logical_or(
        jnp.logical_not(coarse_of(frame, levels, frames_ctx)), lane % per == 0
    )
    biases[...] = jnp.zeros_like(biases)
    biases[0:1] = jnp.where(live, 0.0, NEGATIVE)
    for g in range(masks.shape[0]):
        seen = frame < 0
        for f in range(frames_ctx):
            seen = jnp.logical_or(seen, jnp.logical_and(frame == f, masks[g, f] == 1))
        biases[g + 1 : g + 2] = jnp.where(jnp.logical_and(live, seen), 0.0, NEGATIVE)


def far_places(z):
    across = 3 - z
    beside = jnp.where(z == 1, 0, 3)
    return (z, beside, across, 3 - beside)


def middle(z):
    return jnp.logical_or(z == 1, z == 2)


def run_jobs(jobs, keys, values, fresh, factor):
    hdim = values.shape[2] // 2

    def score(head, q):
        lanes = slice(head * hdim, (head + 1) * hdim)
        return lax.dot_general(
            q, keys[:, lanes], (((1,), (1,)), ((), ())), preferred_element_type=jnp.float32
        )

    def finish(head, scores, bias):
        ahead = scores[:, :fresh]
        behind = scores[:, fresh:] + bias
        top = jnp.maximum(
            jnp.max(ahead, axis=1, keepdims=True), jnp.max(behind, axis=1, keepdims=True)
        )
        w_ahead = jnp.exp2((ahead - top) * factor).astype(jnp.bfloat16)
        w_behind = jnp.exp2((behind - top) * factor).astype(jnp.bfloat16)
        both = jnp.dot(
            w_ahead, values[head, :fresh], preferred_element_type=jnp.float32
        ) + jnp.dot(w_behind, values[head, fresh:], preferred_element_type=jnp.float32)
        return both[:, :hdim] / both[:, hdim:]

    held = None
    for job in [*jobs, None]:
        scores = None if job is None else score(job[0], job[1]())
        if held is not None:
            held[3](finish(held[0], held[4], held[2]))
        held = None if job is None else (*job, scores)


def first_kernel(
    factor, new_rows, frames_new,
    a0, a1, a2, a3, b0, order, alive, biases,
    keys, values, n0, qc,
):
    z = lax.axis_index("seq")
    ctx_rows = qc.shape[0] // 4
    rows = new_rows + ctx_rows
    fresh = 4 * new_rows
    heads = values.shape[0]
    hdim = values.shape[2] // 2

    @pl.when(middle(z))
    def _():
        places = far_places(z)
        values[:, :, hdim:] = jnp.ones((heads, values.shape[1], hdim), jnp.bfloat16)
        for i, src in enumerate((a0, a1, a2, a3)):
            at = slice(i * new_rows, (i + 1) * new_rows)
            spot = pl.multiple_of(places[i] * ctx_rows, ctx_rows)
            to = pl.ds(fresh + spot, ctx_rows)
            keys[at] = src[0:new_rows]
            keys[to] = src[new_rows:rows]
            for h in range(heads):
                lanes = slice(h * hdim, (h + 1) * hdim)
                values[h, at, :hdim] = src[rows : rows + new_rows, lanes]
                values[h, to, :hdim] = src[rows + new_rows : 2 * rows, lanes]
            qc[pl.ds(spot, ctx_rows)] = src[2 * rows : 2 * rows + ctx_rows]
        qc[...] = jnp.dot(order[...], qc[...], preferred_element_type=jnp.float32).astype(
            jnp.bfloat16
        )
        mine = biases[pl.ds(1 + z * frames_new // 4, 1)]
        jobs = []
        for h in range(heads):
            lanes = slice(h * hdim, (h + 1) * hdim)

            def put_ctx(r, lanes=lanes):
                qc[:, lanes] = (r * alive[...]).astype(jnp.bfloat16)

            def put_new(r, lanes=lanes):
                n0[:, lanes] = r.astype(jnp.bfloat16)

            jobs.append((h, lambda lanes=lanes: qc[:, lanes], biases[0:1], put_ctx))
            jobs.append((h, lambda lanes=lanes: b0[:, lanes], mine, put_new))
        run_jobs(jobs, keys, values, fresh, factor)


def second_kernel(
    factor, frames_new, b1, b2, b3, keys, values, biases, n0, held, o0, o1, o2, o3
):
    z = lax.axis_index("seq")
    new_rows = b1.shape[0]
    ctx_rows = held.shape[0] // 4
    heads = values.shape[0]
    hdim = values.shape[2] // 2

    @pl.when(middle(z))
    def _():
        places = far_places(z)
        near = biases[pl.ds(1 + places[1] * frames_new // 4, 1)]
        away = biases[pl.ds(1 + places[2] * frames_new // 4, 1)]
        jobs = []
        for h in range(heads):
            lanes = slice(h * hdim, (h + 1) * hdim)

            def put_near(r, lanes=lanes):
                o1[:new_rows, lanes] = r.astype(jnp.bfloat16)

            def put_away(r, lanes=lanes):
                o2[:new_rows, lanes] = r[:new_rows].astype(jnp.bfloat16)
                o3[:new_rows, lanes] = r[new_rows:].astype(jnp.bfloat16)

            def two(lanes=lanes):
                return jnp.concatenate([b2[:, lanes], b3[:, lanes]], axis=0)

            jobs.append((h, two, away, put_away))
            jobs.append((h, lambda lanes=lanes: b1[:, lanes], near, put_near))
        run_jobs(jobs, keys, values, 4 * new_rows, factor)
        o0[:new_rows] = n0[...]
        for place, out in zip(places, (o0, o1, o2, o3)):
            part = pl.ds(pl.multiple_of(place * ctx_rows, ctx_rows), ctx_rows)
            out[new_rows:] = held[part]


def cache_kernel(new_rows, a0, a1, a2, a3, order, c0, c1, c2, c3, kk):
    z = lax.axis_index("seq")
    ctx_rows = c0.shape[0] // 2
    rows = new_rows + ctx_rows
    width = a0.shape[1]

    @pl.when(middle(z))
    def _():
        places = far_places(z)
        for place, src in zip(places, (a0, a1, a2, a3)):
            to = pl.ds(pl.multiple_of(place * ctx_rows, ctx_rows), ctx_rows)
            kk[to, :width] = src[new_rows:rows]
            kk[to, width:] = src[rows + new_rows : 2 * rows]
        for place, out in zip(places, (c0, c1, c2, c3)):
            part = pl.ds(pl.multiple_of(place * ctx_rows, ctx_rows), ctx_rows)
            moved = jnp.dot(order[part], kk[...], preferred_element_type=jnp.float32)
            out[:ctx_rows] = moved[:, :width].astype(jnp.bfloat16)
            out[ctx_rows:] = moved[:, width:].astype(jnp.bfloat16)


def halves(z, at, *parts):
    own, beside, across, beyond = (part[at] for part in parts)
    inner = middle(z)
    low = z < 2
    near = jnp.where(inner, own, beside)
    far = jnp.where(inner, across, beyond)
    return (jnp.where(low, near, far), jnp.where(low, far, near))


def project_kernel(mine, here, o0, o1, o3, o2, weight, out):
    a, b = halves(lax.axis_index("seq"), slice(None), o0, o1, o2, o3)
    mixed = jnp.concatenate([a, b], axis=1)
    width = mixed.shape[1]
    me = lax.axis_index("tensor")
    core = me % 2 if mine else 1 - me % 2
    chip = me // 2 if here else 1 - me // 2
    lanes = pl.ds(pl.multiple_of((2 * chip + core) * width, width), width)
    total = jnp.dot(mixed, weight[:, lanes], preferred_element_type=jnp.float32)
    out[...] = total.astype(out.dtype)


def add_kernel(keep, came, out):
    out[...] = (keep[...] + came[...].astype(jnp.float32)).astype(jnp.bfloat16)


def finish_kernel(last, keep, came, out, out_ctx):
    total = keep[...] + came[...].astype(jnp.float32) + last[...].astype(jnp.float32)
    total = total.astype(jnp.bfloat16)
    out[...] = total[: out.shape[0]]
    out_ctx[...] = total[out.shape[0] :]


def store_kernel(c0, c3, c2, c1, keys, values):
    z = lax.axis_index("seq")
    ctx_rows, width = keys.shape
    half = width // 2
    for i, out in enumerate((keys, values)):
        at = slice(i * ctx_rows, (i + 1) * ctx_rows)
        a, b = halves(z, at, c0, c1, c2, c3)
        out[:, :half] = a
        out[:, half:] = b


SMALL = pl.BlockSpec(memory_space=pltpu.SMEM)
AWAY = pl.BlockSpec(memory_space=pltpu.HBM)
WHOLE = pl.BlockSpec(memory_space=pltpu.VMEM)
LIMIT = pltpu.CompilerParams(vmem_limit_bytes=32 * 1024 * 1024)


def lasts(us):
    return pl.CostEstimate(flops=int(us * 1.1e9), bytes_accessed=0, transcendentals=0)


def shape16(*dims):
    return jax.ShapeDtypeStruct(dims, jnp.bfloat16)


def permute(x, pairs):
    return lax.ppermute(x, "seq", pairs)


BESIDE = ((0, 1), (3, 2))
ACROSS = ((1, 2), (2, 1))
BEYOND = ((0, 2), (3, 1))
SIBLING = ((0, 1), (1, 0), (2, 3), (3, 2))
OPPOSITE = ((0, 2), (2, 0), (1, 3), (3, 1))


def back(pairs):
    return tuple((b, a) for a, b in pairs)


def home(own, beside, across, beyond):
    return (
        own,
        permute(beside, back(BESIDE)),
        permute(across, ACROSS),
        permute(beyond, back(BEYOND)),
    )


def fast_device(
    queries,
    new_keys,
    new_values,
    context_queries,
    context_keys,
    context_values,
    levels,
    frame_mask,
    owners,
    out_weight,
):
    new_rows, width = queries.shape
    ctx_rows = context_keys.shape[0]
    rows = new_rows + ctx_rows
    half = width // 2
    devices = lax.axis_size("seq")
    ctx_all = ctx_rows * devices
    hdim = HEAD_DIM
    heads = half // hdim
    frames_new = frame_mask.shape[0]
    factor = math.log2(math.e) / math.sqrt(hdim)
    near_a, near_b, far_a, far_b = pl.pallas_call(
        pack_kernel,
        out_shape=(
            shape16(2 * rows + ctx_rows, half),
            shape16(new_rows, half),
            shape16(2 * rows + ctx_rows, half),
            shape16(new_rows, half),
        ),
        in_specs=[AWAY] * 7,
        out_specs=[WHOLE] * 4,
        scratch_shapes=[pltpu.SMEM(levels.shape, jnp.int32)]
        + [pltpu.VMEM((ctx_rows, width), jnp.bfloat16)] * 3
        + [pltpu.SemaphoreType.DMA((10,))],
        name="pack",
    )(levels, queries, new_keys, new_values, context_queries, context_keys, context_values)
    beside_a = permute(near_a, BESIDE)
    across_a = permute(far_a, ACROSS)
    beyond_a = permute(far_a, BEYOND)
    near_b, far_b = lax.optimization_barrier((near_b, far_b, beside_a))[:2]
    beside_b = permute(near_b, BESIDE)
    across_b = permute(far_b, ACROSS)
    beyond_b = permute(far_b, BEYOND)
    order, alive, biases = pl.pallas_call(
        plan_kernel,
        out_shape=(
            shape16(ctx_all, ctx_all),
            jax.ShapeDtypeStruct((ctx_all, hdim), jnp.float32),
            jax.ShapeDtypeStruct((8, ctx_all), jnp.float32),
        ),
        in_specs=[WHOLE, SMALL, SMALL],
        compiler_params=LIMIT,
        name="plan", cost_estimate=lasts(1.6),
    )(owners.reshape(1, -1), levels, frame_mask)
    keys, values, n0, held = pl.pallas_call(
        functools.partial(first_kernel, factor, new_rows, frames_new),
        out_shape=[
            shape16(rows * devices, half),
            shape16(heads, rows * devices, 2 * hdim),
            shape16(new_rows, half),
            shape16(ctx_all, half),
        ],
        compiler_params=LIMIT,
        name="attend_first",
        cost_estimate=lasts(4.4),
    )(near_a, beside_a, across_a, beyond_a, near_b, order, alive, biases)
    results = pl.pallas_call(
        functools.partial(second_kernel, factor, frames_new),
        out_shape=[shape16(rows, half)] * 4,
        compiler_params=LIMIT,
        name="attend_second",
        cost_estimate=lasts(3.0),
    )(beside_b, across_b, beyond_b, keys, values, biases, n0, held)
    mixed = home(*results)
    near_a = lax.optimization_barrier((near_a, results[0]))[0]
    caches = pl.pallas_call(
        functools.partial(cache_kernel, new_rows),
        out_shape=[shape16(2 * ctx_rows, half)] * 4,
        scratch_shapes=[pltpu.VMEM((ctx_all, width), jnp.bfloat16)],
        compiler_params=LIMIT,
        name="caches",
        cost_estimate=lasts(0.8),
    )(near_a, beside_a, across_a, beyond_a, order)

    def project(mine, here, dtype):
        return pl.pallas_call(
            functools.partial(project_kernel, mine, here),
            out_shape=jax.ShapeDtypeStruct((rows, width), dtype),
            in_specs=[WHOLE] * 5,
            compiler_params=LIMIT,
            name=("keep" if mine else "give") + ("_here" if here else "_there"),
            cost_estimate=lasts(0.6),
        )(mixed[0], mixed[1], mixed[3], mixed[2], out_weight)

    came_there = lax.ppermute(project(False, False, jnp.bfloat16), "tensor", SIBLING)
    keep_there = project(True, False, jnp.float32)
    other = pl.pallas_call(
        add_kernel,
        out_shape=shape16(rows, width),
        compiler_params=LIMIT,
        name="add",
        cost_estimate=lasts(0.1),
    )(keep_there, came_there)
    last = lax.ppermute(other, "tensor", OPPOSITE)
    caches = lax.optimization_barrier((*caches, other))[:4]
    beyond = permute(caches[3], back(BEYOND))
    across = permute(caches[2], ACROSS)
    beside = permute(caches[1], back(BESIDE))
    stored = (caches[0], beyond, across, beside)
    mixed = lax.optimization_barrier((*mixed, other))[:4]
    came = lax.ppermute(project(False, True, jnp.bfloat16), "tensor", SIBLING)
    keep = project(True, True, jnp.float32)
    block_out, context_out = pl.pallas_call(
        finish_kernel,
        out_shape=(shape16(new_rows, width), shape16(ctx_rows, width)),
        compiler_params=LIMIT,
        name="finish",
        cost_estimate=lasts(0.9),
    )(last, keep, came)
    cache_keys, cache_values = pl.pallas_call(
        store_kernel,
        out_shape=(shape16(ctx_rows, width), shape16(ctx_rows, width)),
        compiler_params=LIMIT,
        name="store", cost_estimate=lasts(0.8),
    )(*stored)
    return (block_out, context_out, cache_keys, cache_values)


def solution(mesh):
    rows = P(("session", "seq"), "tensor")
    in_specs = (rows,) * 6 + (P("session"), P("session", None), P("session"), P("tensor", None))
    sizes = mesh.shape
    step = fast_device if sizes["seq"] == 4 and sizes["tensor"] == 4 else per_device
    return jax.shard_map(
        step, mesh=mesh, in_specs=in_specs, out_specs=(rows,) * 4, check_vma=False
    )
```

```python
import functools
import math

import jax
import jax.numpy as jnp
from jax import lax
from jax.experimental import pallas as pl
from jax.experimental.pallas import tpu as pltpu
from jax.sharding import PartitionSpec as P

HEAD_DIM = 128


NEGATIVE = -1e30


def lookup(table, index):
    hits = index[..., None] == jnp.arange(table.shape[0], dtype=jnp.int32)
    return jnp.sum(jnp.where(hits, table, 0), axis=-1)


def pool_blocks(rows, coarse):
    blocks = rows.reshape(-1, 4, rows.shape[-1])
    mean = jnp.mean(blocks.astype(jnp.float32), axis=1).astype(jnp.bfloat16)
    first = (jnp.arange(4) == 0)[None, :, None]
    pooled = jnp.where(first, mean[:, None, :], jnp.zeros_like(blocks))
    return jnp.where(coarse[:, None, None], pooled, blocks)


def group_plan(total_rows, shard_rows):
    shards = total_rows // shard_rows
    group = math.gcd(shards, max(1, 1024 // shard_rows))
    return (shards // group, group)


def attend(state, heads_q, keys, values, allowed, scale):
    best, total, accum = state
    count = keys.shape[0]
    heads = heads_q.shape[0]
    hdim = heads_q.shape[2]
    keys_h = keys.reshape(count, heads, hdim)
    values_h = values.reshape(count, heads, hdim)
    scores = jnp.einsum("hqd,khd->hqk", heads_q, keys_h, preferred_element_type=jnp.float32) * scale
    if allowed is not None:
        scores = jnp.where(allowed[None], scores, NEGATIVE)
    fresh = jnp.maximum(best, jnp.max(scores, axis=2))
    weights = jnp.exp(scores - fresh[..., None])
    if allowed is not None:
        weights = jnp.where(allowed[None], weights, 0.0)
    decay = jnp.exp(best - fresh)
    total = total * decay + jnp.sum(weights, axis=2)
    accum = accum * decay[..., None] + jnp.einsum(
        "hqk,khd->hqd", weights.astype(jnp.bfloat16), values_h, preferred_element_type=jnp.float32
    )
    return (fresh, total, accum)


def per_device(
    queries,
    new_keys,
    new_values,
    context_queries,
    context_keys,
    context_values,
    levels,
    frame_mask,
    owners,
    out_weight,
):
    width = queries.shape[1]
    new_rows = queries.shape[0]
    ctx_rows = context_keys.shape[0]
    blocks_dev = ctx_rows // 4
    devices = lax.axis_size("seq")
    place = lax.axis_index("seq")
    blocks_all = blocks_dev * devices
    frames_ctx = levels.shape[0]
    frames_new = frame_mask.shape[0]
    new_all = new_rows * devices
    hdim = HEAD_DIM
    heads = width // hdim
    scale = 1.0 / math.sqrt(hdim)
    pair = max(2, 2 * blocks_dev // devices)
    block_ids = jnp.arange(blocks_all, dtype=jnp.int32)
    block_frame = block_ids * frames_ctx // blocks_all
    coarse_all = lookup(levels, block_frame) == 1
    mine = owners == place
    rank = jnp.cumsum(mine.astype(jnp.int32)) - 1
    own_coarse = lax.dynamic_slice_in_dim(coarse_all, place * blocks_dev, blocks_dev)
    pooled_q = pool_blocks(context_queries, own_coarse)
    pooled_k = pool_blocks(context_keys, own_coarse)
    pooled_v = pool_blocks(context_values, own_coarse)
    slots = jnp.arange(blocks_dev, dtype=jnp.int32)[:, None] == rank[None, :]
    held_coarse = jnp.any(slots & mine[None, :] & coarse_all[None, :], axis=1)
    held_live = jnp.logical_or(
        jnp.logical_not(held_coarse)[:, None], (jnp.arange(4) == 0)[None, :]
    ).reshape(ctx_rows)
    my_owners = lax.dynamic_slice_in_dim(owners, place * blocks_dev, blocks_dev)
    hits = my_owners[:, None] == jnp.arange(devices, dtype=jnp.int32)[None, :]
    within = jnp.sum(jnp.where(hits, jnp.cumsum(hits.astype(jnp.int32), axis=0) - 1, 0), axis=1)
    send_slot = my_owners * pair + within

    def pack(blocks):
        buffer = jnp.zeros((devices * pair, 4, width), blocks.dtype).at[send_slot].set(blocks)
        return buffer.reshape(devices, pair * 4, width)

    counts = jnp.sum((owners.reshape(devices, blocks_dev) == place).astype(jnp.int32), axis=1)
    before = jnp.cumsum(counts) - counts
    order_in = jnp.arange(pair, dtype=jnp.int32)[None, :]
    target = jnp.where(order_in < counts[:, None], before[:, None] + order_in, blocks_dev).reshape(
        -1
    )

    def unpack(arrived):
        blocks = arrived.reshape(devices * pair, 4, width)
        return jnp.zeros((blocks_dev, 4, width), arrived.dtype).at[target].set(blocks, mode="drop")

    arrived = (
        lax.all_to_all(pack(pooled_q), "seq", split_axis=0, concat_axis=0, tiled=True),
        lax.all_to_all(pack(pooled_k), "seq", split_axis=0, concat_axis=0, tiled=True),
        lax.all_to_all(pack(pooled_v), "seq", split_axis=0, concat_axis=0, tiled=True),
    )
    held_q = unpack(arrived[0])
    held_k = unpack(arrived[1])
    held_v = unpack(arrived[2])
    all_q = jnp.concatenate([queries, held_q.reshape(ctx_rows, width)], axis=0)
    rows_q = all_q.shape[0]
    heads_q = all_q.reshape(rows_q, heads, hdim).transpose(1, 0, 2)
    q_global = place * new_rows + jnp.arange(new_rows, dtype=jnp.int32)
    q_frame = q_global * frames_new // new_all
    frame_hits = (q_frame[:, None] == jnp.arange(frames_new, dtype=jnp.int32)[None, :])[:, :, None]
    new_mask = jnp.sum(jnp.where(frame_hits, frame_mask[None], 0), axis=1)
    query_mask = jnp.concatenate(
        [new_mask, jnp.ones((ctx_rows, frames_ctx), jnp.int32)], axis=0
    ).astype(jnp.float32)

    def context_allowed(first_shard, count_rows):
        index = first_shard * ctx_rows + jnp.arange(count_rows, dtype=jnp.int32)
        frame = index // 4 * frames_ctx // blocks_all
        coarse = lookup(levels, frame) == 1
        live = jnp.logical_or(jnp.logical_not(coarse), index % 4 == 0)
        onehot = (frame[:, None] == jnp.arange(frames_ctx, dtype=jnp.int32)[None, :]).astype(
            jnp.float32
        )
        reach = jnp.dot(query_mask, onehot.T) > 0.5
        return jnp.logical_and(reach, live[None, :])

    def take_new(state, keys, values):
        return attend(state, heads_q, keys, values, None, scale)

    def take_context(state, keys, values, first_shard):
        allowed = context_allowed(first_shard, keys.shape[0])
        return attend(state, heads_q, keys, values, allowed, scale)

    start_state = (
        jnp.full((heads, rows_q), NEGATIVE, jnp.float32),
        jnp.zeros((heads, rows_q), jnp.float32),
        jnp.zeros((heads, rows_q, hdim), jnp.float32),
    )
    empty_cache = (
        jnp.zeros((blocks_dev, 4, width), jnp.bfloat16),
        jnp.zeros((blocks_dev, 4, width), jnp.bfloat16),
    )
    flat_k = pooled_k.reshape(ctx_rows, width)
    flat_v = pooled_v.reshape(ctx_rows, width)
    piece = (
        lax.all_gather(new_keys, "seq", axis=0, tiled=True),
        lax.all_gather(new_values, "seq", axis=0, tiled=True),
    )
    steps, group = group_plan(piece[0].shape[0], new_rows)
    size = group * new_rows
    stacked = (piece[0].reshape(steps, size, width), piece[1].reshape(steps, size, width))

    def one(carry, item):
        return (take_new(carry, item[0], item[1]), None)

    state = lax.scan(one, start_state, stacked)[0]
    piece = (
        lax.all_gather(flat_k, "seq", axis=0, tiled=True),
        lax.all_gather(flat_v, "seq", axis=0, tiled=True),
    )
    steps, group = group_plan(piece[0].shape[0], ctx_rows)
    size = group * ctx_rows
    firsts = jnp.arange(steps, dtype=jnp.int32) * group
    stacked = (piece[0].reshape(steps, size, width), piece[1].reshape(steps, size, width), firsts)

    def one(inner, item):
        keys, values, first = item
        attended = take_context(inner[0], keys, values, first)
        cache = inner[1]
        return ((attended, cache), None)

    state, cache = lax.scan(one, (state, empty_cache), stacked)[0]
    best, total, accum = state
    mixed = (accum / total[..., None]).transpose(1, 0, 2).reshape(rows_q, width)
    live_rows = jnp.concatenate([jnp.ones((new_rows,), dtype=bool), held_live], axis=0)
    mixed = jnp.where(live_rows[:, None], mixed, 0.0).astype(jnp.bfloat16)
    summed = lax.psum_scatter(
        lax.dot_general(
            out_weight, mixed, (((0,), (1,)), ((), ())), preferred_element_type=jnp.float32
        ).astype(jnp.bfloat16),
        "tensor",
        scatter_dimension=0,
        tiled=True,
    ).astype(jnp.float32)
    result = summed.T.astype(jnp.bfloat16)
    return (
        result[:new_rows],
        result[new_rows:],
        held_k.reshape(ctx_rows, width),
        held_v.reshape(ctx_rows, width),
    )


def place_index(shape, dim):
    return lax.broadcasted_iota(jnp.int32, shape, dim)


def coarse_of(frame, levels_ref, frames_ctx):
    coarse = frame < 0
    for f in range(frames_ctx):
        coarse = jnp.logical_or(coarse, jnp.logical_and(frame == f, levels_ref[f] == 1))
    return coarse


def pack_kernel(
    levels, q, k, v, cq, ck, cv, near_a, near_b, far_a, far_b, lv, sk, sv, sq, sems
):
    z = lax.axis_index("seq")
    devices = lax.axis_size("seq")
    new_rows, width = q.shape
    ctx_rows = cq.shape[0]
    half = width // 2
    most = near_a.shape[1]
    rows = new_rows + ctx_rows
    frames_ctx = levels.shape[0]
    low = jnp.where(z < devices // 2, 0, half)
    places = (
        (far_a, half - low, most),
        (near_a, low, most),
        (far_b, half - low + most, half - most),
        (near_b, low + most, half - most),
    )
    places = [(out, pl.ds(pl.multiple_of(at, 128), size)) for out, at, size in places]
    started = []

    def start(src, dst):
        copy = pltpu.make_async_copy(src, dst, sems.at[len(started)])
        copy.start()
        started.append(copy)
        return copy

    reads = [start(levels, lv), start(ck, sk), start(cv, sv), start(cq, sq)]
    for out, lanes in places:
        for part, fresh in enumerate((k, v, q)):
            start(fresh.at[:, lanes], out.at[part * rows : part * rows + new_rows])
    reads[0].wait()
    index = place_index((ctx_rows, 1), 0)
    first = index % 4 == 0
    frame = (z * ctx_rows + index) * frames_ctx // (devices * ctx_rows)
    coarse = coarse_of(frame, lv, frames_ctx)
    for part, src in enumerate((sk, sv, sq)):
        reads[part + 1].wait()
        wide = src[...].astype(jnp.float32)
        pair = wide + pltpu.roll(wide, ctx_rows - 1, 0)
        quad = pair + pltpu.roll(pair, ctx_rows - 2, 0)
        mean = jnp.where(first, quad * 0.25, 0.0)
        src[...] = jnp.where(coarse, mean, wide).astype(jnp.bfloat16)
        for out, lanes in places:
            out[part * rows + new_rows : (part + 1) * rows] = src[:, lanes]
    for copy in started[4:]:
        copy.wait()


def plan_kernel(owners, levels, masks, order, alive, biases):
    blocks = owners.shape[1]
    size = order.shape[0]
    per = size // blocks
    devices = lax.axis_size("seq")
    frames_ctx = levels.shape[0]
    row = owners[...].astype(jnp.float32)
    r = place_index((blocks, blocks), 0)
    c = place_index((blocks, blocks), 1)
    col = jnp.sum(jnp.where(r == c, row, 0.0), axis=1, keepdims=True)
    ahead = jnp.logical_and(col == row, r < c)
    rank = jnp.sum(ahead.astype(jnp.float32), axis=0, keepdims=True)
    spot = row * float(blocks // devices) + rank
    spread = (
        place_index((blocks, size), 1) // per == place_index((blocks, size), 0)
    ).astype(jnp.bfloat16)
    wide = jnp.dot(
        jnp.broadcast_to(spot, (16, blocks)).astype(jnp.bfloat16),
        spread,
        preferred_element_type=jnp.float32,
    )[0:1]
    lane = place_index((1, size), 1)
    target = wide.astype(jnp.int32) * per + lane % per
    move = (place_index((size, size), 0) == target).astype(jnp.bfloat16)
    order[...] = move
    index = place_index((size, alive.shape[1]), 0)
    coarse = coarse_of(index * frames_ctx // size, levels, frames_ctx)
    live = jnp.logical_or(jnp.logical_not(coarse), index % per == 0)
    alive[...] = jnp.dot(
        move, live.astype(jnp.bfloat16), preferred_element_type=jnp.float32
    )
    frame = lane * frames_ctx // size
    live = jnp.logical_or(
        jnp.logical_not(coarse_of(frame, levels, frames_ctx)), lane % per == 0
    )
    biases[...] = jnp.zeros_like(biases)
    biases[0:1] = jnp.where(live, 0.0, NEGATIVE)
    for g in range(masks.shape[0]):
        seen = frame < 0
        for f in range(frames_ctx):
            seen = jnp.logical_or(seen, jnp.logical_and(frame == f, masks[g, f] == 1))
        biases[g + 1 : g + 2] = jnp.where(jnp.logical_and(live, seen), 0.0, NEGATIVE)


def far_places(z):
    across = 3 - z
    beside = jnp.where(z == 1, 0, 3)
    return (z, beside, across, 3 - beside)


def middle(z):
    return jnp.logical_or(z == 1, z == 2)


def run_jobs(jobs, keys, values, fresh, factor):
    hdim = values.shape[2] // 2

    def score(head, q):
        lanes = slice(head * hdim, (head + 1) * hdim)
        return lax.dot_general(
            q, keys[:, lanes], (((1,), (1,)), ((), ())), preferred_element_type=jnp.float32
        )

    def finish(head, scores, bias):
        ahead = scores[:, :fresh]
        behind = scores[:, fresh:] + bias
        top = jnp.maximum(
            jnp.max(ahead, axis=1, keepdims=True), jnp.max(behind, axis=1, keepdims=True)
        )
        w_ahead = jnp.exp2((ahead - top) * factor).astype(jnp.bfloat16)
        w_behind = jnp.exp2((behind - top) * factor).astype(jnp.bfloat16)
        both = jnp.dot(
            w_ahead, values[head, :fresh], preferred_element_type=jnp.float32
        ) + jnp.dot(w_behind, values[head, fresh:], preferred_element_type=jnp.float32)
        return both[:, :hdim] / both[:, hdim:]

    held = None
    for job in [*jobs, None]:
        scores = None if job is None else score(job[0], job[1]())
        if held is not None:
            held[3](finish(held[0], held[4], held[2]))
        held = None if job is None else (*job, scores)


def gather_heads(places, sources, ctx_rows, keys, values, qn, qc):
    rows = sources[0].shape[0] // 3
    new_rows = rows - ctx_rows
    fresh = len(sources) * new_rows
    heads = values.shape[0]
    hdim = values.shape[2] // 2
    values[:, :, hdim:] = jnp.ones((heads, values.shape[1], hdim), jnp.bfloat16)
    for place, src in zip(places, sources):
        at = pl.ds(pl.multiple_of(place * new_rows, new_rows), new_rows)
        spot = pl.ds(pl.multiple_of(place * ctx_rows, ctx_rows), ctx_rows)
        to = pl.ds(pl.multiple_of(fresh + place * ctx_rows, ctx_rows), ctx_rows)
        keys[at] = src[0:new_rows]
        keys[to] = src[new_rows:rows]
        qn[at] = src[2 * rows : 2 * rows + new_rows]
        qc[spot] = src[2 * rows + new_rows : 3 * rows]
        for h in range(heads):
            lanes = slice(h * hdim, (h + 1) * hdim)
            values[h, at, :hdim] = src[rows : rows + new_rows, lanes]
            values[h, to, :hdim] = src[rows + new_rows : 2 * rows, lanes]


def attend_heads(factor, frames_new, order, alive, biases, keys, values, qn, qc):
    heads = values.shape[0]
    hdim = values.shape[2] // 2
    fresh = qn.shape[0]
    per = fresh // frames_new
    qc[...] = jnp.dot(order[...], qc[...], preferred_element_type=jnp.float32).astype(
        jnp.bfloat16
    )
    jobs = []
    for h in range(heads):
        lanes = slice(h * hdim, (h + 1) * hdim)
        for g in range(frames_new):
            at = slice(g * per, (g + 1) * per)

            def put_new(r, at=at, lanes=lanes):
                qn[at, lanes] = r.astype(jnp.bfloat16)

            jobs.append(
                (h, lambda at=at, lanes=lanes: qn[at, lanes], biases[g + 1 : g + 2], put_new)
            )

        def put_ctx(r, lanes=lanes):
            qc[:, lanes] = (r * alive[...]).astype(jnp.bfloat16)

        jobs.append((h, lambda lanes=lanes: qc[:, lanes], biases[0:1], put_ctx))
    run_jobs(jobs, keys, values, fresh, factor)


def first_kernel(
    factor, frames_new, a0, a1, a2, a3, order, alive, biases, qn, qc, keys, values
):
    z = lax.axis_index("seq")

    @pl.when(middle(z))
    def _():
        gather_heads(far_places(z), (a0, a1, a2, a3), qc.shape[0] // 4, keys, values, qn, qc)
        attend_heads(factor, frames_new, order, alive, biases, keys, values, qn, qc)


def second_kernel(
    factor, frames_new, b0, b3, b2, b1, order, alive, biases, fn, fc,
    o0, o1, o2, o3, keys, values, qn, qc,
):
    z = lax.axis_index("seq")
    ctx_rows = qc.shape[0] // 4
    new_rows = qn.shape[0] // 4
    most = fn.shape[1]

    @pl.when(middle(z))
    def _():
        places = far_places(z)
        gather_heads(places, (b0, b1, b2, b3), ctx_rows, keys, values, qn, qc)
        attend_heads(factor, frames_new, order, alive, biases, keys, values, qn, qc)
        for place, out in zip(places, (o0, o1, o2, o3)):
            at = pl.ds(pl.multiple_of(place * new_rows, new_rows), new_rows)
            part = pl.ds(pl.multiple_of(place * ctx_rows, ctx_rows), ctx_rows)
            out[:new_rows, :most] = fn[at]
            out[:new_rows, most:] = qn[at]
            out[new_rows:, :most] = fc[part]
            out[new_rows:, most:] = qc[part]


def cache_kernel(
    a0, a1, a2, a3, b0, b1, b2, b3, order, c0, c1, c2, c3, kk
):
    z = lax.axis_index("seq")
    ctx_rows, half = c0.shape[0] // 2, c0.shape[1]
    rows = a0.shape[0] // 3
    new_rows = rows - ctx_rows
    most = a0.shape[1]

    @pl.when(middle(z))
    def _():
        places = far_places(z)
        for place, a, b in zip(places, (a0, a1, a2, a3), (b0, b1, b2, b3)):
            to = pl.ds(pl.multiple_of(place * ctx_rows, ctx_rows), ctx_rows)
            for part in range(2):
                at = slice(part * rows + new_rows, (part + 1) * rows)
                kk[to, part * half : part * half + most] = a[at]
                kk[to, part * half + most : (part + 1) * half] = b[at]
        for place, out in zip(places, (c0, c1, c2, c3)):
            part = pl.ds(pl.multiple_of(place * ctx_rows, ctx_rows), ctx_rows)
            moved = jnp.dot(order[part], kk[...], preferred_element_type=jnp.float32)
            out[:ctx_rows] = moved[:, :half].astype(jnp.bfloat16)
            out[ctx_rows:] = moved[:, half:].astype(jnp.bfloat16)


def halves(z, at, *parts):
    own, beside, across, beyond = (part[at] for part in parts)
    inner = middle(z)
    low = z < 2
    near = jnp.where(inner, own, beside)
    far = jnp.where(inner, across, beyond)
    return (jnp.where(low, near, far), jnp.where(low, far, near))


def project_kernel(mine, here, o0, o1, o3, o2, weight, out):
    a, b = halves(lax.axis_index("seq"), slice(None), o0, o1, o2, o3)
    mixed = jnp.concatenate([a, b], axis=1)
    width = mixed.shape[1]
    me = lax.axis_index("tensor")
    core = me % 2 if mine else 1 - me % 2
    chip = me // 2 if here else 1 - me // 2
    lanes = pl.ds(pl.multiple_of((2 * chip + core) * width, width), width)
    total = jnp.dot(mixed, weight[:, lanes], preferred_element_type=jnp.float32)
    out[...] = total.astype(out.dtype)


def add_kernel(keep, came, out):
    out[...] = (keep[...] + came[...].astype(jnp.float32)).astype(jnp.bfloat16)


def finish_kernel(last, keep, came, c0, c3, c1, c2, out, out_ctx, keys, values):
    total = keep[...] + came[...].astype(jnp.float32) + last[...].astype(jnp.float32)
    total = total.astype(jnp.bfloat16)
    out[...] = total[: out.shape[0]]
    out_ctx[...] = total[out.shape[0] :]
    z = lax.axis_index("seq")
    ctx_rows, width = keys.shape
    half = width // 2
    for i, part in enumerate((keys, values)):
        at = slice(i * ctx_rows, (i + 1) * ctx_rows)
        a, b = halves(z, at, c0, c1, c2, c3)
        part[:, :half] = a
        part[:, half:] = b


SMALL = pl.BlockSpec(memory_space=pltpu.SMEM)
AWAY = pl.BlockSpec(memory_space=pltpu.HBM)
WHOLE = pl.BlockSpec(memory_space=pltpu.VMEM)
LIMIT = pltpu.CompilerParams(vmem_limit_bytes=32 * 1024 * 1024)


def lasts(us):
    return pl.CostEstimate(flops=int(us * 1.1e9), bytes_accessed=0, transcendentals=0)


def shape16(*dims):
    return jax.ShapeDtypeStruct(dims, jnp.bfloat16)


def permute(x, pairs):
    return lax.ppermute(x, "seq", pairs)


BESIDE = ((0, 1), (3, 2))
ACROSS = ((1, 2), (2, 1))
BEYOND = ((0, 2), (3, 1))
SIBLING = ((0, 1), (1, 0), (2, 3), (3, 2))
OPPOSITE = ((0, 2), (2, 0), (1, 3), (3, 1))


def back(pairs):
    return tuple((b, a) for a, b in pairs)


def home(own, beside, across, beyond):
    return (
        own,
        permute(beside, back(BESIDE)),
        permute(across, ACROSS),
        permute(beyond, back(BEYOND)),
    )


def fast_device(
    queries,
    new_keys,
    new_values,
    context_queries,
    context_keys,
    context_values,
    levels,
    frame_mask,
    owners,
    out_weight,
):
    new_rows, width = queries.shape
    ctx_rows = context_keys.shape[0]
    rows = new_rows + ctx_rows
    half = width // 2
    devices = lax.axis_size("seq")
    ctx_all = ctx_rows * devices
    hdim = HEAD_DIM
    frames_new = frame_mask.shape[0]
    factor = math.log2(math.e) / math.sqrt(hdim)
    most = max(hdim, half - hdim)
    near_a, near_b, far_a, far_b = pl.pallas_call(
        pack_kernel,
        out_shape=(
            shape16(3 * rows, most),
            shape16(3 * rows, half - most),
            shape16(3 * rows, most),
            shape16(3 * rows, half - most),
        ),
        in_specs=[AWAY] * 7,
        out_specs=[WHOLE] * 4,
        scratch_shapes=[pltpu.SMEM(levels.shape, jnp.int32)]
        + [pltpu.VMEM((ctx_rows, width), jnp.bfloat16)] * 3
        + [pltpu.SemaphoreType.DMA((16,))],
        name="pack",
    )(levels, queries, new_keys, new_values, context_queries, context_keys, context_values)
    beside_a = permute(near_a, BESIDE)
    across_a = permute(far_a, ACROSS)
    beyond_a = permute(far_a, BEYOND)
    beside_b = permute(near_b, BESIDE)
    across_b = permute(far_b, ACROSS)
    beyond_b = permute(far_b, BEYOND)
    order, alive, biases = pl.pallas_call(
        plan_kernel,
        out_shape=(
            shape16(ctx_all, ctx_all),
            jax.ShapeDtypeStruct((ctx_all, hdim), jnp.float32),
            jax.ShapeDtypeStruct((8, ctx_all), jnp.float32),
        ),
        in_specs=[WHOLE, SMALL, SMALL],
        compiler_params=LIMIT,
        name="plan", cost_estimate=lasts(1.6),
    )(owners.reshape(1, -1), levels, frame_mask)
    def scratch(lanes):
        return [
            pltpu.VMEM((rows * devices, lanes), jnp.bfloat16),
            pltpu.VMEM((lanes // hdim, rows * devices, 2 * hdim), jnp.bfloat16),
        ]

    fresh, held = pl.pallas_call(
        functools.partial(first_kernel, factor, frames_new),
        out_shape=[shape16(new_rows * devices, most), shape16(ctx_all, most)],
        scratch_shapes=scratch(most),
        compiler_params=LIMIT,
        name="attend_first",
        cost_estimate=lasts(4.8),
    )(near_a, beside_a, across_a, beyond_a, order, alive, biases)
    results = pl.pallas_call(
        functools.partial(second_kernel, factor, frames_new),
        out_shape=[shape16(rows, half)] * 4,
        scratch_shapes=scratch(half - most)
        + [
            pltpu.VMEM((new_rows * devices, half - most), jnp.bfloat16),
            pltpu.VMEM((ctx_all, half - most), jnp.bfloat16),
        ],
        compiler_params=LIMIT,
        name="attend_second",
        cost_estimate=lasts(2.4),
    )(near_b, beyond_b, across_b, beside_b, order, alive, biases, fresh, held)
    mixed = home(*results)
    near_a = lax.optimization_barrier((near_a, results[0]))[0]
    caches = pl.pallas_call(
        cache_kernel,
        out_shape=[shape16(2 * ctx_rows, half)] * 4,
        scratch_shapes=[pltpu.VMEM((ctx_all, width), jnp.bfloat16)],
        compiler_params=LIMIT,
        name="caches",
        cost_estimate=lasts(0.8),
    )(near_a, beside_a, across_a, beyond_a, near_b, beside_b, across_b, beyond_b, order)

    own, beside, across, beyond = mixed
    own, beside, beyond, across = lax.optimization_barrier(
        (own, beside, beyond, across, caches[0])
    )[:4]
    mixed = (own, beside, across, beyond)

    def project(mine, here, dtype):
        return pl.pallas_call(
            functools.partial(project_kernel, mine, here),
            out_shape=jax.ShapeDtypeStruct((rows, width), dtype),
            in_specs=[WHOLE] * 5,
            compiler_params=LIMIT,
            name=("keep" if mine else "give") + ("_here" if here else "_there"),
            cost_estimate=lasts(0.6),
        )(mixed[0], mixed[1], mixed[3], mixed[2], out_weight)

    give_there = project(False, False, jnp.bfloat16)
    came_there = lax.ppermute(give_there, "tensor", SIBLING)
    keep_there = project(True, False, jnp.float32)
    other = pl.pallas_call(
        add_kernel,
        out_shape=shape16(rows, width),
        compiler_params=LIMIT,
        name="add",
        cost_estimate=lasts(0.1),
    )(keep_there, came_there)
    last = lax.ppermute(other, "tensor", OPPOSITE)
    caches = lax.optimization_barrier((*caches, other))[:4]
    beyond = permute(caches[3], back(BEYOND))
    across = permute(caches[2], ACROSS)
    beside = permute(caches[1], back(BESIDE))
    stored = (caches[0], beyond, beside, across)
    mixed = lax.optimization_barrier((*mixed, keep_there))[:4]
    came = lax.ppermute(project(False, True, jnp.bfloat16), "tensor", SIBLING)
    keep = project(True, True, jnp.float32)
    block_out, context_out, cache_keys, cache_values = pl.pallas_call(
        finish_kernel,
        out_shape=(
            shape16(new_rows, width),
            shape16(ctx_rows, width),
            shape16(ctx_rows, width),
            shape16(ctx_rows, width),
        ),
        compiler_params=LIMIT,
        name="finish",
        cost_estimate=lasts(1.0),
    )(last, keep, came, *stored)
    return (block_out, context_out, cache_keys, cache_values)


def solution(mesh):
    rows = P(("session", "seq"), "tensor")
    in_specs = (rows,) * 6 + (P("session"), P("session", None), P("session"), P("tensor", None))
    sizes = mesh.shape
    step = fast_device if sizes["seq"] == 4 and sizes["tensor"] == 4 else per_device
    return jax.shard_map(
        step, mesh=mesh, in_specs=in_specs, out_specs=(rows,) * 4, check_vma=False
    )
```

```python
import functools
import math

import jax
import jax.numpy as jnp
from jax import lax
from jax.experimental import pallas as pl
from jax.experimental.pallas import tpu as pltpu
from jax.sharding import PartitionSpec as P

HEAD_DIM = 128


NEGATIVE = -1e30


def lookup(table, index):
    hits = index[..., None] == jnp.arange(table.shape[0], dtype=jnp.int32)
    return jnp.sum(jnp.where(hits, table, 0), axis=-1)


def pool_blocks(rows, coarse):
    blocks = rows.reshape(-1, 4, rows.shape[-1])
    mean = jnp.mean(blocks.astype(jnp.float32), axis=1).astype(jnp.bfloat16)
    first = (jnp.arange(4) == 0)[None, :, None]
    pooled = jnp.where(first, mean[:, None, :], jnp.zeros_like(blocks))
    return jnp.where(coarse[:, None, None], pooled, blocks)


def group_plan(total_rows, shard_rows):
    shards = total_rows // shard_rows
    group = math.gcd(shards, max(1, 1024 // shard_rows))
    return (shards // group, group)


def attend(state, heads_q, keys, values, allowed, scale):
    best, total, accum = state
    count = keys.shape[0]
    heads = heads_q.shape[0]
    hdim = heads_q.shape[2]
    keys_h = keys.reshape(count, heads, hdim)
    values_h = values.reshape(count, heads, hdim)
    scores = jnp.einsum("hqd,khd->hqk", heads_q, keys_h, preferred_element_type=jnp.float32) * scale
    if allowed is not None:
        scores = jnp.where(allowed[None], scores, NEGATIVE)
    fresh = jnp.maximum(best, jnp.max(scores, axis=2))
    weights = jnp.exp(scores - fresh[..., None])
    if allowed is not None:
        weights = jnp.where(allowed[None], weights, 0.0)
    decay = jnp.exp(best - fresh)
    total = total * decay + jnp.sum(weights, axis=2)
    accum = accum * decay[..., None] + jnp.einsum(
        "hqk,khd->hqd", weights.astype(jnp.bfloat16), values_h, preferred_element_type=jnp.float32
    )
    return (fresh, total, accum)


def per_device(
    queries,
    new_keys,
    new_values,
    context_queries,
    context_keys,
    context_values,
    levels,
    frame_mask,
    owners,
    out_weight,
):
    width = queries.shape[1]
    new_rows = queries.shape[0]
    ctx_rows = context_keys.shape[0]
    blocks_dev = ctx_rows // 4
    devices = lax.axis_size("seq")
    place = lax.axis_index("seq")
    blocks_all = blocks_dev * devices
    frames_ctx = levels.shape[0]
    frames_new = frame_mask.shape[0]
    new_all = new_rows * devices
    hdim = HEAD_DIM
    heads = width // hdim
    scale = 1.0 / math.sqrt(hdim)
    pair = max(2, 2 * blocks_dev // devices)
    block_ids = jnp.arange(blocks_all, dtype=jnp.int32)
    block_frame = block_ids * frames_ctx // blocks_all
    coarse_all = lookup(levels, block_frame) == 1
    mine = owners == place
    rank = jnp.cumsum(mine.astype(jnp.int32)) - 1
    own_coarse = lax.dynamic_slice_in_dim(coarse_all, place * blocks_dev, blocks_dev)
    pooled_q = pool_blocks(context_queries, own_coarse)
    pooled_k = pool_blocks(context_keys, own_coarse)
    pooled_v = pool_blocks(context_values, own_coarse)
    slots = jnp.arange(blocks_dev, dtype=jnp.int32)[:, None] == rank[None, :]
    held_coarse = jnp.any(slots & mine[None, :] & coarse_all[None, :], axis=1)
    held_live = jnp.logical_or(
        jnp.logical_not(held_coarse)[:, None], (jnp.arange(4) == 0)[None, :]
    ).reshape(ctx_rows)
    my_owners = lax.dynamic_slice_in_dim(owners, place * blocks_dev, blocks_dev)
    hits = my_owners[:, None] == jnp.arange(devices, dtype=jnp.int32)[None, :]
    within = jnp.sum(jnp.where(hits, jnp.cumsum(hits.astype(jnp.int32), axis=0) - 1, 0), axis=1)
    send_slot = my_owners * pair + within

    def pack(blocks):
        buffer = jnp.zeros((devices * pair, 4, width), blocks.dtype).at[send_slot].set(blocks)
        return buffer.reshape(devices, pair * 4, width)

    counts = jnp.sum((owners.reshape(devices, blocks_dev) == place).astype(jnp.int32), axis=1)
    before = jnp.cumsum(counts) - counts
    order_in = jnp.arange(pair, dtype=jnp.int32)[None, :]
    target = jnp.where(order_in < counts[:, None], before[:, None] + order_in, blocks_dev).reshape(
        -1
    )

    def unpack(arrived):
        blocks = arrived.reshape(devices * pair, 4, width)
        return jnp.zeros((blocks_dev, 4, width), arrived.dtype).at[target].set(blocks, mode="drop")

    arrived = (
        lax.all_to_all(pack(pooled_q), "seq", split_axis=0, concat_axis=0, tiled=True),
        lax.all_to_all(pack(pooled_k), "seq", split_axis=0, concat_axis=0, tiled=True),
        lax.all_to_all(pack(pooled_v), "seq", split_axis=0, concat_axis=0, tiled=True),
    )
    held_q = unpack(arrived[0])
    held_k = unpack(arrived[1])
    held_v = unpack(arrived[2])
    all_q = jnp.concatenate([queries, held_q.reshape(ctx_rows, width)], axis=0)
    rows_q = all_q.shape[0]
    heads_q = all_q.reshape(rows_q, heads, hdim).transpose(1, 0, 2)
    q_global = place * new_rows + jnp.arange(new_rows, dtype=jnp.int32)
    q_frame = q_global * frames_new // new_all
    frame_hits = (q_frame[:, None] == jnp.arange(frames_new, dtype=jnp.int32)[None, :])[:, :, None]
    new_mask = jnp.sum(jnp.where(frame_hits, frame_mask[None], 0), axis=1)
    query_mask = jnp.concatenate(
        [new_mask, jnp.ones((ctx_rows, frames_ctx), jnp.int32)], axis=0
    ).astype(jnp.float32)

    def context_allowed(first_shard, count_rows):
        index = first_shard * ctx_rows + jnp.arange(count_rows, dtype=jnp.int32)
        frame = index // 4 * frames_ctx // blocks_all
        coarse = lookup(levels, frame) == 1
        live = jnp.logical_or(jnp.logical_not(coarse), index % 4 == 0)
        onehot = (frame[:, None] == jnp.arange(frames_ctx, dtype=jnp.int32)[None, :]).astype(
            jnp.float32
        )
        reach = jnp.dot(query_mask, onehot.T) > 0.5
        return jnp.logical_and(reach, live[None, :])

    def take_new(state, keys, values):
        return attend(state, heads_q, keys, values, None, scale)

    def take_context(state, keys, values, first_shard):
        allowed = context_allowed(first_shard, keys.shape[0])
        return attend(state, heads_q, keys, values, allowed, scale)

    start_state = (
        jnp.full((heads, rows_q), NEGATIVE, jnp.float32),
        jnp.zeros((heads, rows_q), jnp.float32),
        jnp.zeros((heads, rows_q, hdim), jnp.float32),
    )
    empty_cache = (
        jnp.zeros((blocks_dev, 4, width), jnp.bfloat16),
        jnp.zeros((blocks_dev, 4, width), jnp.bfloat16),
    )
    flat_k = pooled_k.reshape(ctx_rows, width)
    flat_v = pooled_v.reshape(ctx_rows, width)
    piece = (
        lax.all_gather(new_keys, "seq", axis=0, tiled=True),
        lax.all_gather(new_values, "seq", axis=0, tiled=True),
    )
    steps, group = group_plan(piece[0].shape[0], new_rows)
    size = group * new_rows
    stacked = (piece[0].reshape(steps, size, width), piece[1].reshape(steps, size, width))

    def one(carry, item):
        return (take_new(carry, item[0], item[1]), None)

    state = lax.scan(one, start_state, stacked)[0]
    piece = (
        lax.all_gather(flat_k, "seq", axis=0, tiled=True),
        lax.all_gather(flat_v, "seq", axis=0, tiled=True),
    )
    steps, group = group_plan(piece[0].shape[0], ctx_rows)
    size = group * ctx_rows
    firsts = jnp.arange(steps, dtype=jnp.int32) * group
    stacked = (piece[0].reshape(steps, size, width), piece[1].reshape(steps, size, width), firsts)

    def one(inner, item):
        keys, values, first = item
        attended = take_context(inner[0], keys, values, first)
        cache = inner[1]
        return ((attended, cache), None)

    state, cache = lax.scan(one, (state, empty_cache), stacked)[0]
    best, total, accum = state
    mixed = (accum / total[..., None]).transpose(1, 0, 2).reshape(rows_q, width)
    live_rows = jnp.concatenate([jnp.ones((new_rows,), dtype=bool), held_live], axis=0)
    mixed = jnp.where(live_rows[:, None], mixed, 0.0).astype(jnp.bfloat16)
    summed = lax.psum_scatter(
        lax.dot_general(
            out_weight, mixed, (((0,), (1,)), ((), ())), preferred_element_type=jnp.float32
        ).astype(jnp.bfloat16),
        "tensor",
        scatter_dimension=0,
        tiled=True,
    ).astype(jnp.float32)
    result = summed.T.astype(jnp.bfloat16)
    return (
        result[:new_rows],
        result[new_rows:],
        held_k.reshape(ctx_rows, width),
        held_v.reshape(ctx_rows, width),
    )


def place_index(shape, dim):
    return lax.broadcasted_iota(jnp.int32, shape, dim)


def coarse_of(frame, levels_ref, frames_ctx):
    coarse = frame < 0
    for f in range(frames_ctx):
        coarse = jnp.logical_or(coarse, jnp.logical_and(frame == f, levels_ref[f] == 1))
    return coarse


def pack_kernel(
    levels, q, k, v, cq, ck, cv, near_a, near_b, far_a, far_b, lv, sk, sv, sq, sems
):
    z = lax.axis_index("seq")
    devices = lax.axis_size("seq")
    new_rows, width = q.shape
    ctx_rows = cq.shape[0]
    half = width // 2
    most = near_a.shape[1]
    rows = new_rows + ctx_rows
    frames_ctx = levels.shape[0]
    low = jnp.where(z < devices // 2, 0, half)
    places = (
        (far_a, half - low, most),
        (near_a, low, most),
        (far_b, half - low + most, half - most),
        (near_b, low + most, half - most),
    )
    places = [(out, pl.ds(pl.multiple_of(at, 128), size)) for out, at, size in places]
    started = []

    def start(src, dst):
        copy = pltpu.make_async_copy(src, dst, sems.at[len(started)])
        copy.start()
        started.append(copy)
        return copy

    reads = [start(levels, lv), start(ck, sk), start(cv, sv), start(cq, sq)]
    for out, lanes in places:
        for part, fresh in enumerate((k, v, q)):
            start(fresh.at[:, lanes], out.at[part * rows : part * rows + new_rows])
    reads[0].wait()
    index = place_index((ctx_rows, 1), 0)
    first = index % 4 == 0
    frame = (z * ctx_rows + index) * frames_ctx // (devices * ctx_rows)
    coarse = coarse_of(frame, lv, frames_ctx)
    for part, src in enumerate((sk, sv, sq)):
        reads[part + 1].wait()
        wide = src[...].astype(jnp.float32)
        pair = wide + pltpu.roll(wide, ctx_rows - 1, 0)
        quad = pair + pltpu.roll(pair, ctx_rows - 2, 0)
        mean = jnp.where(first, quad * 0.25, 0.0)
        src[...] = jnp.where(coarse, mean, wide).astype(jnp.bfloat16)
        for out, lanes in places:
            out[part * rows + new_rows : (part + 1) * rows] = src[:, lanes]
    for copy in started[4:]:
        copy.wait()


def plan_kernel(owners, levels, masks, order, alive, biases):
    blocks = owners.shape[1]
    size = order.shape[0]
    per = size // blocks
    devices = lax.axis_size("seq")
    frames_ctx = levels.shape[0]
    row = owners[...].astype(jnp.float32)
    r = place_index((blocks, blocks), 0)
    c = place_index((blocks, blocks), 1)
    col = jnp.sum(jnp.where(r == c, row, 0.0), axis=1, keepdims=True)
    ahead = jnp.logical_and(col == row, r < c)
    rank = jnp.sum(ahead.astype(jnp.float32), axis=0, keepdims=True)
    spot = row * float(blocks // devices) + rank
    spread = (
        place_index((blocks, size), 1) // per == place_index((blocks, size), 0)
    ).astype(jnp.bfloat16)
    wide = jnp.dot(
        jnp.broadcast_to(spot, (16, blocks)).astype(jnp.bfloat16),
        spread,
        preferred_element_type=jnp.float32,
    )[0:1]
    lane = place_index((1, size), 1)
    target = wide.astype(jnp.int32) * per + lane % per
    move = (place_index((size, size), 0) == target).astype(jnp.bfloat16)
    order[...] = move
    index = place_index((size, alive.shape[1]), 0)
    coarse = coarse_of(index * frames_ctx // size, levels, frames_ctx)
    live = jnp.logical_or(jnp.logical_not(coarse), index % per == 0)
    alive[...] = jnp.dot(
        move, live.astype(jnp.bfloat16), preferred_element_type=jnp.float32
    )
    frame = lane * frames_ctx // size
    live = jnp.logical_or(
        jnp.logical_not(coarse_of(frame, levels, frames_ctx)), lane % per == 0
    )
    biases[...] = jnp.zeros_like(biases)
    biases[0:1] = jnp.where(live, 0.0, NEGATIVE)
    for g in range(masks.shape[0]):
        seen = frame < 0
        for f in range(frames_ctx):
            seen = jnp.logical_or(seen, jnp.logical_and(frame == f, masks[g, f] == 1))
        biases[g + 1 : g + 2] = jnp.where(jnp.logical_and(live, seen), 0.0, NEGATIVE)


def far_places(z):
    across = 3 - z
    beside = jnp.where(z == 1, 0, 3)
    return (z, beside, across, 3 - beside)


def middle(z):
    return jnp.logical_or(z == 1, z == 2)


def run_jobs(jobs, keys, values, fresh, factor):
    hdim = values.shape[2] // 2

    def score(head, q):
        lanes = slice(head * hdim, (head + 1) * hdim)
        return lax.dot_general(
            q, keys[:, lanes], (((1,), (1,)), ((), ())), preferred_element_type=jnp.float32
        )

    def finish(head, scores, bias):
        ahead = scores[:, :fresh]
        behind = scores[:, fresh:] + bias
        top = jnp.maximum(
            jnp.max(ahead, axis=1, keepdims=True), jnp.max(behind, axis=1, keepdims=True)
        )
        w_ahead = jnp.exp2((ahead - top) * factor).astype(jnp.bfloat16)
        w_behind = jnp.exp2((behind - top) * factor).astype(jnp.bfloat16)
        both = jnp.dot(
            w_ahead, values[head, :fresh], preferred_element_type=jnp.float32
        ) + jnp.dot(w_behind, values[head, fresh:], preferred_element_type=jnp.float32)
        return both[:, :hdim] / both[:, hdim:]

    held = None
    for job in [*jobs, None]:
        scores = None if job is None else score(job[0], job[1]())
        if held is not None:
            held[3](finish(held[0], held[4], held[2]))
        held = None if job is None else (*job, scores)


def gather_heads(places, sources, ctx_rows, keys, values, qn, qc):
    rows = sources[0].shape[0] // 3
    new_rows = rows - ctx_rows
    fresh = len(sources) * new_rows
    heads = values.shape[0]
    hdim = values.shape[2] // 2
    values[:, :, hdim:] = jnp.ones((heads, values.shape[1], hdim), jnp.bfloat16)
    for place, src in zip(places, sources):
        at = pl.ds(pl.multiple_of(place * new_rows, new_rows), new_rows)
        spot = pl.ds(pl.multiple_of(place * ctx_rows, ctx_rows), ctx_rows)
        to = pl.ds(pl.multiple_of(fresh + place * ctx_rows, ctx_rows), ctx_rows)
        keys[at] = src[0:new_rows]
        keys[to] = src[new_rows:rows]
        qn[at] = src[2 * rows : 2 * rows + new_rows]
        qc[spot] = src[2 * rows + new_rows : 3 * rows]
        for h in range(heads):
            lanes = slice(h * hdim, (h + 1) * hdim)
            values[h, at, :hdim] = src[rows : rows + new_rows, lanes]
            values[h, to, :hdim] = src[rows + new_rows : 2 * rows, lanes]


def attend_heads(factor, frames_new, order, alive, biases, keys, values, qn, qc):
    heads = values.shape[0]
    hdim = values.shape[2] // 2
    fresh = qn.shape[0]
    per = fresh // frames_new
    qc[...] = jnp.dot(order[...], qc[...], preferred_element_type=jnp.float32).astype(
        jnp.bfloat16
    )
    jobs = []
    for h in range(heads):
        lanes = slice(h * hdim, (h + 1) * hdim)
        for g in range(frames_new):
            at = slice(g * per, (g + 1) * per)

            def put_new(r, at=at, lanes=lanes):
                qn[at, lanes] = r.astype(jnp.bfloat16)

            jobs.append(
                (h, lambda at=at, lanes=lanes: qn[at, lanes], biases[g + 1 : g + 2], put_new)
            )

        def put_ctx(r, lanes=lanes):
            qc[:, lanes] = (r * alive[...]).astype(jnp.bfloat16)

        jobs.append((h, lambda lanes=lanes: qc[:, lanes], biases[0:1], put_ctx))
    run_jobs(jobs, keys, values, fresh, factor)


def hand_out(place, out, lanes, qn, qc):
    new_rows = qn.shape[0] // 4
    ctx_rows = qc.shape[0] // 4
    at = pl.ds(pl.multiple_of(place * new_rows, new_rows), new_rows)
    part = pl.ds(pl.multiple_of(place * ctx_rows, ctx_rows), ctx_rows)
    out[:new_rows, lanes] = qn[at]
    out[new_rows:, lanes] = qc[part]


def first_kernel(
    factor, frames_new, a0, a1, a2, a3, order, alive, biases, qn, qc, e1, e3, keys, values
):
    z = lax.axis_index("seq")

    @pl.when(middle(z))
    def _():
        places = far_places(z)
        gather_heads(places, (a0, a1, a2, a3), qc.shape[0] // 4, keys, values, qn, qc)
        attend_heads(factor, frames_new, order, alive, biases, keys, values, qn, qc)
        hand_out(places[1], e1, slice(None), qn, qc)
        hand_out(places[3], e3, slice(None), qn, qc)


def second_kernel(
    factor, frames_new, b0, b3, b2, b1, order, alive, biases, fn, fc,
    o0, o2, n1, n3, keys, values, qn, qc,
):
    z = lax.axis_index("seq")
    most = fn.shape[1]

    @pl.when(middle(z))
    def _():
        places = far_places(z)
        gather_heads(places, (b0, b1, b2, b3), qc.shape[0] // 4, keys, values, qn, qc)
        attend_heads(factor, frames_new, order, alive, biases, keys, values, qn, qc)
        hand_out(places[1], n1, slice(None), qn, qc)
        hand_out(places[3], n3, slice(None), qn, qc)
        for place, out in ((places[0], o0), (places[2], o2)):
            hand_out(place, out, slice(0, most), fn, fc)
            hand_out(place, out, slice(most, None), qn, qc)


def cache_kernel(
    a0, a1, a2, a3, b0, b1, b2, b3, order, c0, c1, c2, c3, kk
):
    z = lax.axis_index("seq")
    ctx_rows, half = c0.shape[0] // 2, c0.shape[1]
    rows = a0.shape[0] // 3
    new_rows = rows - ctx_rows
    most = a0.shape[1]

    @pl.when(middle(z))
    def _():
        places = far_places(z)
        for place, a, b in zip(places, (a0, a1, a2, a3), (b0, b1, b2, b3)):
            to = pl.ds(pl.multiple_of(place * ctx_rows, ctx_rows), ctx_rows)
            for part in range(2):
                at = slice(part * rows + new_rows, (part + 1) * rows)
                kk[to, part * half : part * half + most] = a[at]
                kk[to, part * half + most : (part + 1) * half] = b[at]
        for place, out in zip(places, (c0, c1, c2, c3)):
            part = pl.ds(pl.multiple_of(place * ctx_rows, ctx_rows), ctx_rows)
            moved = jnp.dot(order[part], kk[...], preferred_element_type=jnp.float32)
            out[:ctx_rows] = moved[:, :half].astype(jnp.bfloat16)
            out[ctx_rows:] = moved[:, half:].astype(jnp.bfloat16)


def halves(z, at, *parts):
    own, beside, across, beyond = (part[at] for part in parts)
    inner = middle(z)
    low = z < 2
    near = jnp.where(inner, own, beside)
    far = jnp.where(inner, across, beyond)
    return (jnp.where(low, near, far), jnp.where(low, far, near))


def project_kernel(mine, here, e1, e3, o0, n1, n3, o2, weight, out):
    o1 = jnp.concatenate([e1[...], n1[...]], axis=1)
    o3 = jnp.concatenate([e3[...], n3[...]], axis=1)
    a, b = halves(lax.axis_index("seq"), slice(None), o0, o1, o2, o3)
    mixed = jnp.concatenate([a, b], axis=1)
    width = mixed.shape[1]
    me = lax.axis_index("tensor")
    core = me % 2 if mine else 1 - me % 2
    chip = me // 2 if here else 1 - me // 2
    lanes = pl.ds(pl.multiple_of((2 * chip + core) * width, width), width)
    total = jnp.dot(mixed, weight[:, lanes], preferred_element_type=jnp.float32)
    out[...] = total.astype(out.dtype)


def add_kernel(keep, came, out):
    out[...] = (keep[...] + came[...].astype(jnp.float32)).astype(jnp.bfloat16)


def finish_kernel(last, keep, came, c0, c3, c1, c2, out, out_ctx, keys, values):
    total = keep[...] + came[...].astype(jnp.float32) + last[...].astype(jnp.float32)
    total = total.astype(jnp.bfloat16)
    out[...] = total[: out.shape[0]]
    out_ctx[...] = total[out.shape[0] :]
    z = lax.axis_index("seq")
    ctx_rows, width = keys.shape
    half = width // 2
    for i, part in enumerate((keys, values)):
        at = slice(i * ctx_rows, (i + 1) * ctx_rows)
        a, b = halves(z, at, c0, c1, c2, c3)
        part[:, :half] = a
        part[:, half:] = b


SMALL = pl.BlockSpec(memory_space=pltpu.SMEM)
AWAY = pl.BlockSpec(memory_space=pltpu.HBM)
WHOLE = pl.BlockSpec(memory_space=pltpu.VMEM)
LIMIT = pltpu.CompilerParams(vmem_limit_bytes=32 * 1024 * 1024)


def lasts(us):
    return pl.CostEstimate(flops=int(us * 1.1e9), bytes_accessed=0, transcendentals=0)


def shape16(*dims):
    return jax.ShapeDtypeStruct(dims, jnp.bfloat16)


def permute(x, pairs):
    return lax.ppermute(x, "seq", pairs)


BESIDE = ((0, 1), (3, 2))
ACROSS = ((1, 2), (2, 1))
BEYOND = ((0, 2), (3, 1))
SIBLING = ((0, 1), (1, 0), (2, 3), (3, 2))
OPPOSITE = ((0, 2), (2, 0), (1, 3), (3, 1))


def back(pairs):
    return tuple((b, a) for a, b in pairs)


def fast_device(
    queries,
    new_keys,
    new_values,
    context_queries,
    context_keys,
    context_values,
    levels,
    frame_mask,
    owners,
    out_weight,
):
    new_rows, width = queries.shape
    ctx_rows = context_keys.shape[0]
    rows = new_rows + ctx_rows
    half = width // 2
    devices = lax.axis_size("seq")
    ctx_all = ctx_rows * devices
    hdim = HEAD_DIM
    frames_new = frame_mask.shape[0]
    factor = math.log2(math.e) / math.sqrt(hdim)
    most = max(hdim, half - hdim)
    near_a, near_b, far_a, far_b = pl.pallas_call(
        pack_kernel,
        out_shape=(
            shape16(3 * rows, most),
            shape16(3 * rows, half - most),
            shape16(3 * rows, most),
            shape16(3 * rows, half - most),
        ),
        in_specs=[AWAY] * 7,
        out_specs=[WHOLE] * 4,
        scratch_shapes=[pltpu.SMEM(levels.shape, jnp.int32)]
        + [pltpu.VMEM((ctx_rows, width), jnp.bfloat16)] * 3
        + [pltpu.SemaphoreType.DMA((16,))],
        name="pack",
    )(levels, queries, new_keys, new_values, context_queries, context_keys, context_values)
    beside_a = permute(near_a, BESIDE)
    across_a = permute(far_a, ACROSS)
    beyond_a = permute(far_a, BEYOND)
    beside_b = permute(near_b, BESIDE)
    across_b = permute(far_b, ACROSS)
    beyond_b = permute(far_b, BEYOND)
    order, alive, biases = pl.pallas_call(
        plan_kernel,
        out_shape=(
            shape16(ctx_all, ctx_all),
            jax.ShapeDtypeStruct((ctx_all, hdim), jnp.float32),
            jax.ShapeDtypeStruct((8, ctx_all), jnp.float32),
        ),
        in_specs=[WHOLE, SMALL, SMALL],
        compiler_params=LIMIT,
        name="plan", cost_estimate=lasts(1.6),
    )(owners.reshape(1, -1), levels, frame_mask)
    def scratch(lanes):
        return [
            pltpu.VMEM((rows * devices, lanes), jnp.bfloat16),
            pltpu.VMEM((lanes // hdim, rows * devices, 2 * hdim), jnp.bfloat16),
        ]

    fresh, held, early_beside, early_beyond = pl.pallas_call(
        functools.partial(first_kernel, factor, frames_new),
        out_shape=[
            shape16(new_rows * devices, most),
            shape16(ctx_all, most),
            shape16(rows, most),
            shape16(rows, most),
        ],
        scratch_shapes=scratch(most),
        compiler_params=LIMIT,
        name="attend_first",
        cost_estimate=lasts(4.8),
    )(near_a, beside_a, across_a, beyond_a, order, alive, biases)
    results = pl.pallas_call(
        functools.partial(second_kernel, factor, frames_new),
        out_shape=[
            shape16(rows, half),
            shape16(rows, half),
            shape16(rows, half - most),
            shape16(rows, half - most),
        ],
        scratch_shapes=scratch(half - most)
        + [
            pltpu.VMEM((new_rows * devices, half - most), jnp.bfloat16),
            pltpu.VMEM((ctx_all, half - most), jnp.bfloat16),
        ],
        compiler_params=LIMIT,
        name="attend_second",
        cost_estimate=lasts(2.4),
    )(near_b, beyond_b, across_b, beside_b, order, alive, biases, fresh, held)
    own, across, late_beside, late_beyond = results
    early_beside = permute(early_beside, back(BESIDE))
    early_beyond = permute(early_beyond, back(BEYOND))
    across = lax.optimization_barrier((across, early_beside, early_beyond))[0]
    mixed = (
        early_beside,
        early_beyond,
        own,
        permute(late_beside, back(BESIDE)),
        permute(late_beyond, back(BEYOND)),
        permute(across, ACROSS),
    )
    near_a = lax.optimization_barrier((near_a, results[0]))[0]
    caches = pl.pallas_call(
        cache_kernel,
        out_shape=[shape16(2 * ctx_rows, half)] * 4,
        scratch_shapes=[pltpu.VMEM((ctx_all, width), jnp.bfloat16)],
        compiler_params=LIMIT,
        name="caches",
        cost_estimate=lasts(3),
    )(near_a, beside_a, across_a, beyond_a, near_b, beside_b, across_b, beyond_b, order)

    mixed = lax.optimization_barrier((*mixed, caches[0]))[:6]

    def project(mine, here, dtype):
        return pl.pallas_call(
            functools.partial(project_kernel, mine, here),
            out_shape=jax.ShapeDtypeStruct((rows, width), dtype),
            in_specs=[WHOLE] * 7,
            compiler_params=LIMIT,
            name=("keep" if mine else "give") + ("_here" if here else "_there"),
            cost_estimate=lasts(0.6),
        )(*mixed, out_weight)

    give_there = project(False, False, jnp.bfloat16)
    came_there = lax.ppermute(give_there, "tensor", SIBLING)
    keep_there = project(True, False, jnp.float32)
    other = pl.pallas_call(
        add_kernel,
        out_shape=shape16(rows, width),
        compiler_params=LIMIT,
        name="add",
        cost_estimate=lasts(0.1),
    )(keep_there, came_there)
    last = lax.ppermute(other, "tensor", OPPOSITE)
    caches = lax.optimization_barrier((*caches, other))[:4]
    beyond = permute(caches[3], back(BEYOND))
    across = permute(caches[2], ACROSS)
    beside = permute(caches[1], back(BESIDE))
    stored = (caches[0], beyond, beside, across)
    mixed = lax.optimization_barrier((*mixed, keep_there))[:6]
    came = lax.ppermute(project(False, True, jnp.bfloat16), "tensor", SIBLING)
    keep = project(True, True, jnp.float32)
    block_out, context_out, cache_keys, cache_values = pl.pallas_call(
        finish_kernel,
        out_shape=(
            shape16(new_rows, width),
            shape16(ctx_rows, width),
            shape16(ctx_rows, width),
            shape16(ctx_rows, width),
        ),
        compiler_params=LIMIT,
        name="finish",
        cost_estimate=lasts(1.0),
    )(last, keep, came, *stored)
    return (block_out, context_out, cache_keys, cache_values)


def solution(mesh):
    rows = P(("session", "seq"), "tensor")
    in_specs = (rows,) * 6 + (P("session"), P("session", None), P("session"), P("tensor", None))
    sizes = mesh.shape
    step = fast_device if sizes["seq"] == 4 and sizes["tensor"] == 4 else per_device
    return jax.shard_map(
        step, mesh=mesh, in_specs=in_specs, out_specs=(rows,) * 4, check_vma=False
    )
```

```python
import functools
import math

import jax
import jax.numpy as jnp
from jax import lax
from jax.experimental import pallas as pl
from jax.experimental.pallas import tpu as pltpu
from jax.sharding import PartitionSpec as P

HEAD_DIM = 128


NEGATIVE = -1e30


def lookup(table, index):
    hits = index[..., None] == jnp.arange(table.shape[0], dtype=jnp.int32)
    return jnp.sum(jnp.where(hits, table, 0), axis=-1)


def pool_blocks(rows, coarse):
    blocks = rows.reshape(-1, 4, rows.shape[-1])
    mean = jnp.mean(blocks.astype(jnp.float32), axis=1).astype(jnp.bfloat16)
    first = (jnp.arange(4) == 0)[None, :, None]
    pooled = jnp.where(first, mean[:, None, :], jnp.zeros_like(blocks))
    return jnp.where(coarse[:, None, None], pooled, blocks)


def group_plan(total_rows, shard_rows):
    shards = total_rows // shard_rows
    group = math.gcd(shards, max(1, 1024 // shard_rows))
    return (shards // group, group)


def attend(state, heads_q, keys, values, allowed, scale):
    best, total, accum = state
    count = keys.shape[0]
    heads = heads_q.shape[0]
    hdim = heads_q.shape[2]
    keys_h = keys.reshape(count, heads, hdim)
    values_h = values.reshape(count, heads, hdim)
    scores = jnp.einsum("hqd,khd->hqk", heads_q, keys_h, preferred_element_type=jnp.float32) * scale
    if allowed is not None:
        scores = jnp.where(allowed[None], scores, NEGATIVE)
    fresh = jnp.maximum(best, jnp.max(scores, axis=2))
    weights = jnp.exp(scores - fresh[..., None])
    if allowed is not None:
        weights = jnp.where(allowed[None], weights, 0.0)
    decay = jnp.exp(best - fresh)
    total = total * decay + jnp.sum(weights, axis=2)
    accum = accum * decay[..., None] + jnp.einsum(
        "hqk,khd->hqd", weights.astype(jnp.bfloat16), values_h, preferred_element_type=jnp.float32
    )
    return (fresh, total, accum)


def per_device(
    queries,
    new_keys,
    new_values,
    context_queries,
    context_keys,
    context_values,
    levels,
    frame_mask,
    owners,
    out_weight,
):
    width = queries.shape[1]
    new_rows = queries.shape[0]
    ctx_rows = context_keys.shape[0]
    blocks_dev = ctx_rows // 4
    devices = lax.axis_size("seq")
    place = lax.axis_index("seq")
    blocks_all = blocks_dev * devices
    frames_ctx = levels.shape[0]
    frames_new = frame_mask.shape[0]
    new_all = new_rows * devices
    hdim = HEAD_DIM
    heads = width // hdim
    scale = 1.0 / math.sqrt(hdim)
    pair = max(2, 2 * blocks_dev // devices)
    block_ids = jnp.arange(blocks_all, dtype=jnp.int32)
    block_frame = block_ids * frames_ctx // blocks_all
    coarse_all = lookup(levels, block_frame) == 1
    mine = owners == place
    rank = jnp.cumsum(mine.astype(jnp.int32)) - 1
    own_coarse = lax.dynamic_slice_in_dim(coarse_all, place * blocks_dev, blocks_dev)
    pooled_q = pool_blocks(context_queries, own_coarse)
    pooled_k = pool_blocks(context_keys, own_coarse)
    pooled_v = pool_blocks(context_values, own_coarse)
    slots = jnp.arange(blocks_dev, dtype=jnp.int32)[:, None] == rank[None, :]
    held_coarse = jnp.any(slots & mine[None, :] & coarse_all[None, :], axis=1)
    held_live = jnp.logical_or(
        jnp.logical_not(held_coarse)[:, None], (jnp.arange(4) == 0)[None, :]
    ).reshape(ctx_rows)
    my_owners = lax.dynamic_slice_in_dim(owners, place * blocks_dev, blocks_dev)
    hits = my_owners[:, None] == jnp.arange(devices, dtype=jnp.int32)[None, :]
    within = jnp.sum(jnp.where(hits, jnp.cumsum(hits.astype(jnp.int32), axis=0) - 1, 0), axis=1)
    send_slot = my_owners * pair + within

    def pack(blocks):
        buffer = jnp.zeros((devices * pair, 4, width), blocks.dtype).at[send_slot].set(blocks)
        return buffer.reshape(devices, pair * 4, width)

    counts = jnp.sum((owners.reshape(devices, blocks_dev) == place).astype(jnp.int32), axis=1)
    before = jnp.cumsum(counts) - counts
    order_in = jnp.arange(pair, dtype=jnp.int32)[None, :]
    target = jnp.where(order_in < counts[:, None], before[:, None] + order_in, blocks_dev).reshape(
        -1
    )

    def unpack(arrived):
        blocks = arrived.reshape(devices * pair, 4, width)
        return jnp.zeros((blocks_dev, 4, width), arrived.dtype).at[target].set(blocks, mode="drop")

    arrived = (
        lax.all_to_all(pack(pooled_q), "seq", split_axis=0, concat_axis=0, tiled=True),
        lax.all_to_all(pack(pooled_k), "seq", split_axis=0, concat_axis=0, tiled=True),
        lax.all_to_all(pack(pooled_v), "seq", split_axis=0, concat_axis=0, tiled=True),
    )
    held_q = unpack(arrived[0])
    held_k = unpack(arrived[1])
    held_v = unpack(arrived[2])
    all_q = jnp.concatenate([queries, held_q.reshape(ctx_rows, width)], axis=0)
    rows_q = all_q.shape[0]
    heads_q = all_q.reshape(rows_q, heads, hdim).transpose(1, 0, 2)
    q_global = place * new_rows + jnp.arange(new_rows, dtype=jnp.int32)
    q_frame = q_global * frames_new // new_all
    frame_hits = (q_frame[:, None] == jnp.arange(frames_new, dtype=jnp.int32)[None, :])[:, :, None]
    new_mask = jnp.sum(jnp.where(frame_hits, frame_mask[None], 0), axis=1)
    query_mask = jnp.concatenate(
        [new_mask, jnp.ones((ctx_rows, frames_ctx), jnp.int32)], axis=0
    ).astype(jnp.float32)

    def context_allowed(first_shard, count_rows):
        index = first_shard * ctx_rows + jnp.arange(count_rows, dtype=jnp.int32)
        frame = index // 4 * frames_ctx // blocks_all
        coarse = lookup(levels, frame) == 1
        live = jnp.logical_or(jnp.logical_not(coarse), index % 4 == 0)
        onehot = (frame[:, None] == jnp.arange(frames_ctx, dtype=jnp.int32)[None, :]).astype(
            jnp.float32
        )
        reach = jnp.dot(query_mask, onehot.T) > 0.5
        return jnp.logical_and(reach, live[None, :])

    def take_new(state, keys, values):
        return attend(state, heads_q, keys, values, None, scale)

    def take_context(state, keys, values, first_shard):
        allowed = context_allowed(first_shard, keys.shape[0])
        return attend(state, heads_q, keys, values, allowed, scale)

    start_state = (
        jnp.full((heads, rows_q), NEGATIVE, jnp.float32),
        jnp.zeros((heads, rows_q), jnp.float32),
        jnp.zeros((heads, rows_q, hdim), jnp.float32),
    )
    empty_cache = (
        jnp.zeros((blocks_dev, 4, width), jnp.bfloat16),
        jnp.zeros((blocks_dev, 4, width), jnp.bfloat16),
    )
    flat_k = pooled_k.reshape(ctx_rows, width)
    flat_v = pooled_v.reshape(ctx_rows, width)
    piece = (
        lax.all_gather(new_keys, "seq", axis=0, tiled=True),
        lax.all_gather(new_values, "seq", axis=0, tiled=True),
    )
    steps, group = group_plan(piece[0].shape[0], new_rows)
    size = group * new_rows
    stacked = (piece[0].reshape(steps, size, width), piece[1].reshape(steps, size, width))

    def one(carry, item):
        return (take_new(carry, item[0], item[1]), None)

    state = lax.scan(one, start_state, stacked)[0]
    piece = (
        lax.all_gather(flat_k, "seq", axis=0, tiled=True),
        lax.all_gather(flat_v, "seq", axis=0, tiled=True),
    )
    steps, group = group_plan(piece[0].shape[0], ctx_rows)
    size = group * ctx_rows
    firsts = jnp.arange(steps, dtype=jnp.int32) * group
    stacked = (piece[0].reshape(steps, size, width), piece[1].reshape(steps, size, width), firsts)

    def one(inner, item):
        keys, values, first = item
        attended = take_context(inner[0], keys, values, first)
        cache = inner[1]
        return ((attended, cache), None)

    state, cache = lax.scan(one, (state, empty_cache), stacked)[0]
    best, total, accum = state
    mixed = (accum / total[..., None]).transpose(1, 0, 2).reshape(rows_q, width)
    live_rows = jnp.concatenate([jnp.ones((new_rows,), dtype=bool), held_live], axis=0)
    mixed = jnp.where(live_rows[:, None], mixed, 0.0).astype(jnp.bfloat16)
    summed = lax.psum_scatter(
        lax.dot_general(
            out_weight, mixed, (((0,), (1,)), ((), ())), preferred_element_type=jnp.float32
        ).astype(jnp.bfloat16),
        "tensor",
        scatter_dimension=0,
        tiled=True,
    ).astype(jnp.float32)
    result = summed.T.astype(jnp.bfloat16)
    return (
        result[:new_rows],
        result[new_rows:],
        held_k.reshape(ctx_rows, width),
        held_v.reshape(ctx_rows, width),
    )


def place_index(shape, dim):
    return lax.broadcasted_iota(jnp.int32, shape, dim)


def coarse_of(frame, levels_ref, frames_ctx):
    coarse = frame < 0
    for f in range(frames_ctx):
        coarse = jnp.logical_or(coarse, jnp.logical_and(frame == f, levels_ref[f] == 1))
    return coarse


def pack_kernel(
    levels, q, k, v, cq, ck, cv, near_a, near_b, far_a, far_b, lv, sk, sv, sq, sems
):
    z = lax.axis_index("seq")
    devices = lax.axis_size("seq")
    new_rows, width = q.shape
    ctx_rows = cq.shape[0]
    half = width // 2
    most = near_a.shape[1]
    rows = new_rows + ctx_rows
    frames_ctx = levels.shape[0]
    low = jnp.where(z < devices // 2, 0, half)
    places = (
        (far_a, half - low, most),
        (near_a, low, most),
        (far_b, half - low + most, half - most),
        (near_b, low + most, half - most),
    )
    places = [(out, pl.ds(pl.multiple_of(at, 128), size)) for out, at, size in places]
    started = []

    def start(src, dst):
        copy = pltpu.make_async_copy(src, dst, sems.at[len(started)])
        copy.start()
        started.append(copy)
        return copy

    reads = [start(levels, lv), start(ck, sk), start(cv, sv), start(cq, sq)]
    for out, lanes in places:
        for part, fresh in enumerate((k, v, q)):
            start(fresh.at[:, lanes], out.at[part * rows : part * rows + new_rows])
    reads[0].wait()
    index = place_index((ctx_rows, 1), 0)
    first = index % 4 == 0
    frame = (z * ctx_rows + index) * frames_ctx // (devices * ctx_rows)
    coarse = coarse_of(frame, lv, frames_ctx)
    for part, src in enumerate((sk, sv, sq)):
        reads[part + 1].wait()
        wide = src[...].astype(jnp.float32)
        pair = wide + pltpu.roll(wide, ctx_rows - 1, 0)
        quad = pair + pltpu.roll(pair, ctx_rows - 2, 0)
        mean = jnp.where(first, quad * 0.25, 0.0)
        src[...] = jnp.where(coarse, mean, wide).astype(jnp.bfloat16)
        for out, lanes in places:
            out[part * rows + new_rows : (part + 1) * rows] = src[:, lanes]
    for copy in started[4:]:
        copy.wait()


def plan_kernel(owners, levels, masks, order, alive, biases):
    blocks = owners.shape[1]
    size = order.shape[0]
    per = size // blocks
    devices = lax.axis_size("seq")
    frames_ctx = levels.shape[0]
    row = owners[...].astype(jnp.float32)
    r = place_index((blocks, blocks), 0)
    c = place_index((blocks, blocks), 1)
    col = jnp.sum(jnp.where(r == c, row, 0.0), axis=1, keepdims=True)
    ahead = jnp.logical_and(col == row, r < c)
    rank = jnp.sum(ahead.astype(jnp.float32), axis=0, keepdims=True)
    spot = row * float(blocks // devices) + rank
    spread = (
        place_index((blocks, size), 1) // per == place_index((blocks, size), 0)
    ).astype(jnp.bfloat16)
    wide = jnp.dot(
        jnp.broadcast_to(spot, (16, blocks)).astype(jnp.bfloat16),
        spread,
        preferred_element_type=jnp.float32,
    )[0:1]
    lane = place_index((1, size), 1)
    target = wide.astype(jnp.int32) * per + lane % per
    move = (place_index((size, size), 0) == target).astype(jnp.bfloat16)
    order[...] = move
    index = place_index((size, alive.shape[1]), 0)
    coarse = coarse_of(index * frames_ctx // size, levels, frames_ctx)
    live = jnp.logical_or(jnp.logical_not(coarse), index % per == 0)
    alive[...] = jnp.dot(
        move, live.astype(jnp.bfloat16), preferred_element_type=jnp.float32
    )
    frame = lane * frames_ctx // size
    live = jnp.logical_or(
        jnp.logical_not(coarse_of(frame, levels, frames_ctx)), lane % per == 0
    )
    biases[...] = jnp.zeros_like(biases)
    biases[0:1] = jnp.where(live, 0.0, NEGATIVE)
    for g in range(masks.shape[0]):
        seen = frame < 0
        for f in range(frames_ctx):
            seen = jnp.logical_or(seen, jnp.logical_and(frame == f, masks[g, f] == 1))
        biases[g + 1 : g + 2] = jnp.where(jnp.logical_and(live, seen), 0.0, NEGATIVE)


def far_places(z):
    across = 3 - z
    beside = jnp.where(z == 1, 0, 3)
    return (z, beside, across, 3 - beside)


def middle(z):
    return jnp.logical_or(z == 1, z == 2)


def run_jobs(jobs, keys, values, fresh, factor):
    hdim = values.shape[2] // 2

    def score(head, q):
        lanes = slice(head * hdim, (head + 1) * hdim)
        return lax.dot_general(
            q, keys[:, lanes], (((1,), (1,)), ((), ())), preferred_element_type=jnp.float32
        )

    def finish(head, scores, bias):
        ahead = scores[:, :fresh]
        behind = scores[:, fresh:] + bias
        top = jnp.maximum(
            jnp.max(ahead, axis=1, keepdims=True), jnp.max(behind, axis=1, keepdims=True)
        )
        w_ahead = jnp.exp2((ahead - top) * factor).astype(jnp.bfloat16)
        w_behind = jnp.exp2((behind - top) * factor).astype(jnp.bfloat16)
        both = jnp.dot(
            w_ahead, values[head, :fresh], preferred_element_type=jnp.float32
        ) + jnp.dot(w_behind, values[head, fresh:], preferred_element_type=jnp.float32)
        return both[:, :hdim] / both[:, hdim:]

    held = None
    for job in [*jobs, None]:
        scores = None if job is None else score(job[0], job[1]())
        if held is not None:
            held[3](finish(held[0], held[4], held[2]))
        held = None if job is None else (*job, scores)


def gather_heads(places, sources, ctx_rows, keys, values, qn, qc):
    rows = sources[0].shape[0] // 3
    new_rows = rows - ctx_rows
    fresh = len(sources) * new_rows
    heads = values.shape[0]
    hdim = values.shape[2] // 2
    values[:, :, hdim:] = jnp.ones((heads, values.shape[1], hdim), jnp.bfloat16)
    for place, src in zip(places, sources):
        at = pl.ds(pl.multiple_of(place * new_rows, new_rows), new_rows)
        spot = pl.ds(pl.multiple_of(place * ctx_rows, ctx_rows), ctx_rows)
        to = pl.ds(pl.multiple_of(fresh + place * ctx_rows, ctx_rows), ctx_rows)
        keys[at] = src[0:new_rows]
        keys[to] = src[new_rows:rows]
        qn[at] = src[2 * rows : 2 * rows + new_rows]
        qc[spot] = src[2 * rows + new_rows : 3 * rows]
        for h in range(heads):
            lanes = slice(h * hdim, (h + 1) * hdim)
            values[h, at, :hdim] = src[rows : rows + new_rows, lanes]
            values[h, to, :hdim] = src[rows + new_rows : 2 * rows, lanes]


def attend_heads(factor, frames_new, order, alive, biases, keys, values, qn, qc):
    heads = values.shape[0]
    hdim = values.shape[2] // 2
    fresh = qn.shape[0]
    per = fresh // frames_new
    qc[...] = jnp.dot(order[...], qc[...], preferred_element_type=jnp.float32).astype(
        jnp.bfloat16
    )
    jobs = []
    for h in range(heads):
        lanes = slice(h * hdim, (h + 1) * hdim)
        for g in range(frames_new):
            at = slice(g * per, (g + 1) * per)

            def put_new(r, at=at, lanes=lanes):
                qn[at, lanes] = r.astype(jnp.bfloat16)

            jobs.append(
                (h, lambda at=at, lanes=lanes: qn[at, lanes], biases[g + 1 : g + 2], put_new)
            )

        def put_ctx(r, lanes=lanes):
            qc[:, lanes] = (r * alive[...]).astype(jnp.bfloat16)

        jobs.append((h, lambda lanes=lanes: qc[:, lanes], biases[0:1], put_ctx))
    run_jobs(jobs, keys, values, fresh, factor)


def hand_out(place, out, lanes, qn, qc):
    new_rows = qn.shape[0] // 4
    ctx_rows = qc.shape[0] // 4
    at = pl.ds(pl.multiple_of(place * new_rows, new_rows), new_rows)
    part = pl.ds(pl.multiple_of(place * ctx_rows, ctx_rows), ctx_rows)
    out[:new_rows, lanes] = qn[at]
    out[new_rows:, lanes] = qc[part]


def first_kernel(
    factor, frames_new, a0, a1, a2, a3, order, alive, biases, qn, qc, cn, e3, keys, values
):
    z = lax.axis_index("seq")

    @pl.when(middle(z))
    def _():
        places = far_places(z)
        gather_heads(places, (a0, a1, a2, a3), qc.shape[0] // 4, keys, values, qn, qc)
        attend_heads(factor, frames_new, order, alive, biases, keys, values, qn, qc)
        hand_out(places[3], e3, slice(None), qn, qc)
        ctx_rows = cn.shape[0] // 2
        fresh = qn.shape[0]
        hdim = values.shape[2] // 2
        spot = pl.ds(pl.multiple_of(places[1] * ctx_rows, ctx_rows), ctx_rows)
        move = order[spot]
        cn[:ctx_rows] = jnp.dot(
            move, keys[fresh:], preferred_element_type=jnp.float32
        ).astype(jnp.bfloat16)
        for h in range(values.shape[0]):
            cn[ctx_rows:, h * hdim : (h + 1) * hdim] = jnp.dot(
                move, values[h, fresh:, :hdim], preferred_element_type=jnp.float32
            ).astype(jnp.bfloat16)


def second_kernel(
    factor, frames_new, b0, b3, b2, b1, order, alive, biases, fn, fc,
    o0, o1, o2, n3, keys, values, qn, qc,
):
    z = lax.axis_index("seq")
    most = fn.shape[1]

    @pl.when(middle(z))
    def _():
        places = far_places(z)
        gather_heads(places, (b0, b1, b2, b3), qc.shape[0] // 4, keys, values, qn, qc)
        attend_heads(factor, frames_new, order, alive, biases, keys, values, qn, qc)
        hand_out(places[3], n3, slice(None), qn, qc)
        for place, out in zip(places, (o0, o1, o2)):
            hand_out(place, out, slice(0, most), fn, fc)
            hand_out(place, out, slice(most, None), qn, qc)


def cache_kernel(
    a0, a1, a2, a3, b0, b1, b2, b3, order, c0, c1, c2, c3, kk
):
    z = lax.axis_index("seq")
    ctx_rows, half = c0.shape[0] // 2, c0.shape[1]
    rows = a0.shape[0] // 3
    new_rows = rows - ctx_rows
    most = a0.shape[1]

    @pl.when(middle(z))
    def _():
        places = far_places(z)
        for place, a, b in zip(places, (a0, a1, a2, a3), (b0, b1, b2, b3)):
            to = pl.ds(pl.multiple_of(place * ctx_rows, ctx_rows), ctx_rows)
            for part in range(2):
                at = slice(part * rows + new_rows, (part + 1) * rows)
                kk[to, part * half : part * half + most] = a[at]
                kk[to, part * half + most : (part + 1) * half] = b[at]
        spot = pl.ds(pl.multiple_of(places[1] * ctx_rows, ctx_rows), ctx_rows)
        for part in range(2):
            moved = jnp.dot(
                order[spot],
                kk[:, part * half + most : (part + 1) * half],
                preferred_element_type=jnp.float32,
            )
            c1[part * ctx_rows : (part + 1) * ctx_rows] = moved.astype(jnp.bfloat16)
        for place, out in ((places[0], c0), (places[2], c2), (places[3], c3)):
            part = pl.ds(pl.multiple_of(place * ctx_rows, ctx_rows), ctx_rows)
            moved = jnp.dot(order[part], kk[...], preferred_element_type=jnp.float32)
            out[:ctx_rows] = moved[:, :half].astype(jnp.bfloat16)
            out[ctx_rows:] = moved[:, half:].astype(jnp.bfloat16)


def halves(z, at, *parts):
    own, beside, across, beyond = (part[at] for part in parts)
    inner = middle(z)
    low = z < 2
    near = jnp.where(inner, own, beside)
    far = jnp.where(inner, across, beyond)
    return (jnp.where(low, near, far), jnp.where(low, far, near))


def project_kernel(mine, here, e3, o0, o1, n3, o2, weight, out):
    o3 = jnp.concatenate([e3[...], n3[...]], axis=1)
    a, b = halves(lax.axis_index("seq"), slice(None), o0, o1, o2, o3)
    mixed = jnp.concatenate([a, b], axis=1)
    width = mixed.shape[1]
    me = lax.axis_index("tensor")
    core = me % 2 if mine else 1 - me % 2
    chip = me // 2 if here else 1 - me // 2
    lanes = pl.ds(pl.multiple_of((2 * chip + core) * width, width), width)
    total = jnp.dot(mixed, weight[:, lanes], preferred_element_type=jnp.float32)
    out[...] = total.astype(out.dtype)


def add_kernel(keep, came, out):
    out[...] = (keep[...] + came[...].astype(jnp.float32)).astype(jnp.bfloat16)


def finish_kernel(last, keep, came, cn, c0, c3, cl, c2, out, out_ctx, keys, values):
    total = keep[...] + came[...].astype(jnp.float32) + last[...].astype(jnp.float32)
    total = total.astype(jnp.bfloat16)
    out[...] = total[: out.shape[0]]
    out_ctx[...] = total[out.shape[0] :]
    z = lax.axis_index("seq")
    ctx_rows, width = keys.shape
    half = width // 2
    c1 = jnp.concatenate([cn[...], cl[...]], axis=1)
    for i, part in enumerate((keys, values)):
        at = slice(i * ctx_rows, (i + 1) * ctx_rows)
        a, b = halves(z, at, c0, c1, c2, c3)
        part[:, :half] = a
        part[:, half:] = b


SMALL = pl.BlockSpec(memory_space=pltpu.SMEM)
AWAY = pl.BlockSpec(memory_space=pltpu.HBM)
WHOLE = pl.BlockSpec(memory_space=pltpu.VMEM)
LIMIT = pltpu.CompilerParams(vmem_limit_bytes=32 * 1024 * 1024)


def lasts(us):
    return pl.CostEstimate(flops=int(us * 1.1e9), bytes_accessed=0, transcendentals=0)


def shape16(*dims):
    return jax.ShapeDtypeStruct(dims, jnp.bfloat16)


def permute(x, pairs):
    return lax.ppermute(x, "seq", pairs)


BESIDE = ((0, 1), (3, 2))
ACROSS = ((1, 2), (2, 1))
BEYOND = ((0, 2), (3, 1))
SIBLING = ((0, 1), (1, 0), (2, 3), (3, 2))
OPPOSITE = ((0, 2), (2, 0), (1, 3), (3, 1))


def back(pairs):
    return tuple((b, a) for a, b in pairs)


def fast_device(
    queries,
    new_keys,
    new_values,
    context_queries,
    context_keys,
    context_values,
    levels,
    frame_mask,
    owners,
    out_weight,
):
    new_rows, width = queries.shape
    ctx_rows = context_keys.shape[0]
    rows = new_rows + ctx_rows
    half = width // 2
    devices = lax.axis_size("seq")
    ctx_all = ctx_rows * devices
    hdim = HEAD_DIM
    frames_new = frame_mask.shape[0]
    factor = math.log2(math.e) / math.sqrt(hdim)
    most = max(hdim, half - hdim)
    near_a, near_b, far_a, far_b = pl.pallas_call(
        pack_kernel,
        out_shape=(
            shape16(3 * rows, most),
            shape16(3 * rows, half - most),
            shape16(3 * rows, most),
            shape16(3 * rows, half - most),
        ),
        in_specs=[AWAY] * 7,
        out_specs=[WHOLE] * 4,
        scratch_shapes=[pltpu.SMEM(levels.shape, jnp.int32)]
        + [pltpu.VMEM((ctx_rows, width), jnp.bfloat16)] * 3
        + [pltpu.SemaphoreType.DMA((16,))],
        name="pack",
    )(levels, queries, new_keys, new_values, context_queries, context_keys, context_values)
    beside_a = permute(near_a, BESIDE)
    across_a = permute(far_a, ACROSS)
    beyond_a = permute(far_a, BEYOND)
    beside_b = permute(near_b, BESIDE)
    across_b = permute(far_b, ACROSS)
    beyond_b = permute(far_b, BEYOND)
    order, alive, biases = pl.pallas_call(
        plan_kernel,
        out_shape=(
            shape16(ctx_all, ctx_all),
            jax.ShapeDtypeStruct((ctx_all, hdim), jnp.float32),
            jax.ShapeDtypeStruct((8, ctx_all), jnp.float32),
        ),
        in_specs=[WHOLE, SMALL, SMALL],
        compiler_params=LIMIT,
        name="plan", cost_estimate=lasts(1.6),
    )(owners.reshape(1, -1), levels, frame_mask)
    def scratch(lanes):
        return [
            pltpu.VMEM((rows * devices, lanes), jnp.bfloat16),
            pltpu.VMEM((lanes // hdim, rows * devices, 2 * hdim), jnp.bfloat16),
        ]

    fresh, held, early_cache, early_beyond = pl.pallas_call(
        functools.partial(first_kernel, factor, frames_new),
        out_shape=[
            shape16(new_rows * devices, most),
            shape16(ctx_all, most),
            shape16(2 * ctx_rows, most),
            shape16(rows, most),
        ],
        scratch_shapes=scratch(most),
        compiler_params=LIMIT,
        name="attend_first",
        cost_estimate=lasts(4.8),
    )(near_a, beside_a, across_a, beyond_a, order, alive, biases)
    results = pl.pallas_call(
        functools.partial(second_kernel, factor, frames_new),
        out_shape=[
            shape16(rows, half),
            shape16(rows, half),
            shape16(rows, half),
            shape16(rows, half - most),
        ],
        scratch_shapes=scratch(half - most)
        + [
            pltpu.VMEM((new_rows * devices, half - most), jnp.bfloat16),
            pltpu.VMEM((ctx_all, half - most), jnp.bfloat16),
        ],
        compiler_params=LIMIT,
        name="attend_second",
        cost_estimate=lasts(2.4),
    )(near_b, beyond_b, across_b, beside_b, order, alive, biases, fresh, held)
    own, beside, across, late_beyond = results
    early_cache = permute(early_cache, back(BESIDE))
    early_beyond = permute(early_beyond, back(BEYOND))
    across = lax.optimization_barrier((across, early_cache, early_beyond))[0]
    mixed = (
        early_beyond,
        own,
        permute(beside, back(BESIDE)),
        permute(late_beyond, back(BEYOND)),
        permute(across, ACROSS),
    )
    near_a = lax.optimization_barrier((near_a, results[0]))[0]
    caches = pl.pallas_call(
        cache_kernel,
        out_shape=[
            shape16(2 * ctx_rows, half),
            shape16(2 * ctx_rows, half - most),
            shape16(2 * ctx_rows, half),
            shape16(2 * ctx_rows, half),
        ],
        scratch_shapes=[pltpu.VMEM((ctx_all, width), jnp.bfloat16)],
        compiler_params=LIMIT,
        name="caches",
        cost_estimate=lasts(3),
    )(near_a, beside_a, across_a, beyond_a, near_b, beside_b, across_b, beyond_b, order)

    mixed = lax.optimization_barrier((*mixed, caches[0]))[:5]

    def project(mine, here, dtype):
        return pl.pallas_call(
            functools.partial(project_kernel, mine, here),
            out_shape=jax.ShapeDtypeStruct((rows, width), dtype),
            in_specs=[WHOLE] * 6,
            compiler_params=LIMIT,
            name=("keep" if mine else "give") + ("_here" if here else "_there"),
            cost_estimate=lasts(0.6),
        )(*mixed, out_weight)

    give_there = project(False, False, jnp.bfloat16)
    came_there = lax.ppermute(give_there, "tensor", SIBLING)
    keep_there = project(True, False, jnp.float32)
    other = pl.pallas_call(
        add_kernel,
        out_shape=shape16(rows, width),
        compiler_params=LIMIT,
        name="add",
        cost_estimate=lasts(0.1),
    )(keep_there, came_there)
    last = lax.ppermute(other, "tensor", OPPOSITE)
    caches = lax.optimization_barrier((*caches, other))[:4]
    beyond = permute(caches[3], back(BEYOND))
    across = permute(caches[2], ACROSS)
    beside = permute(caches[1], back(BESIDE))
    stored = (early_cache, caches[0], beyond, beside, across)
    mixed = lax.optimization_barrier((*mixed, keep_there))[:5]
    came = lax.ppermute(project(False, True, jnp.bfloat16), "tensor", SIBLING)
    keep = project(True, True, jnp.float32)
    block_out, context_out, cache_keys, cache_values = pl.pallas_call(
        finish_kernel,
        out_shape=(
            shape16(new_rows, width),
            shape16(ctx_rows, width),
            shape16(ctx_rows, width),
            shape16(ctx_rows, width),
        ),
        compiler_params=LIMIT,
        name="finish",
        cost_estimate=lasts(1.0),
    )(last, keep, came, *stored)
    return (block_out, context_out, cache_keys, cache_values)


def solution(mesh):
    rows = P(("session", "seq"), "tensor")
    in_specs = (rows,) * 6 + (P("session"), P("session", None), P("session"), P("tensor", None))
    sizes = mesh.shape
    step = fast_device if sizes["seq"] == 4 and sizes["tensor"] == 4 else per_device
    return jax.shard_map(
        step, mesh=mesh, in_specs=in_specs, out_specs=(rows,) * 4, check_vma=False
    )
```

```python
import functools
import math

import jax
import jax.numpy as jnp
from jax import lax
from jax.experimental import pallas as pl
from jax.experimental.pallas import tpu as pltpu
from jax.sharding import PartitionSpec as P

HEAD_DIM = 128


NEGATIVE = -1e30


def lookup(table, index):
    hits = index[..., None] == jnp.arange(table.shape[0], dtype=jnp.int32)
    return jnp.sum(jnp.where(hits, table, 0), axis=-1)


def pool_blocks(rows, coarse):
    blocks = rows.reshape(-1, 4, rows.shape[-1])
    mean = jnp.mean(blocks.astype(jnp.float32), axis=1).astype(jnp.bfloat16)
    first = (jnp.arange(4) == 0)[None, :, None]
    pooled = jnp.where(first, mean[:, None, :], jnp.zeros_like(blocks))
    return jnp.where(coarse[:, None, None], pooled, blocks)


def group_plan(total_rows, shard_rows):
    shards = total_rows // shard_rows
    group = math.gcd(shards, max(1, 1024 // shard_rows))
    return (shards // group, group)


def attend(state, heads_q, keys, values, allowed, scale):
    best, total, accum = state
    count = keys.shape[0]
    heads = heads_q.shape[0]
    hdim = heads_q.shape[2]
    keys_h = keys.reshape(count, heads, hdim)
    values_h = values.reshape(count, heads, hdim)
    scores = jnp.einsum("hqd,khd->hqk", heads_q, keys_h, preferred_element_type=jnp.float32) * scale
    if allowed is not None:
        scores = jnp.where(allowed[None], scores, NEGATIVE)
    fresh = jnp.maximum(best, jnp.max(scores, axis=2))
    weights = jnp.exp(scores - fresh[..., None])
    if allowed is not None:
        weights = jnp.where(allowed[None], weights, 0.0)
    decay = jnp.exp(best - fresh)
    total = total * decay + jnp.sum(weights, axis=2)
    accum = accum * decay[..., None] + jnp.einsum(
        "hqk,khd->hqd", weights.astype(jnp.bfloat16), values_h, preferred_element_type=jnp.float32
    )
    return (fresh, total, accum)


def per_device(
    queries,
    new_keys,
    new_values,
    context_queries,
    context_keys,
    context_values,
    levels,
    frame_mask,
    owners,
    out_weight,
):
    width = queries.shape[1]
    new_rows = queries.shape[0]
    ctx_rows = context_keys.shape[0]
    blocks_dev = ctx_rows // 4
    devices = lax.axis_size("seq")
    place = lax.axis_index("seq")
    blocks_all = blocks_dev * devices
    frames_ctx = levels.shape[0]
    frames_new = frame_mask.shape[0]
    new_all = new_rows * devices
    hdim = HEAD_DIM
    heads = width // hdim
    scale = 1.0 / math.sqrt(hdim)
    pair = max(2, 2 * blocks_dev // devices)
    block_ids = jnp.arange(blocks_all, dtype=jnp.int32)
    block_frame = block_ids * frames_ctx // blocks_all
    coarse_all = lookup(levels, block_frame) == 1
    mine = owners == place
    rank = jnp.cumsum(mine.astype(jnp.int32)) - 1
    own_coarse = lax.dynamic_slice_in_dim(coarse_all, place * blocks_dev, blocks_dev)
    pooled_q = pool_blocks(context_queries, own_coarse)
    pooled_k = pool_blocks(context_keys, own_coarse)
    pooled_v = pool_blocks(context_values, own_coarse)
    slots = jnp.arange(blocks_dev, dtype=jnp.int32)[:, None] == rank[None, :]
    held_coarse = jnp.any(slots & mine[None, :] & coarse_all[None, :], axis=1)
    held_live = jnp.logical_or(
        jnp.logical_not(held_coarse)[:, None], (jnp.arange(4) == 0)[None, :]
    ).reshape(ctx_rows)
    my_owners = lax.dynamic_slice_in_dim(owners, place * blocks_dev, blocks_dev)
    hits = my_owners[:, None] == jnp.arange(devices, dtype=jnp.int32)[None, :]
    within = jnp.sum(jnp.where(hits, jnp.cumsum(hits.astype(jnp.int32), axis=0) - 1, 0), axis=1)
    send_slot = my_owners * pair + within

    def pack(blocks):
        buffer = jnp.zeros((devices * pair, 4, width), blocks.dtype).at[send_slot].set(blocks)
        return buffer.reshape(devices, pair * 4, width)

    counts = jnp.sum((owners.reshape(devices, blocks_dev) == place).astype(jnp.int32), axis=1)
    before = jnp.cumsum(counts) - counts
    order_in = jnp.arange(pair, dtype=jnp.int32)[None, :]
    target = jnp.where(order_in < counts[:, None], before[:, None] + order_in, blocks_dev).reshape(
        -1
    )

    def unpack(arrived):
        blocks = arrived.reshape(devices * pair, 4, width)
        return jnp.zeros((blocks_dev, 4, width), arrived.dtype).at[target].set(blocks, mode="drop")

    arrived = (
        lax.all_to_all(pack(pooled_q), "seq", split_axis=0, concat_axis=0, tiled=True),
        lax.all_to_all(pack(pooled_k), "seq", split_axis=0, concat_axis=0, tiled=True),
        lax.all_to_all(pack(pooled_v), "seq", split_axis=0, concat_axis=0, tiled=True),
    )
    held_q = unpack(arrived[0])
    held_k = unpack(arrived[1])
    held_v = unpack(arrived[2])
    all_q = jnp.concatenate([queries, held_q.reshape(ctx_rows, width)], axis=0)
    rows_q = all_q.shape[0]
    heads_q = all_q.reshape(rows_q, heads, hdim).transpose(1, 0, 2)
    q_global = place * new_rows + jnp.arange(new_rows, dtype=jnp.int32)
    q_frame = q_global * frames_new // new_all
    frame_hits = (q_frame[:, None] == jnp.arange(frames_new, dtype=jnp.int32)[None, :])[:, :, None]
    new_mask = jnp.sum(jnp.where(frame_hits, frame_mask[None], 0), axis=1)
    query_mask = jnp.concatenate(
        [new_mask, jnp.ones((ctx_rows, frames_ctx), jnp.int32)], axis=0
    ).astype(jnp.float32)

    def context_allowed(first_shard, count_rows):
        index = first_shard * ctx_rows + jnp.arange(count_rows, dtype=jnp.int32)
        frame = index // 4 * frames_ctx // blocks_all
        coarse = lookup(levels, frame) == 1
        live = jnp.logical_or(jnp.logical_not(coarse), index % 4 == 0)
        onehot = (frame[:, None] == jnp.arange(frames_ctx, dtype=jnp.int32)[None, :]).astype(
            jnp.float32
        )
        reach = jnp.dot(query_mask, onehot.T) > 0.5
        return jnp.logical_and(reach, live[None, :])

    def take_new(state, keys, values):
        return attend(state, heads_q, keys, values, None, scale)

    def take_context(state, keys, values, first_shard):
        allowed = context_allowed(first_shard, keys.shape[0])
        return attend(state, heads_q, keys, values, allowed, scale)

    start_state = (
        jnp.full((heads, rows_q), NEGATIVE, jnp.float32),
        jnp.zeros((heads, rows_q), jnp.float32),
        jnp.zeros((heads, rows_q, hdim), jnp.float32),
    )
    empty_cache = (
        jnp.zeros((blocks_dev, 4, width), jnp.bfloat16),
        jnp.zeros((blocks_dev, 4, width), jnp.bfloat16),
    )
    flat_k = pooled_k.reshape(ctx_rows, width)
    flat_v = pooled_v.reshape(ctx_rows, width)
    piece = (
        lax.all_gather(new_keys, "seq", axis=0, tiled=True),
        lax.all_gather(new_values, "seq", axis=0, tiled=True),
    )
    steps, group = group_plan(piece[0].shape[0], new_rows)
    size = group * new_rows
    stacked = (piece[0].reshape(steps, size, width), piece[1].reshape(steps, size, width))

    def one(carry, item):
        return (take_new(carry, item[0], item[1]), None)

    state = lax.scan(one, start_state, stacked)[0]
    piece = (
        lax.all_gather(flat_k, "seq", axis=0, tiled=True),
        lax.all_gather(flat_v, "seq", axis=0, tiled=True),
    )
    steps, group = group_plan(piece[0].shape[0], ctx_rows)
    size = group * ctx_rows
    firsts = jnp.arange(steps, dtype=jnp.int32) * group
    stacked = (piece[0].reshape(steps, size, width), piece[1].reshape(steps, size, width), firsts)

    def one(inner, item):
        keys, values, first = item
        attended = take_context(inner[0], keys, values, first)
        cache = inner[1]
        return ((attended, cache), None)

    state, cache = lax.scan(one, (state, empty_cache), stacked)[0]
    best, total, accum = state
    mixed = (accum / total[..., None]).transpose(1, 0, 2).reshape(rows_q, width)
    live_rows = jnp.concatenate([jnp.ones((new_rows,), dtype=bool), held_live], axis=0)
    mixed = jnp.where(live_rows[:, None], mixed, 0.0).astype(jnp.bfloat16)
    summed = lax.psum_scatter(
        lax.dot_general(
            out_weight, mixed, (((0,), (1,)), ((), ())), preferred_element_type=jnp.float32
        ).astype(jnp.bfloat16),
        "tensor",
        scatter_dimension=0,
        tiled=True,
    ).astype(jnp.float32)
    result = summed.T.astype(jnp.bfloat16)
    return (
        result[:new_rows],
        result[new_rows:],
        held_k.reshape(ctx_rows, width),
        held_v.reshape(ctx_rows, width),
    )


def place_index(shape, dim):
    return lax.broadcasted_iota(jnp.int32, shape, dim)


def coarse_of(frame, levels_ref, frames_ctx):
    coarse = frame < 0
    for f in range(frames_ctx):
        coarse = jnp.logical_or(coarse, jnp.logical_and(frame == f, levels_ref[f] == 1))
    return coarse


def pack_kernel(
    levels, q, k, v, cq, ck, cv, near_a, near_b, far_a, far_b,
    lv, nk, nv, nq, sk, sv, sq, tk, tv, tq, sems,
):
    z = lax.axis_index("seq")
    devices = lax.axis_size("seq")
    new_rows, width = q.shape
    ctx_rows = cq.shape[0]
    half = width // 2
    most = near_a.shape[1]
    rows = new_rows + ctx_rows
    frames_ctx = levels.shape[0]
    low = jnp.where(z < devices // 2, 0, half)
    places = (
        (far_a, half - low, most),
        (near_a, low, most),
        (far_b, half - low + most, half - most),
        (near_b, low + most, half - most),
    )
    places = [(out, pl.ds(pl.multiple_of(at, 128), size)) for out, at, size in places]
    started = []

    def start(src, dst):
        copy = pltpu.make_async_copy(src, dst, sems.at[len(started)])
        copy.start()
        started.append(copy)
        return copy

    def send(src, base):
        for out, lanes in places:
            start(src.at[:, lanes], out.at[base : base + src.shape[0]])

    reads = [start(levels, lv), start(ck, sk), start(cv, sv), start(cq, sq)]
    reads += [start(k, nk), start(v, nv), start(q, nq)]
    reads[0].wait()
    index = place_index((ctx_rows, 1), 0)
    first = index % 4 == 0
    frame = (z * ctx_rows + index) * frames_ctx // (devices * ctx_rows)
    coarse = coarse_of(frame, lv, frames_ctx)
    for part, (src, dst) in enumerate(((sk, tk), (sv, tv), (sq, tq))):
        reads[part + 1].wait()
        wide = src[...].astype(jnp.float32)
        pair = wide + pltpu.roll(wide, ctx_rows - 1, 0)
        quad = pair + pltpu.roll(pair, ctx_rows - 2, 0)
        mean = jnp.where(first, quad * 0.25, 0.0)
        dst[...] = jnp.where(coarse, mean, wide).astype(jnp.bfloat16)
        send(dst, part * rows + new_rows)
    for part, src in enumerate((nk, nv, nq)):
        reads[part + 4].wait()
        send(src, part * rows)
    for copy in started[7:]:
        copy.wait()


def plan_kernel(owners, levels, masks, order, alive, biases):
    blocks = owners.shape[1]
    size = order.shape[0]
    per = size // blocks
    devices = lax.axis_size("seq")
    frames_ctx = levels.shape[0]
    row = owners[...].astype(jnp.float32)
    r = place_index((blocks, blocks), 0)
    c = place_index((blocks, blocks), 1)
    col = jnp.sum(jnp.where(r == c, row, 0.0), axis=1, keepdims=True)
    ahead = jnp.logical_and(col == row, r < c)
    rank = jnp.sum(ahead.astype(jnp.float32), axis=0, keepdims=True)
    spot = row * float(blocks // devices) + rank
    spread = (
        place_index((blocks, size), 1) // per == place_index((blocks, size), 0)
    ).astype(jnp.bfloat16)
    wide = jnp.dot(
        jnp.broadcast_to(spot, (16, blocks)).astype(jnp.bfloat16),
        spread,
        preferred_element_type=jnp.float32,
    )[0:1]
    lane = place_index((1, size), 1)
    target = wide.astype(jnp.int32) * per + lane % per
    move = (place_index((size, size), 0) == target).astype(jnp.bfloat16)
    order[...] = move
    index = place_index((size, alive.shape[1]), 0)
    coarse = coarse_of(index * frames_ctx // size, levels, frames_ctx)
    live = jnp.logical_or(jnp.logical_not(coarse), index % per == 0)
    alive[...] = jnp.dot(
        move, live.astype(jnp.bfloat16), preferred_element_type=jnp.float32
    )
    frame = lane * frames_ctx // size
    live = jnp.logical_or(
        jnp.logical_not(coarse_of(frame, levels, frames_ctx)), lane % per == 0
    )
    biases[...] = jnp.zeros_like(biases)
    biases[0:1] = jnp.where(live, 0.0, NEGATIVE)
    for g in range(masks.shape[0]):
        seen = frame < 0
        for f in range(frames_ctx):
            seen = jnp.logical_or(seen, jnp.logical_and(frame == f, masks[g, f] == 1))
        biases[g + 1 : g + 2] = jnp.where(jnp.logical_and(live, seen), 0.0, NEGATIVE)


def far_places(z):
    across = 3 - z
    beside = jnp.where(z == 1, 0, 3)
    return (z, beside, across, 3 - beside)


def middle(z):
    return jnp.logical_or(z == 1, z == 2)


def run_jobs(jobs, keys, values, fresh, factor):
    hdim = values.shape[2] // 2

    def score(head, q):
        lanes = slice(head * hdim, (head + 1) * hdim)
        return lax.dot_general(
            q, keys[:, lanes], (((1,), (1,)), ((), ())), preferred_element_type=jnp.float32
        )

    def finish(head, scores, bias):
        ahead = scores[:, :fresh]
        behind = scores[:, fresh:] + bias
        top = jnp.maximum(
            jnp.max(ahead, axis=1, keepdims=True), jnp.max(behind, axis=1, keepdims=True)
        )
        w_ahead = jnp.exp2((ahead - top) * factor).astype(jnp.bfloat16)
        w_behind = jnp.exp2((behind - top) * factor).astype(jnp.bfloat16)
        both = jnp.dot(
            w_ahead, values[head, :fresh], preferred_element_type=jnp.float32
        ) + jnp.dot(w_behind, values[head, fresh:], preferred_element_type=jnp.float32)
        return both[:, :hdim] / both[:, hdim:]

    held = None
    for job in [*jobs, None]:
        scores = None if job is None else score(job[0], job[1]())
        if held is not None:
            held[3](finish(held[0], held[4], held[2]))
        held = None if job is None else (*job, scores)


def gather_heads(places, sources, ctx_rows, keys, values, qn, qc):
    rows = sources[0].shape[0] // 3
    new_rows = rows - ctx_rows
    fresh = len(sources) * new_rows
    heads = values.shape[0]
    hdim = values.shape[2] // 2
    values[:, :, hdim:] = jnp.ones((heads, values.shape[1], hdim), jnp.bfloat16)
    for place, src in zip(places, sources):
        at = pl.ds(pl.multiple_of(place * new_rows, new_rows), new_rows)
        spot = pl.ds(pl.multiple_of(place * ctx_rows, ctx_rows), ctx_rows)
        to = pl.ds(pl.multiple_of(fresh + place * ctx_rows, ctx_rows), ctx_rows)
        keys[at] = src[0:new_rows]
        keys[to] = src[new_rows:rows]
        qn[at] = src[2 * rows : 2 * rows + new_rows]
        qc[spot] = src[2 * rows + new_rows : 3 * rows]
        for h in range(heads):
            lanes = slice(h * hdim, (h + 1) * hdim)
            values[h, at, :hdim] = src[rows : rows + new_rows, lanes]
            values[h, to, :hdim] = src[rows + new_rows : 2 * rows, lanes]


def attend_heads(factor, frames_new, order, alive, biases, keys, values, qn, qc):
    heads = values.shape[0]
    hdim = values.shape[2] // 2
    fresh = qn.shape[0]
    per = fresh // frames_new
    qc[...] = jnp.dot(order[...], qc[...], preferred_element_type=jnp.float32).astype(
        jnp.bfloat16
    )
    jobs = []
    for h in range(heads):
        lanes = slice(h * hdim, (h + 1) * hdim)
        for g in range(frames_new):
            at = slice(g * per, (g + 1) * per)

            def put_new(r, at=at, lanes=lanes):
                qn[at, lanes] = r.astype(jnp.bfloat16)

            jobs.append(
                (h, lambda at=at, lanes=lanes: qn[at, lanes], biases[g + 1 : g + 2], put_new)
            )

        def put_ctx(r, lanes=lanes):
            qc[:, lanes] = (r * alive[...]).astype(jnp.bfloat16)

        jobs.append((h, lambda lanes=lanes: qc[:, lanes], biases[0:1], put_ctx))
    run_jobs(jobs, keys, values, fresh, factor)


def hand_out(place, out, lanes, qn, qc):
    new_rows = qn.shape[0] // 4
    ctx_rows = qc.shape[0] // 4
    at = pl.ds(pl.multiple_of(place * new_rows, new_rows), new_rows)
    part = pl.ds(pl.multiple_of(place * ctx_rows, ctx_rows), ctx_rows)
    out[:new_rows, lanes] = qn[at]
    out[new_rows:, lanes] = qc[part]


def first_kernel(
    factor, frames_new, a0, a1, a2, a3, order, alive, biases, qn, qc, cn, e3, keys, values
):
    z = lax.axis_index("seq")

    @pl.when(middle(z))
    def _():
        places = far_places(z)
        gather_heads(places, (a0, a1, a2, a3), qc.shape[0] // 4, keys, values, qn, qc)
        attend_heads(factor, frames_new, order, alive, biases, keys, values, qn, qc)
        hand_out(places[3], e3, slice(None), qn, qc)
        ctx_rows = cn.shape[0] // 2
        fresh = qn.shape[0]
        hdim = values.shape[2] // 2
        spot = pl.ds(pl.multiple_of(places[1] * ctx_rows, ctx_rows), ctx_rows)
        move = order[spot]
        cn[:ctx_rows] = jnp.dot(
            move, keys[fresh:], preferred_element_type=jnp.float32
        ).astype(jnp.bfloat16)
        for h in range(values.shape[0]):
            cn[ctx_rows:, h * hdim : (h + 1) * hdim] = jnp.dot(
                move, values[h, fresh:, :hdim], preferred_element_type=jnp.float32
            ).astype(jnp.bfloat16)


def second_kernel(
    factor, frames_new, b0, b3, b2, b1, order, alive, biases, fn, fc,
    o0, o1, o2, n3, keys, values, qn, qc,
):
    z = lax.axis_index("seq")
    most = fn.shape[1]

    @pl.when(middle(z))
    def _():
        places = far_places(z)
        gather_heads(places, (b0, b1, b2, b3), qc.shape[0] // 4, keys, values, qn, qc)
        attend_heads(factor, frames_new, order, alive, biases, keys, values, qn, qc)
        hand_out(places[3], n3, slice(None), qn, qc)
        for place, out in zip(places, (o0, o1, o2)):
            hand_out(place, out, slice(0, most), fn, fc)
            hand_out(place, out, slice(most, None), qn, qc)


def cache_kernel(
    a0, a1, a2, a3, b0, b1, b2, b3, order, c0, c1, c2, c3, kk
):
    z = lax.axis_index("seq")
    ctx_rows, half = c0.shape[0] // 2, c0.shape[1]
    rows = a0.shape[0] // 3
    new_rows = rows - ctx_rows
    most = a0.shape[1]

    @pl.when(middle(z))
    def _():
        places = far_places(z)
        for place, a, b in zip(places, (a0, a1, a2, a3), (b0, b1, b2, b3)):
            to = pl.ds(pl.multiple_of(place * ctx_rows, ctx_rows), ctx_rows)
            for part in range(2):
                at = slice(part * rows + new_rows, (part + 1) * rows)
                kk[to, part * half : part * half + most] = a[at]
                kk[to, part * half + most : (part + 1) * half] = b[at]
        spot = pl.ds(pl.multiple_of(places[1] * ctx_rows, ctx_rows), ctx_rows)
        for part in range(2):
            moved = jnp.dot(
                order[spot],
                kk[:, part * half + most : (part + 1) * half],
                preferred_element_type=jnp.float32,
            )
            c1[part * ctx_rows : (part + 1) * ctx_rows] = moved.astype(jnp.bfloat16)
        for place, out in ((places[0], c0), (places[2], c2), (places[3], c3)):
            part = pl.ds(pl.multiple_of(place * ctx_rows, ctx_rows), ctx_rows)
            moved = jnp.dot(order[part], kk[...], preferred_element_type=jnp.float32)
            out[:ctx_rows] = moved[:, :half].astype(jnp.bfloat16)
            out[ctx_rows:] = moved[:, half:].astype(jnp.bfloat16)


def halves(z, at, *parts):
    own, beside, across, beyond = (part[at] for part in parts)
    inner = middle(z)
    low = z < 2
    near = jnp.where(inner, own, beside)
    far = jnp.where(inner, across, beyond)
    return (jnp.where(low, near, far), jnp.where(low, far, near))


def project_kernel(mine, here, e3, o0, o1, n3, o2, weight, out):
    o3 = jnp.concatenate([e3[...], n3[...]], axis=1)
    a, b = halves(lax.axis_index("seq"), slice(None), o0, o1, o2, o3)
    mixed = jnp.concatenate([a, b], axis=1)
    width = mixed.shape[1]
    me = lax.axis_index("tensor")
    core = me % 2 if mine else 1 - me % 2
    chip = me // 2 if here else 1 - me // 2
    lanes = pl.ds(pl.multiple_of((2 * chip + core) * width, width), width)
    total = jnp.dot(mixed, weight[:, lanes], preferred_element_type=jnp.float32)
    out[...] = total.astype(out.dtype)


def add_kernel(keep, came, out):
    out[...] = (keep[...] + came[...].astype(jnp.float32)).astype(jnp.bfloat16)


def finish_kernel(last, keep, came, cn, c0, cl, c3, c2, out, out_ctx, keys, values):
    total = keep[...] + came[...].astype(jnp.float32) + last[...].astype(jnp.float32)
    total = total.astype(jnp.bfloat16)
    out[...] = total[: out.shape[0]]
    out_ctx[...] = total[out.shape[0] :]
    z = lax.axis_index("seq")
    ctx_rows, width = keys.shape
    half = width // 2
    c1 = jnp.concatenate([cn[...], cl[...]], axis=1)
    for i, part in enumerate((keys, values)):
        at = slice(i * ctx_rows, (i + 1) * ctx_rows)
        a, b = halves(z, at, c0, c1, c2, c3)
        part[:, :half] = a
        part[:, half:] = b


SMALL = pl.BlockSpec(memory_space=pltpu.SMEM)
AWAY = pl.BlockSpec(memory_space=pltpu.HBM)
WHOLE = pl.BlockSpec(memory_space=pltpu.VMEM)
LIMIT = pltpu.CompilerParams(vmem_limit_bytes=32 * 1024 * 1024)


def lasts(us):
    return pl.CostEstimate(flops=int(us * 1.1e9), bytes_accessed=0, transcendentals=0)


def shape16(*dims):
    return jax.ShapeDtypeStruct(dims, jnp.bfloat16)


def permute(x, pairs):
    return lax.ppermute(x, "seq", pairs)


BESIDE = ((0, 1), (3, 2))
ACROSS = ((1, 2), (2, 1))
BEYOND = ((0, 2), (3, 1))
SIBLING = ((0, 1), (1, 0), (2, 3), (3, 2))
OPPOSITE = ((0, 2), (2, 0), (1, 3), (3, 1))


def back(pairs):
    return tuple((b, a) for a, b in pairs)


def fast_device(
    queries,
    new_keys,
    new_values,
    context_queries,
    context_keys,
    context_values,
    levels,
    frame_mask,
    owners,
    out_weight,
):
    new_rows, width = queries.shape
    ctx_rows = context_keys.shape[0]
    rows = new_rows + ctx_rows
    half = width // 2
    devices = lax.axis_size("seq")
    ctx_all = ctx_rows * devices
    hdim = HEAD_DIM
    frames_new = frame_mask.shape[0]
    factor = math.log2(math.e) / math.sqrt(hdim)
    most = max(hdim, half - hdim)
    near_a, near_b, far_a, far_b = pl.pallas_call(
        pack_kernel,
        out_shape=(
            shape16(3 * rows, most),
            shape16(3 * rows, half - most),
            shape16(3 * rows, most),
            shape16(3 * rows, half - most),
        ),
        in_specs=[AWAY] * 7,
        out_specs=[AWAY] * 4,
        scratch_shapes=[pltpu.SMEM(levels.shape, jnp.int32)]
        + [pltpu.VMEM((new_rows, width), jnp.bfloat16)] * 3
        + [pltpu.VMEM((ctx_rows, width), jnp.bfloat16)] * 6
        + [pltpu.SemaphoreType.DMA((31,))],
        name="pack",
    )(levels, queries, new_keys, new_values, context_queries, context_keys, context_values)
    beside_a = permute(near_a, BESIDE)
    across_a = permute(far_a, ACROSS)
    beyond_a = permute(far_a, BEYOND)
    beside_b = permute(near_b, BESIDE)
    across_b = permute(far_b, ACROSS)
    beyond_b = permute(far_b, BEYOND)
    order, alive, biases = pl.pallas_call(
        plan_kernel,
        out_shape=(
            shape16(ctx_all, ctx_all),
            jax.ShapeDtypeStruct((ctx_all, hdim), jnp.float32),
            jax.ShapeDtypeStruct((8, ctx_all), jnp.float32),
        ),
        in_specs=[WHOLE, SMALL, SMALL],
        compiler_params=LIMIT,
        name="plan", cost_estimate=lasts(1.6),
    )(owners.reshape(1, -1), levels, frame_mask)
    def scratch(lanes):
        return [
            pltpu.VMEM((rows * devices, lanes), jnp.bfloat16),
            pltpu.VMEM((lanes // hdim, rows * devices, 2 * hdim), jnp.bfloat16),
        ]

    fresh, held, early_cache, early_beyond = pl.pallas_call(
        functools.partial(first_kernel, factor, frames_new),
        out_shape=[
            shape16(new_rows * devices, most),
            shape16(ctx_all, most),
            shape16(2 * ctx_rows, most),
            shape16(rows, most),
        ],
        scratch_shapes=scratch(most),
        compiler_params=LIMIT,
        name="attend_first",
        cost_estimate=lasts(4.8),
    )(near_a, beside_a, across_a, beyond_a, order, alive, biases)
    results = pl.pallas_call(
        functools.partial(second_kernel, factor, frames_new),
        out_shape=[
            shape16(rows, half),
            shape16(rows, half),
            shape16(rows, half),
            shape16(rows, half - most),
        ],
        scratch_shapes=scratch(half - most)
        + [
            pltpu.VMEM((new_rows * devices, half - most), jnp.bfloat16),
            pltpu.VMEM((ctx_all, half - most), jnp.bfloat16),
        ],
        compiler_params=LIMIT,
        name="attend_second",
        cost_estimate=lasts(2.4),
    )(near_b, beyond_b, across_b, beside_b, order, alive, biases, fresh, held)
    own, beside, across, late_beyond = results
    early_cache = permute(early_cache, back(BESIDE))
    early_beyond = permute(early_beyond, back(BEYOND))
    across = lax.optimization_barrier((across, early_cache, early_beyond))[0]
    mixed = (
        early_beyond,
        own,
        permute(beside, back(BESIDE)),
        permute(late_beyond, back(BEYOND)),
        permute(across, ACROSS),
    )
    near_a = lax.optimization_barrier((near_a, results[0]))[0]
    caches = pl.pallas_call(
        cache_kernel,
        out_shape=[
            shape16(2 * ctx_rows, half),
            shape16(2 * ctx_rows, half - most),
            shape16(2 * ctx_rows, half),
            shape16(2 * ctx_rows, half),
        ],
        scratch_shapes=[pltpu.VMEM((ctx_all, width), jnp.bfloat16)],
        compiler_params=LIMIT,
        name="caches",
        cost_estimate=lasts(3),
    )(near_a, beside_a, across_a, beyond_a, near_b, beside_b, across_b, beyond_b, order)

    mixed = lax.optimization_barrier((*mixed, caches[0]))[:5]

    def project(mine, here, dtype):
        return pl.pallas_call(
            functools.partial(project_kernel, mine, here),
            out_shape=jax.ShapeDtypeStruct((rows, width), dtype),
            in_specs=[WHOLE] * 6,
            compiler_params=LIMIT,
            name=("keep" if mine else "give") + ("_here" if here else "_there"),
            cost_estimate=lasts(0.6),
        )(*mixed, out_weight)

    give_there = project(False, False, jnp.bfloat16)
    came_there = lax.ppermute(give_there, "tensor", SIBLING)
    keep_there = project(True, False, jnp.float32)
    other = pl.pallas_call(
        add_kernel,
        out_shape=shape16(rows, width),
        compiler_params=LIMIT,
        name="add",
        cost_estimate=lasts(0.1),
    )(keep_there, came_there)
    last = lax.ppermute(other, "tensor", OPPOSITE)
    caches = lax.optimization_barrier((*caches, other))[:4]
    beyond = permute(caches[3], back(BEYOND))
    across = permute(caches[2], ACROSS)
    beside = permute(caches[1], back(BESIDE))
    stored = (early_cache, caches[0], beside, beyond, across)
    mixed = lax.optimization_barrier((*mixed, keep_there))[:5]
    came = lax.ppermute(project(False, True, jnp.bfloat16), "tensor", SIBLING)
    keep = project(True, True, jnp.float32)
    block_out, context_out, cache_keys, cache_values = pl.pallas_call(
        finish_kernel,
        out_shape=(
            shape16(new_rows, width),
            shape16(ctx_rows, width),
            shape16(ctx_rows, width),
            shape16(ctx_rows, width),
        ),
        compiler_params=LIMIT,
        name="finish",
        cost_estimate=lasts(1.0),
    )(last, keep, came, *stored)
    return (block_out, context_out, cache_keys, cache_values)


def solution(mesh):
    rows = P(("session", "seq"), "tensor")
    in_specs = (rows,) * 6 + (P("session"), P("session", None), P("session"), P("tensor", None))
    sizes = mesh.shape
    step = fast_device if sizes["seq"] == 4 and sizes["tensor"] == 4 else per_device
    return jax.shard_map(
        step, mesh=mesh, in_specs=in_specs, out_specs=(rows,) * 4, check_vma=False
    )
```

```python
import functools
import math

import jax
import jax.numpy as jnp
from jax import lax
from jax.experimental import pallas as pl
from jax.experimental.pallas import tpu as pltpu
from jax.sharding import PartitionSpec as P

HEAD_DIM = 128


NEGATIVE = -1e30


def lookup(table, index):
    hits = index[..., None] == jnp.arange(table.shape[0], dtype=jnp.int32)
    return jnp.sum(jnp.where(hits, table, 0), axis=-1)


def pool_blocks(rows, coarse):
    blocks = rows.reshape(-1, 4, rows.shape[-1])
    mean = jnp.mean(blocks.astype(jnp.float32), axis=1).astype(jnp.bfloat16)
    first = (jnp.arange(4) == 0)[None, :, None]
    pooled = jnp.where(first, mean[:, None, :], jnp.zeros_like(blocks))
    return jnp.where(coarse[:, None, None], pooled, blocks)


def group_plan(total_rows, shard_rows):
    shards = total_rows // shard_rows
    group = math.gcd(shards, max(1, 1024 // shard_rows))
    return (shards // group, group)


def attend(state, heads_q, keys, values, allowed, scale):
    best, total, accum = state
    count = keys.shape[0]
    heads = heads_q.shape[0]
    hdim = heads_q.shape[2]
    keys_h = keys.reshape(count, heads, hdim)
    values_h = values.reshape(count, heads, hdim)
    scores = jnp.einsum("hqd,khd->hqk", heads_q, keys_h, preferred_element_type=jnp.float32) * scale
    if allowed is not None:
        scores = jnp.where(allowed[None], scores, NEGATIVE)
    fresh = jnp.maximum(best, jnp.max(scores, axis=2))
    weights = jnp.exp(scores - fresh[..., None])
    if allowed is not None:
        weights = jnp.where(allowed[None], weights, 0.0)
    decay = jnp.exp(best - fresh)
    total = total * decay + jnp.sum(weights, axis=2)
    accum = accum * decay[..., None] + jnp.einsum(
        "hqk,khd->hqd", weights.astype(jnp.bfloat16), values_h, preferred_element_type=jnp.float32
    )
    return (fresh, total, accum)


def per_device(
    queries,
    new_keys,
    new_values,
    context_queries,
    context_keys,
    context_values,
    levels,
    frame_mask,
    owners,
    out_weight,
):
    width = queries.shape[1]
    new_rows = queries.shape[0]
    ctx_rows = context_keys.shape[0]
    blocks_dev = ctx_rows // 4
    devices = lax.axis_size("seq")
    place = lax.axis_index("seq")
    blocks_all = blocks_dev * devices
    frames_ctx = levels.shape[0]
    frames_new = frame_mask.shape[0]
    new_all = new_rows * devices
    hdim = HEAD_DIM
    heads = width // hdim
    scale = 1.0 / math.sqrt(hdim)
    pair = max(2, 2 * blocks_dev // devices)
    block_ids = jnp.arange(blocks_all, dtype=jnp.int32)
    block_frame = block_ids * frames_ctx // blocks_all
    coarse_all = lookup(levels, block_frame) == 1
    mine = owners == place
    rank = jnp.cumsum(mine.astype(jnp.int32)) - 1
    own_coarse = lax.dynamic_slice_in_dim(coarse_all, place * blocks_dev, blocks_dev)
    pooled_q = pool_blocks(context_queries, own_coarse)
    pooled_k = pool_blocks(context_keys, own_coarse)
    pooled_v = pool_blocks(context_values, own_coarse)
    slots = jnp.arange(blocks_dev, dtype=jnp.int32)[:, None] == rank[None, :]
    held_coarse = jnp.any(slots & mine[None, :] & coarse_all[None, :], axis=1)
    held_live = jnp.logical_or(
        jnp.logical_not(held_coarse)[:, None], (jnp.arange(4) == 0)[None, :]
    ).reshape(ctx_rows)
    my_owners = lax.dynamic_slice_in_dim(owners, place * blocks_dev, blocks_dev)
    hits = my_owners[:, None] == jnp.arange(devices, dtype=jnp.int32)[None, :]
    within = jnp.sum(jnp.where(hits, jnp.cumsum(hits.astype(jnp.int32), axis=0) - 1, 0), axis=1)
    send_slot = my_owners * pair + within

    def pack(blocks):
        buffer = jnp.zeros((devices * pair, 4, width), blocks.dtype).at[send_slot].set(blocks)
        return buffer.reshape(devices, pair * 4, width)

    counts = jnp.sum((owners.reshape(devices, blocks_dev) == place).astype(jnp.int32), axis=1)
    before = jnp.cumsum(counts) - counts
    order_in = jnp.arange(pair, dtype=jnp.int32)[None, :]
    target = jnp.where(order_in < counts[:, None], before[:, None] + order_in, blocks_dev).reshape(
        -1
    )

    def unpack(arrived):
        blocks = arrived.reshape(devices * pair, 4, width)
        return jnp.zeros((blocks_dev, 4, width), arrived.dtype).at[target].set(blocks, mode="drop")

    arrived = (
        lax.all_to_all(pack(pooled_q), "seq", split_axis=0, concat_axis=0, tiled=True),
        lax.all_to_all(pack(pooled_k), "seq", split_axis=0, concat_axis=0, tiled=True),
        lax.all_to_all(pack(pooled_v), "seq", split_axis=0, concat_axis=0, tiled=True),
    )
    held_q = unpack(arrived[0])
    held_k = unpack(arrived[1])
    held_v = unpack(arrived[2])
    all_q = jnp.concatenate([queries, held_q.reshape(ctx_rows, width)], axis=0)
    rows_q = all_q.shape[0]
    heads_q = all_q.reshape(rows_q, heads, hdim).transpose(1, 0, 2)
    q_global = place * new_rows + jnp.arange(new_rows, dtype=jnp.int32)
    q_frame = q_global * frames_new // new_all
    frame_hits = (q_frame[:, None] == jnp.arange(frames_new, dtype=jnp.int32)[None, :])[:, :, None]
    new_mask = jnp.sum(jnp.where(frame_hits, frame_mask[None], 0), axis=1)
    query_mask = jnp.concatenate(
        [new_mask, jnp.ones((ctx_rows, frames_ctx), jnp.int32)], axis=0
    ).astype(jnp.float32)

    def context_allowed(first_shard, count_rows):
        index = first_shard * ctx_rows + jnp.arange(count_rows, dtype=jnp.int32)
        frame = index // 4 * frames_ctx // blocks_all
        coarse = lookup(levels, frame) == 1
        live = jnp.logical_or(jnp.logical_not(coarse), index % 4 == 0)
        onehot = (frame[:, None] == jnp.arange(frames_ctx, dtype=jnp.int32)[None, :]).astype(
            jnp.float32
        )
        reach = jnp.dot(query_mask, onehot.T) > 0.5
        return jnp.logical_and(reach, live[None, :])

    def take_new(state, keys, values):
        return attend(state, heads_q, keys, values, None, scale)

    def take_context(state, keys, values, first_shard):
        allowed = context_allowed(first_shard, keys.shape[0])
        return attend(state, heads_q, keys, values, allowed, scale)

    start_state = (
        jnp.full((heads, rows_q), NEGATIVE, jnp.float32),
        jnp.zeros((heads, rows_q), jnp.float32),
        jnp.zeros((heads, rows_q, hdim), jnp.float32),
    )
    empty_cache = (
        jnp.zeros((blocks_dev, 4, width), jnp.bfloat16),
        jnp.zeros((blocks_dev, 4, width), jnp.bfloat16),
    )
    flat_k = pooled_k.reshape(ctx_rows, width)
    flat_v = pooled_v.reshape(ctx_rows, width)
    piece = (
        lax.all_gather(new_keys, "seq", axis=0, tiled=True),
        lax.all_gather(new_values, "seq", axis=0, tiled=True),
    )
    steps, group = group_plan(piece[0].shape[0], new_rows)
    size = group * new_rows
    stacked = (piece[0].reshape(steps, size, width), piece[1].reshape(steps, size, width))

    def one(carry, item):
        return (take_new(carry, item[0], item[1]), None)

    state = lax.scan(one, start_state, stacked)[0]
    piece = (
        lax.all_gather(flat_k, "seq", axis=0, tiled=True),
        lax.all_gather(flat_v, "seq", axis=0, tiled=True),
    )
    steps, group = group_plan(piece[0].shape[0], ctx_rows)
    size = group * ctx_rows
    firsts = jnp.arange(steps, dtype=jnp.int32) * group
    stacked = (piece[0].reshape(steps, size, width), piece[1].reshape(steps, size, width), firsts)

    def one(inner, item):
        keys, values, first = item
        attended = take_context(inner[0], keys, values, first)
        cache = inner[1]
        return ((attended, cache), None)

    state, cache = lax.scan(one, (state, empty_cache), stacked)[0]
    best, total, accum = state
    mixed = (accum / total[..., None]).transpose(1, 0, 2).reshape(rows_q, width)
    live_rows = jnp.concatenate([jnp.ones((new_rows,), dtype=bool), held_live], axis=0)
    mixed = jnp.where(live_rows[:, None], mixed, 0.0).astype(jnp.bfloat16)
    summed = lax.psum_scatter(
        lax.dot_general(
            out_weight, mixed, (((0,), (1,)), ((), ())), preferred_element_type=jnp.float32
        ).astype(jnp.bfloat16),
        "tensor",
        scatter_dimension=0,
        tiled=True,
    ).astype(jnp.float32)
    result = summed.T.astype(jnp.bfloat16)
    return (
        result[:new_rows],
        result[new_rows:],
        held_k.reshape(ctx_rows, width),
        held_v.reshape(ctx_rows, width),
    )


def place_index(shape, dim):
    return lax.broadcasted_iota(jnp.int32, shape, dim)


def coarse_of(frame, levels_ref, frames_ctx):
    coarse = frame < 0
    for f in range(frames_ctx):
        coarse = jnp.logical_or(coarse, jnp.logical_and(frame == f, levels_ref[f] == 1))
    return coarse


def pack_kernel(
    inner, levels, q, k, v, cq, ck, cv, near_a, near_b, far_a, far_b,
    lv, nk, nv, nq, sk, sv, sq, tk, tv, tq, sems,
):
    z = lax.axis_index("seq")

    @pl.when(middle(z) if inner else jnp.logical_not(middle(z)))
    def _():
        devices = lax.axis_size("seq")
        new_rows, width = q.shape
        ctx_rows = cq.shape[0]
        half = width // 2
        most = near_a.shape[1]
        rows = new_rows + ctx_rows
        frames_ctx = levels.shape[0]
        low = jnp.where(z < devices // 2, 0, half)
        places = (
            (far_a, half - low, most),
            (near_a, low, most),
            (far_b, half - low + most, half - most),
            (near_b, low + most, half - most),
        )
        places = [(out, pl.ds(pl.multiple_of(at, 128), size)) for out, at, size in places]
        started = []

        def start(src, dst):
            copy = pltpu.make_async_copy(src, dst, sems.at[len(started)])
            copy.start()
            started.append(copy)
            return copy

        def send(src, base):
            for out, lanes in places:
                start(src.at[:, lanes], out.at[base : base + src.shape[0]])

        reads = [start(levels, lv), start(ck, sk), start(cv, sv), start(cq, sq)]
        reads += [start(k, nk), start(v, nv), start(q, nq)]
        reads[0].wait()
        index = place_index((ctx_rows, 1), 0)
        first = index % 4 == 0
        frame = (z * ctx_rows + index) * frames_ctx // (devices * ctx_rows)
        coarse = coarse_of(frame, lv, frames_ctx)
        for part, (src, dst) in enumerate(((sk, tk), (sv, tv), (sq, tq))):
            reads[part + 1].wait()
            wide = src[...].astype(jnp.float32)
            pair = wide + pltpu.roll(wide, ctx_rows - 1, 0)
            quad = pair + pltpu.roll(pair, ctx_rows - 2, 0)
            mean = jnp.where(first, quad * 0.25, 0.0)
            dst[...] = jnp.where(coarse, mean, wide).astype(jnp.bfloat16)
            send(dst, part * rows + new_rows)
        for part, src in enumerate((nk, nv, nq)):
            reads[part + 4].wait()
            send(src, part * rows)
        for copy in started[7:]:
            copy.wait()


def plan_kernel(owners, levels, masks, order, alive, biases):
    blocks = owners.shape[1]
    size = order.shape[0]
    per = size // blocks
    devices = lax.axis_size("seq")
    frames_ctx = levels.shape[0]
    row = owners[...].astype(jnp.float32)
    r = place_index((blocks, blocks), 0)
    c = place_index((blocks, blocks), 1)
    col = jnp.sum(jnp.where(r == c, row, 0.0), axis=1, keepdims=True)
    ahead = jnp.logical_and(col == row, r < c)
    rank = jnp.sum(ahead.astype(jnp.float32), axis=0, keepdims=True)
    spot = row * float(blocks // devices) + rank
    spread = (
        place_index((blocks, size), 1) // per == place_index((blocks, size), 0)
    ).astype(jnp.bfloat16)
    wide = jnp.dot(
        jnp.broadcast_to(spot, (16, blocks)).astype(jnp.bfloat16),
        spread,
        preferred_element_type=jnp.float32,
    )[0:1]
    lane = place_index((1, size), 1)
    target = wide.astype(jnp.int32) * per + lane % per
    move = (place_index((size, size), 0) == target).astype(jnp.bfloat16)
    order[...] = move
    index = place_index((size, alive.shape[1]), 0)
    coarse = coarse_of(index * frames_ctx // size, levels, frames_ctx)
    live = jnp.logical_or(jnp.logical_not(coarse), index % per == 0)
    alive[...] = jnp.dot(
        move, live.astype(jnp.bfloat16), preferred_element_type=jnp.float32
    )
    frame = lane * frames_ctx // size
    live = jnp.logical_or(
        jnp.logical_not(coarse_of(frame, levels, frames_ctx)), lane % per == 0
    )
    biases[...] = jnp.zeros_like(biases)
    biases[0:1] = jnp.where(live, 0.0, NEGATIVE)
    for g in range(masks.shape[0]):
        seen = frame < 0
        for f in range(frames_ctx):
            seen = jnp.logical_or(seen, jnp.logical_and(frame == f, masks[g, f] == 1))
        biases[g + 1 : g + 2] = jnp.where(jnp.logical_and(live, seen), 0.0, NEGATIVE)


def far_places(z):
    across = 3 - z
    beside = jnp.where(z == 1, 0, 3)
    return (z, beside, across, 3 - beside)


def middle(z):
    return jnp.logical_or(z == 1, z == 2)


def run_jobs(jobs, keys, values, fresh, factor):
    hdim = values.shape[2] // 2

    def score(head, q):
        lanes = slice(head * hdim, (head + 1) * hdim)
        return lax.dot_general(
            q, keys[:, lanes], (((1,), (1,)), ((), ())), preferred_element_type=jnp.float32
        )

    def finish(head, scores, bias):
        ahead = scores[:, :fresh]
        behind = scores[:, fresh:] + bias
        top = jnp.maximum(
            jnp.max(ahead, axis=1, keepdims=True), jnp.max(behind, axis=1, keepdims=True)
        )
        w_ahead = jnp.exp2((ahead - top) * factor).astype(jnp.bfloat16)
        w_behind = jnp.exp2((behind - top) * factor).astype(jnp.bfloat16)
        both = jnp.dot(
            w_ahead, values[head, :fresh], preferred_element_type=jnp.float32
        ) + jnp.dot(w_behind, values[head, fresh:], preferred_element_type=jnp.float32)
        return both[:, :hdim] / both[:, hdim:]

    held = None
    for job in [*jobs, None]:
        scores = None if job is None else score(job[0], job[1]())
        if held is not None:
            held[3](finish(held[0], held[4], held[2]))
        held = None if job is None else (*job, scores)


def gather_heads(places, sources, ctx_rows, keys, values, qn, qc):
    rows = sources[0].shape[0] // 3
    new_rows = rows - ctx_rows
    fresh = len(sources) * new_rows
    heads = values.shape[0]
    hdim = values.shape[2] // 2
    values[:, :, hdim:] = jnp.ones((heads, values.shape[1], hdim), jnp.bfloat16)
    for place, src in zip(places, sources):
        at = pl.ds(pl.multiple_of(place * new_rows, new_rows), new_rows)
        spot = pl.ds(pl.multiple_of(place * ctx_rows, ctx_rows), ctx_rows)
        to = pl.ds(pl.multiple_of(fresh + place * ctx_rows, ctx_rows), ctx_rows)
        keys[at] = src[0:new_rows]
        keys[to] = src[new_rows:rows]
        qn[at] = src[2 * rows : 2 * rows + new_rows]
        qc[spot] = src[2 * rows + new_rows : 3 * rows]
        for h in range(heads):
            lanes = slice(h * hdim, (h + 1) * hdim)
            values[h, at, :hdim] = src[rows : rows + new_rows, lanes]
            values[h, to, :hdim] = src[rows + new_rows : 2 * rows, lanes]


def attend_heads(factor, frames_new, order, alive, biases, keys, values, qn, qc):
    heads = values.shape[0]
    hdim = values.shape[2] // 2
    fresh = qn.shape[0]
    per = fresh // frames_new
    qc[...] = jnp.dot(order[...], qc[...], preferred_element_type=jnp.float32).astype(
        jnp.bfloat16
    )
    jobs = []
    for h in range(heads):
        lanes = slice(h * hdim, (h + 1) * hdim)
        for g in range(frames_new):
            at = slice(g * per, (g + 1) * per)

            def put_new(r, at=at, lanes=lanes):
                qn[at, lanes] = r.astype(jnp.bfloat16)

            jobs.append(
                (h, lambda at=at, lanes=lanes: qn[at, lanes], biases[g + 1 : g + 2], put_new)
            )

        def put_ctx(r, lanes=lanes):
            qc[:, lanes] = (r * alive[...]).astype(jnp.bfloat16)

        jobs.append((h, lambda lanes=lanes: qc[:, lanes], biases[0:1], put_ctx))
    run_jobs(jobs, keys, values, fresh, factor)


def hand_out(place, out, lanes, qn, qc):
    new_rows = qn.shape[0] // 4
    ctx_rows = qc.shape[0] // 4
    at = pl.ds(pl.multiple_of(place * new_rows, new_rows), new_rows)
    part = pl.ds(pl.multiple_of(place * ctx_rows, ctx_rows), ctx_rows)
    out[:new_rows, lanes] = qn[at]
    out[new_rows:, lanes] = qc[part]


def first_kernel(
    factor, frames_new, a0, a3, a2, a1, order, alive, biases, qn, qc, cn, e3, keys, values
):
    z = lax.axis_index("seq")

    @pl.when(middle(z))
    def _():
        places = far_places(z)
        gather_heads(places, (a0, a1, a2, a3), qc.shape[0] // 4, keys, values, qn, qc)
        attend_heads(factor, frames_new, order, alive, biases, keys, values, qn, qc)
        hand_out(places[3], e3, slice(None), qn, qc)
        ctx_rows = cn.shape[0] // 2
        fresh = qn.shape[0]
        hdim = values.shape[2] // 2
        spot = pl.ds(pl.multiple_of(places[1] * ctx_rows, ctx_rows), ctx_rows)
        move = order[spot]
        cn[:ctx_rows] = jnp.dot(
            move, keys[fresh:], preferred_element_type=jnp.float32
        ).astype(jnp.bfloat16)
        for h in range(values.shape[0]):
            cn[ctx_rows:, h * hdim : (h + 1) * hdim] = jnp.dot(
                move, values[h, fresh:, :hdim], preferred_element_type=jnp.float32
            ).astype(jnp.bfloat16)


def second_kernel(
    factor, frames_new, b0, b3, b2, b1, order, alive, biases, fn, fc,
    o0, o1, o2, n3, keys, values, qn, qc,
):
    z = lax.axis_index("seq")
    most = fn.shape[1]

    @pl.when(middle(z))
    def _():
        places = far_places(z)
        gather_heads(places, (b0, b1, b2, b3), qc.shape[0] // 4, keys, values, qn, qc)
        attend_heads(factor, frames_new, order, alive, biases, keys, values, qn, qc)
        hand_out(places[3], n3, slice(None), qn, qc)
        for place, out in zip(places, (o0, o1, o2)):
            hand_out(place, out, slice(0, most), fn, fc)
            hand_out(place, out, slice(most, None), qn, qc)


def cache_kernel(
    a0, a1, a2, a3, b0, b1, b2, b3, order, c0, c1, c2, c3, kk
):
    z = lax.axis_index("seq")
    ctx_rows, half = c0.shape[0] // 2, c0.shape[1]
    rows = a0.shape[0] // 3
    new_rows = rows - ctx_rows
    most = a0.shape[1]

    @pl.when(middle(z))
    def _():
        places = far_places(z)
        for place, a, b in zip(places, (a0, a1, a2, a3), (b0, b1, b2, b3)):
            to = pl.ds(pl.multiple_of(place * ctx_rows, ctx_rows), ctx_rows)
            for part in range(2):
                at = slice(part * rows + new_rows, (part + 1) * rows)
                kk[to, part * half : part * half + most] = a[at]
                kk[to, part * half + most : (part + 1) * half] = b[at]
        spot = pl.ds(pl.multiple_of(places[1] * ctx_rows, ctx_rows), ctx_rows)
        for part in range(2):
            moved = jnp.dot(
                order[spot],
                kk[:, part * half + most : (part + 1) * half],
                preferred_element_type=jnp.float32,
            )
            c1[part * ctx_rows : (part + 1) * ctx_rows] = moved.astype(jnp.bfloat16)
        for place, out in ((places[0], c0), (places[2], c2), (places[3], c3)):
            part = pl.ds(pl.multiple_of(place * ctx_rows, ctx_rows), ctx_rows)
            moved = jnp.dot(order[part], kk[...], preferred_element_type=jnp.float32)
            out[:ctx_rows] = moved[:, :half].astype(jnp.bfloat16)
            out[ctx_rows:] = moved[:, half:].astype(jnp.bfloat16)


def halves(z, at, *parts):
    own, beside, across, beyond = (part[at] for part in parts)
    inner = middle(z)
    low = z < 2
    near = jnp.where(inner, own, beside)
    far = jnp.where(inner, across, beyond)
    return (jnp.where(low, near, far), jnp.where(low, far, near))


def project_kernel(mine, here, e3, o0, o1, n3, o2, weight, out):
    o3 = jnp.concatenate([e3[...], n3[...]], axis=1)
    a, b = halves(lax.axis_index("seq"), slice(None), o0, o1, o2, o3)
    mixed = jnp.concatenate([a, b], axis=1)
    width = mixed.shape[1]
    me = lax.axis_index("tensor")
    core = me % 2 if mine else 1 - me % 2
    chip = me // 2 if here else 1 - me // 2
    lanes = pl.ds(pl.multiple_of((2 * chip + core) * width, width), width)
    total = jnp.dot(mixed, weight[:, lanes], preferred_element_type=jnp.float32)
    out[...] = total.astype(out.dtype)


def add_kernel(keep, came, out):
    out[...] = (keep[...] + came[...].astype(jnp.float32)).astype(jnp.bfloat16)


def finish_kernel(last, keep, came, cn, c0, cl, c3, c2, out, out_ctx, keys, values):
    total = keep[...] + came[...].astype(jnp.float32) + last[...].astype(jnp.float32)
    total = total.astype(jnp.bfloat16)
    out[...] = total[: out.shape[0]]
    out_ctx[...] = total[out.shape[0] :]
    z = lax.axis_index("seq")
    ctx_rows, width = keys.shape
    half = width // 2
    c1 = jnp.concatenate([cn[...], cl[...]], axis=1)
    for i, part in enumerate((keys, values)):
        at = slice(i * ctx_rows, (i + 1) * ctx_rows)
        a, b = halves(z, at, c0, c1, c2, c3)
        part[:, :half] = a
        part[:, half:] = b


SMALL = pl.BlockSpec(memory_space=pltpu.SMEM)
AWAY = pl.BlockSpec(memory_space=pltpu.HBM)
WHOLE = pl.BlockSpec(memory_space=pltpu.VMEM)
LIMIT = pltpu.CompilerParams(vmem_limit_bytes=32 * 1024 * 1024)


def lasts(us):
    return pl.CostEstimate(flops=int(us * 1.1e9), bytes_accessed=0, transcendentals=0)


def shape16(*dims):
    return jax.ShapeDtypeStruct(dims, jnp.bfloat16)


def permute(x, pairs):
    return lax.ppermute(x, "seq", pairs)


BESIDE = ((0, 1), (3, 2))
ACROSS = ((1, 2), (2, 1))
BEYOND = ((0, 2), (3, 1))
SIBLING = ((0, 1), (1, 0), (2, 3), (3, 2))
OPPOSITE = ((0, 2), (2, 0), (1, 3), (3, 1))


def back(pairs):
    return tuple((b, a) for a, b in pairs)


def fast_device(
    queries,
    new_keys,
    new_values,
    context_queries,
    context_keys,
    context_values,
    levels,
    frame_mask,
    owners,
    out_weight,
):
    new_rows, width = queries.shape
    ctx_rows = context_keys.shape[0]
    rows = new_rows + ctx_rows
    half = width // 2
    devices = lax.axis_size("seq")
    ctx_all = ctx_rows * devices
    hdim = HEAD_DIM
    frames_new = frame_mask.shape[0]
    factor = math.log2(math.e) / math.sqrt(hdim)
    most = max(hdim, half - hdim)

    def pack(inner):
        return pl.pallas_call(
            functools.partial(pack_kernel, inner),
            out_shape=(
                shape16(3 * rows, most),
                shape16(3 * rows, half - most),
                shape16(3 * rows, most),
                shape16(3 * rows, half - most),
            ),
            in_specs=[AWAY] * 7,
            out_specs=[AWAY] * 4,
            scratch_shapes=[pltpu.SMEM(levels.shape, jnp.int32)]
            + [pltpu.VMEM((new_rows, width), jnp.bfloat16)] * 3
            + [pltpu.VMEM((ctx_rows, width), jnp.bfloat16)] * 6
            + [pltpu.SemaphoreType.DMA((31,))],
            name="pack_inner" if inner else "pack_outer",
            cost_estimate=lasts(2.6),
        )(levels, queries, new_keys, new_values, context_queries, context_keys, context_values)

    end_near_a, end_near_b, end_far_a, end_far_b = pack(False)
    near_a, near_b, far_a, far_b = pack(True)
    beside_a = permute(end_near_a, BESIDE)
    across_a = permute(far_a, ACROSS)
    beyond_a = permute(end_far_a, BEYOND)
    beside_b = permute(end_near_b, BESIDE)
    across_b = permute(far_b, ACROSS)
    beyond_b = permute(end_far_b, BEYOND)
    order, alive, biases = pl.pallas_call(
        plan_kernel,
        out_shape=(
            shape16(ctx_all, ctx_all),
            jax.ShapeDtypeStruct((ctx_all, hdim), jnp.float32),
            jax.ShapeDtypeStruct((8, ctx_all), jnp.float32),
        ),
        in_specs=[WHOLE, SMALL, SMALL],
        compiler_params=LIMIT,
        name="plan", cost_estimate=lasts(1.6),
    )(owners.reshape(1, -1), levels, frame_mask)
    def scratch(lanes):
        return [
            pltpu.VMEM((rows * devices, lanes), jnp.bfloat16),
            pltpu.VMEM((lanes // hdim, rows * devices, 2 * hdim), jnp.bfloat16),
        ]

    fresh, held, early_cache, early_beyond = pl.pallas_call(
        functools.partial(first_kernel, factor, frames_new),
        out_shape=[
            shape16(new_rows * devices, most),
            shape16(ctx_all, most),
            shape16(2 * ctx_rows, most),
            shape16(rows, most),
        ],
        scratch_shapes=scratch(most),
        compiler_params=LIMIT,
        name="attend_first",
        cost_estimate=lasts(4.8),
    )(near_a, beyond_a, across_a, beside_a, order, alive, biases)
    results = pl.pallas_call(
        functools.partial(second_kernel, factor, frames_new),
        out_shape=[
            shape16(rows, half),
            shape16(rows, half),
            shape16(rows, half),
            shape16(rows, half - most),
        ],
        scratch_shapes=scratch(half - most)
        + [
            pltpu.VMEM((new_rows * devices, half - most), jnp.bfloat16),
            pltpu.VMEM((ctx_all, half - most), jnp.bfloat16),
        ],
        compiler_params=LIMIT,
        name="attend_second",
        cost_estimate=lasts(2.4),
    )(near_b, beyond_b, across_b, beside_b, order, alive, biases, fresh, held)
    own, beside, across, late_beyond = results
    early_cache = permute(early_cache, back(BESIDE))
    early_beyond = permute(early_beyond, back(BEYOND))
    across = lax.optimization_barrier((across, early_cache, early_beyond))[0]
    mixed = (
        early_beyond,
        own,
        permute(beside, back(BESIDE)),
        permute(late_beyond, back(BEYOND)),
        permute(across, ACROSS),
    )
    near_a = lax.optimization_barrier((near_a, results[0]))[0]
    caches = pl.pallas_call(
        cache_kernel,
        out_shape=[
            shape16(2 * ctx_rows, half),
            shape16(2 * ctx_rows, half - most),
            shape16(2 * ctx_rows, half),
            shape16(2 * ctx_rows, half),
        ],
        scratch_shapes=[pltpu.VMEM((ctx_all, width), jnp.bfloat16)],
        compiler_params=LIMIT,
        name="caches",
        cost_estimate=lasts(3),
    )(near_a, beside_a, across_a, beyond_a, near_b, beside_b, across_b, beyond_b, order)

    mixed = lax.optimization_barrier((*mixed, caches[0]))[:5]

    def project(mine, here, dtype):
        return pl.pallas_call(
            functools.partial(project_kernel, mine, here),
            out_shape=jax.ShapeDtypeStruct((rows, width), dtype),
            in_specs=[WHOLE] * 6,
            compiler_params=LIMIT,
            name=("keep" if mine else "give") + ("_here" if here else "_there"),
            cost_estimate=lasts(0.6),
        )(*mixed, out_weight)

    give_there = project(False, False, jnp.bfloat16)
    came_there = lax.ppermute(give_there, "tensor", SIBLING)
    keep_there = project(True, False, jnp.float32)
    other = pl.pallas_call(
        add_kernel,
        out_shape=shape16(rows, width),
        compiler_params=LIMIT,
        name="add",
        cost_estimate=lasts(0.1),
    )(keep_there, came_there)
    last = lax.ppermute(other, "tensor", OPPOSITE)
    caches = lax.optimization_barrier((*caches, other))[:4]
    beyond = permute(caches[3], back(BEYOND))
    across = permute(caches[2], ACROSS)
    beside = permute(caches[1], back(BESIDE))
    stored = (early_cache, caches[0], beside, beyond, across)
    mixed = lax.optimization_barrier((*mixed, keep_there))[:5]
    came = lax.ppermute(project(False, True, jnp.bfloat16), "tensor", SIBLING)
    keep = project(True, True, jnp.float32)
    block_out, context_out, cache_keys, cache_values = pl.pallas_call(
        finish_kernel,
        out_shape=(
            shape16(new_rows, width),
            shape16(ctx_rows, width),
            shape16(ctx_rows, width),
            shape16(ctx_rows, width),
        ),
        compiler_params=LIMIT,
        name="finish",
        cost_estimate=lasts(1.0),
    )(last, keep, came, *stored)
    return (block_out, context_out, cache_keys, cache_values)


def solution(mesh):
    rows = P(("session", "seq"), "tensor")
    in_specs = (rows,) * 6 + (P("session"), P("session", None), P("session"), P("tensor", None))
    sizes = mesh.shape
    step = fast_device if sizes["seq"] == 4 and sizes["tensor"] == 4 else per_device
    return jax.shard_map(
        step, mesh=mesh, in_specs=in_specs, out_specs=(rows,) * 4, check_vma=False
    )
```
